32 devices in a mesh: ep: 16 (over z, y, x), tp: 2 (over core).
Axes of the slice: x: 2, y: 2, z: 4, core: 2. Of those that a mesh axis runs over, the one named last changes fastest.
Arguments:
- tokens: bfloat16 [2, 8192, 1024], P(None, ('ep', 'tp')), may hold values from -6 to 6
- gain_attn: bfloat16 [1024], P('ep'), may hold values from 0.5 to 1.5
- w_query: bfloat16 [1024, 1024], P('ep', 'tp'), may hold values from -0.1875 to 0.1875
- w_key: bfloat16 [1024, 512], P('ep', 'tp'), may hold values from -0.1875 to 0.1875
- w_value: bfloat16 [1024, 512], P('ep', 'tp'), may hold values from -0.1875 to 0.1875
- w_output: bfloat16 [1024, 1024], P('tp', 'ep'), may hold values from -3 to 3
- gain_moe: bfloat16 [1024], P('ep'), may hold values from 0.5 to 1.5
- w_router: bfloat16 [1024, 16], P('ep'), may hold values from -0.09375 to 0.09375
- w_gate: bfloat16 [16, 1024, 512], P('ep'), may hold values from -0.1875 to 0.1875
- w_up: bfloat16 [16, 1024, 512], P('ep'), may hold values from -0.1875 to 0.1875
- w_down: bfloat16 [16, 512, 1024], P('ep'), may hold values from -0.75 to 0.75
- routes: int32 [2, 8192, 8], P(None, ('ep', 'tp')), may hold values from 0 to 15, all different within a row; in each aligned block of 256 rows (0 to 255, 256 to 511, ..., all dimensions but the last counted through in order) at most 192 rows name the same one
- piece_starts: int32 [2, 16], replicated, may hold values from 0 to 7936, as said below
- cotangent: bfloat16 [2, 8192, 1024], P(None, ('ep', 'tp')), may hold values from -6 to 6
Outputs:
- mixed: bfloat16 [2, 8192, 1024], P(None, ('ep', 'tp'))
- grad_tokens: float32 [2, 8192, 1024], P(None, ('ep', 'tp'))
- grad_gain_attn: float32 [1024], P(('ep', 'tp'))
- grad_w_query: float32 [1024, 1024], P('ep', 'tp')
- grad_w_key: float32 [1024, 512], P('ep', 'tp')
- grad_w_value: float32 [1024, 512], P('ep', 'tp')
- grad_w_output: float32 [1024, 1024], P('tp', 'ep')
- grad_gain_moe: float32 [1024], P(('ep', 'tp'))
- grad_w_router: float32 [1024, 16], P(('ep', 'tp'))
- grad_w_gate: float32 [16, 1024, 512], P('ep', 'tp')
- grad_w_up: float32 [16, 1024, 512], P('ep', 'tp')
- grad_w_down: float32 [16, 512, 1024], P('ep', None, 'tp')
The draws below stay inside these ranges and needn't reach their ends.
Inputs may be any that keep to these rules, and one draw needn't show every extreme that they name: `routes`: each token names 8 different experts. Within the rows of one device (aligned blocks of 256 positions of a micro-batch) no expert is named more than 192 times, a bound that some block reaches. `piece_starts`: in each sequence the 16 picture pieces [start, start + 256) rise and do not intersect.
All inputs are finite; a program needn't handle non-finite values.
Results may differ from the reference program's by a relative error of at most 0.03.
Values may be sent and summed in bfloat16 or wider, within the bound.
No kernel may reach another device: no remote copies, remote signals or barrier semaphores. Data moves between devices by JAX's collectives and lax.ppermute only.
A program may use at most 256 MiB of HBM per device.

```python
import math
import jax
import jax.numpy as jnp
import numpy as np
from jax import lax

D = 1024
HEADS = 16
KV_HEADS = 8
HEAD_DIM = 64
FF = 512
TOPK = 8
MICRO = 2
PIECE = 256
EXPERTS = 16
LEN = 8192
SLICE = 256
PIECES = 16
CAP = 192


def draw_piece_starts(key, part):
    key = jax.random.fold_in(key, 7)
    slot_len = LEN // PIECES
    offsets = jax.random.randint(key, (MICRO, PIECES), 0, slot_len - PIECE + 1)
    numbers = jnp.arange(PIECES, dtype=jnp.int32)
    starts = numbers[None, :] * slot_len + offsets
    return starts.astype(jnp.int32)


def block_scale(rng, extent, cuts, low, top_value):
    level = 1.0
    for position, parts in cuts:
        draws = jax.random.uniform(jax.random.fold_in(jax.random.fold_in(rng, 6), position), (parts,), jnp.float32, low / len(cuts), top_value / len(cuts))
        level = level * jnp.repeat(jnp.exp(draws), extent[position] // parts).reshape((-1,) + (1,) * (len(extent) - 1 - position))
    return level


def deal_out(key, own, number, rows, count, top, most, skew):
    ranking = jax.random.permutation(key, count)
    crowded, ordinary = shares(count, rows * top, most, skew, True), shares(count, rows * top, most, skew, False)
    places = jnp.arange(count)

    def named(tallies, rotation):
        used = int((tallies > 0).sum())
        fixed = max(1, used // 4)
        passed = fixed + (places - fixed + rotation * (used - fixed)) % max(1, count - fixed)
        return jnp.zeros((count,), jnp.int32).at[ranking[jnp.where(places < fixed, places, passed)]].set(jnp.asarray(tallies, jnp.int32))

    tallies = jnp.where(number % 4 == 0, named(crowded, number // 4), named(ordinary, number - number // 4 - 1))
    mixed = jax.random.permutation(jax.random.fold_in(own, 3), count)
    source_of, sink = mixed[0:count // 2 * 2:2], mixed[1:count // 2 * 2:2]
    room = jnp.minimum(tallies[source_of] - 1, most - tallies[sink]) // 2
    room = jnp.where((source_of == ranking[0]) | (sink == ranking[0]) | (tallies[sink] == 0), 0, jnp.maximum(room, 0))
    passed = jax.random.randint(jax.random.fold_in(own, 4), (count // 2,), 0, 1 << 20) % (room + 1)
    tallies = tallies.at[source_of].add(-passed).at[sink].add(passed)
    members = jnp.searchsorted(jnp.cumsum(tallies), jnp.arange(rows * top), side="right").astype(jnp.int32)
    table = members.reshape(top, rows).T
    table = table[jax.random.permutation(jax.random.fold_in(own, 1), rows)]
    rotation = jax.random.randint(jax.random.fold_in(own, 2), (rows, 1), 0, top)
    return jnp.take_along_axis(table, (jnp.arange(top)[None, :] + rotation) % top, axis=1)


def shares(count, total, reach, slope, full):
    loads = [(1 << 20) // math.isqrt(grade ** slope) + 1 for grade in range(1, count + 1)]
    largest = reach if full else min(reach, max(-(-total // count), total * loads[0] // sum(loads)))
    least = 1 if total - largest >= count - 1 else 0
    given, spare = [largest] + [least] * (count - 1), total - largest - least * (count - 1)
    while spare > 0:
        movable = [i for i in range(1, count) if given[i] < largest] or [i for i in range(1, count) if given[i] < reach]
        mass, remaining = sum([loads[i] for i in movable]), spare
        for i in movable:
            addition = min(reach - given[i], max(1, remaining * loads[i] // mass), spare)
            given[i] = given[i] + addition
            spare = spare - addition
    return np.array(given)


def gaussian(own_key, shape, width, bound, cuts=(), kind=jnp.bfloat16):
    array = width * jax.random.normal(own_key, shape, jnp.float32)
    if cuts:
        array = array * block_scale(own_key, shape, cuts, -0.22, 0.18)
    return jnp.clip(array, -bound, bound).astype(kind)


def setup_inputs(seed: int = 0) -> dict:
    seeds = jax.random.split(jax.random.key(seed), 15)
    tokens = gaussian(seeds[0], (MICRO, LEN, D), 1.0, 6.0, ((1, 32),))
    gain_attn = jnp.clip(1.0 + 0.1 * jax.random.normal(seeds[1], (D,), jnp.float32), 0.5, 1.5).astype(jnp.bfloat16)
    w_query = gaussian(seeds[2], (D, HEADS * HEAD_DIM), D ** -0.5, 0.1875, ((0, 16), (1, 2)))
    w_key = gaussian(seeds[3], (D, KV_HEADS * HEAD_DIM), D ** -0.5, 0.1875, ((0, 16), (1, 2)))
    w_value = gaussian(seeds[4], (D, KV_HEADS * HEAD_DIM), D ** -0.5, 0.1875, ((0, 16), (1, 2)))
    w_output = gaussian(seeds[5], (HEADS * HEAD_DIM, D), (max(1, HEADS * HEAD_DIM // 256)) ** -0.5, 3.0, ((0, 2), (1, 16)))
    gain_moe = jnp.clip(1.0 + 0.1 * jax.random.normal(seeds[6], (D,), jnp.float32), 0.5, 1.5).astype(jnp.bfloat16)
    w_router = gaussian(seeds[7], (D, EXPERTS), (4 * D) ** -0.5, 0.09375, ((0, 16),))
    w_gate = gaussian(seeds[8], (EXPERTS, D, FF), D ** -0.5, 0.1875, ((0, 16),))
    w_up = gaussian(seeds[9], (EXPERTS, D, FF), D ** -0.5, 0.1875, ((0, 16),))
    w_down = gaussian(seeds[10], (EXPERTS, FF, D), (FF // 8) ** -0.5, 0.75, ((0, 16),))
    routes_keys = jax.random.split(jax.random.fold_in(seeds[11], 1), MICRO * LEN // SLICE)
    routes_turns = jax.random.permutation(jax.random.fold_in(seeds[11], 3), MICRO * LEN // SLICE)
    routes = jax.vmap(lambda own, number: deal_out(jax.random.fold_in(seeds[11], 2), own, number, SLICE, EXPERTS, TOPK, CAP, 0))(routes_keys, routes_turns).reshape((MICRO, LEN, TOPK))
    piece_starts = draw_piece_starts(jax.random.fold_in(seeds[14], 71), 0)
    cotangent = gaussian(seeds[13], (MICRO, LEN, D), 1.0, 6.0, ((1, 32),))
    return dict(tokens=tokens, gain_attn=gain_attn, w_query=w_query, w_key=w_key, w_value=w_value, w_output=w_output, gain_moe=gain_moe, w_router=w_router, w_gate=w_gate, w_up=w_up, w_down=w_down, routes=routes, piece_starts=piece_starts, cotangent=cotangent)


EPS = 1e-06
THETA = 10000.0
NEG = -1e+30
HIGH = lax.Precision.HIGHEST

@jax.custom_vjp
def low(v):
    return lax.optimization_barrier(v.astype(jnp.bfloat16)).astype(jnp.float32)

@jax.custom_vjp
def low_back(v):
    return v

def low_keep(v):
    return (low(v), None)

def low_pass(kept, grad):
    return (grad,)

def back_keep(v):
    return (v, None)

def back_low(kept, grad):
    return (low(grad),)
low.defvjp(low_keep, low_pass)
low_back.defvjp(back_keep, back_low)

def matmul(left, right):
    return jnp.dot(left, right, precision=HIGH, preferred_element_type=jnp.float32)

def rms_gain(values, gain):
    return values * lax.rsqrt(lax.optimization_barrier(jnp.mean(values * values, -1, keepdims=True)) + EPS) * gain

def angle_tables(positions):
    halves = jnp.arange(HEAD_DIM // 2, dtype=jnp.float32)
    freqs = THETA ** (-2.0 * halves / HEAD_DIM)
    angles = positions.astype(jnp.float32)[:, None] * freqs[None, :]
    return (jnp.cos(angles)[:, None, :], jnp.sin(angles)[:, None, :])

def rotate(values, cosine, sine):
    half_dim = values.shape[-1] // 2
    first_half = values[..., :half_dim]
    second_half = values[..., half_dim:]
    return jnp.concatenate([first_half * cosine - second_half * sine, second_half * cosine + first_half * sine], -1)

def piece_index(starts, positions):
    inside = (positions[:, None] >= starts[None, :]) & (positions[:, None] < starts[None, :] + PIECE)
    numbers = jnp.arange(1, starts.shape[0] + 1, dtype=jnp.int32)
    return (lax.optimization_barrier(jnp.sum(jnp.where(inside, numbers[None, :], 0), -1)) - 1).astype(jnp.int32)

def attention(queries, keys, values, starts):
    group_size = HEADS // KV_HEADS
    keys_wide = jnp.repeat(keys, group_size, axis=1)
    values_wide = jnp.repeat(values, group_size, axis=1)
    positions = jnp.arange(LEN, dtype=jnp.int32)
    pieces = piece_index(starts, positions)
    block_rows = math.gcd(LEN, 512)
    block_total = LEN // block_rows
    score_scale = HEAD_DIM ** (-0.5)

    def one_block(operands):
        query_block, query_pos, query_piece = operands
        scores = jnp.einsum('qhd,khd->hqk', query_block, keys_wide, precision=HIGH) * score_scale
        scores = low_back(scores)
        allowed = (positions[None, :] <= query_pos[:, None]) | (pieces[None, :] == query_piece[:, None]) & (query_piece[:, None] >= 0)
        scores = jnp.where(allowed[None], scores, NEG)
        highest = lax.optimization_barrier(jnp.max(scores, -1, keepdims=True))
        raised = jnp.exp(scores - highest)
        probs = low(raised / lax.optimization_barrier(jnp.sum(raised, -1, keepdims=True)))
        return jnp.einsum('hqk,khd->qhd', probs, values_wide, precision=HIGH)
    result = lax.map(jax.checkpoint(one_block), (queries.reshape(block_total, block_rows, HEADS, HEAD_DIM), positions.reshape(block_total, block_rows), pieces.reshape(block_total, block_rows)))
    return result.reshape(LEN, HEADS * HEAD_DIM)

def experts_mix(normed_two, combine, w_gate, w_up, w_down):

    def step(running, item):
        gate_w, up_w, down_w, weight = item
        inputs = low_back(normed_two)
        gate_pre = low_back(matmul(inputs, gate_w))
        up_pre = low_back(matmul(inputs, up_w))
        hidden = low(jax.nn.silu(gate_pre) * up_pre)
        expert_out = low_back(low(matmul(hidden, down_w)))
        return (running + weight[:, None] * expert_out, None)
    running, unused = lax.scan(jax.checkpoint(step), jnp.zeros_like(normed_two), (w_gate, w_up, w_down, combine.T))
    return running

def layer(tokens, gain_attn, w_query, w_key, w_value, w_output, gain_moe, w_router, w_gate, w_up, w_down, route_rows, starts):
    positions = jnp.arange(LEN, dtype=jnp.int32)
    cosine, sine = angle_tables(positions)
    normed = low(rms_gain(tokens, gain_attn))
    q_raw = low_back(matmul(normed, w_query)).reshape(LEN, HEADS, HEAD_DIM)
    queries = low(rotate(q_raw, cosine, sine))
    k_raw = low_back(matmul(normed, w_key)).reshape(LEN, KV_HEADS, HEAD_DIM)
    keys = low(rotate(k_raw, cosine, sine))
    values = low(low_back(matmul(normed, w_value))).reshape(LEN, KV_HEADS, HEAD_DIM)
    attended = low(low_back(attention(queries, keys, values, starts)))
    resid = tokens + low_back(matmul(attended, w_output))
    normed_two = low(rms_gain(resid, gain_moe))
    logits = low_back(matmul(normed_two, w_router))
    route_hot = (route_rows[:, :, None] == jnp.arange(EXPERTS, dtype=jnp.int32)[None, None, :]).astype(jnp.float32)
    picked = jnp.einsum('tke,te->tk', route_hot, logits, precision=HIGH)
    highest = lax.optimization_barrier(jnp.max(picked, -1, keepdims=True))
    raised = jnp.exp(picked - highest)
    gates = raised / lax.optimization_barrier(jnp.sum(raised, -1, keepdims=True))
    combine = jnp.einsum('tk,tke->te', gates, route_hot, precision=HIGH)
    return resid + experts_mix(normed_two, combine, w_gate, w_up, w_down)

def reference(tokens, gain_attn, w_query, w_key, w_value, w_output, gain_moe, w_router, w_gate, w_up, w_down, routes, piece_starts, cotangent):
    params = tuple((weight.astype(jnp.float32) for weight in (gain_attn, w_query, w_key, w_value, w_output, gain_moe, w_router, w_gate, w_up, w_down)))
    totals = tuple((jnp.zeros(weight.shape, jnp.float32) for weight in params))
    outputs = []
    input_grads = []
    for micro_index in range(MICRO):
        route_rows = routes[micro_index]
        starts = piece_starts[micro_index]

        def forward(inputs, *weights):
            return layer(inputs, *weights, route_rows, starts)
        result, pull = jax.vjp(forward, tokens[micro_index].astype(jnp.float32), *params)
        grads = pull(cotangent[micro_index].astype(jnp.float32))
        outputs.append(result.astype(jnp.bfloat16))
        input_grads.append(grads[0])
        totals = tuple((total + grad for total, grad in zip(totals, grads[1:])))
    return (jnp.stack(outputs), jnp.stack(input_grads), totals[0], totals[1], totals[2], totals[3], totals[4], totals[5], totals[6], totals[7], totals[8], totals[9])
```

```python
import functools
import math

import jax
import jax.numpy as jnp
from jax import lax
from jax.experimental import pallas as pl
from jax.experimental.pallas import tpu as pltpu
from jax.sharding import PartitionSpec as P

HEAD_DIM = 64
PIECE = 256
PLANE = 4
LANES = 128
MIB = 1 << 20


EPS = 1e-06
THETA = 10000.0
NEG = -1e30
EXP_SCALE = HEAD_DIM ** (-0.5) * math.log2(math.e)


def rms_scale(values):
    return lax.rsqrt(jnp.mean(values * values, -1, keepdims=True) + EPS)


def angle_tables(positions):
    halves = jnp.arange(HEAD_DIM // 2, dtype=jnp.float32)
    freqs = THETA ** (-2.0 * halves / HEAD_DIM)
    angles = positions.astype(jnp.float32)[:, None] * freqs[None, :]
    return (jnp.cos(angles)[:, None, :], jnp.sin(angles)[:, None, :])


def rotate(values, cosine, sine):
    half_dim = values.shape[-1] // 2
    first_half = values[..., :half_dim]
    second_half = values[..., half_dim:]
    return jnp.concatenate(
        [first_half * cosine - second_half * sine, second_half * cosine + first_half * sine], -1
    )


def piece_index(starts, positions):
    inside = (positions[:, None] >= starts[None, :]) & (
        positions[:, None] < starts[None, :] + PIECE
    )
    numbers = jnp.arange(1, starts.shape[0] + 1, dtype=jnp.int32)
    return jnp.sum(jnp.where(inside, numbers[None, :], 0), -1) - 1


def allowed_mask(query_pos, query_piece, key_pos, key_piece):
    return (key_pos[None, :] <= query_pos[:, None]) | (
        key_piece[None, :] == query_piece[:, None]
    ) & (query_piece[:, None] >= 0)


def to_groups(rows, kv_here, group_size):
    row_total = rows.shape[0]
    return (
        rows.reshape(row_total, kv_here, group_size, HEAD_DIM)
        .transpose(1, 2, 0, 3)
        .reshape(kv_here, group_size * row_total, HEAD_DIM)
    )


def from_groups(grouped, row_total):
    kv_here = grouped.shape[0]
    return (
        grouped.reshape(kv_here, -1, row_total, HEAD_DIM)
        .transpose(2, 0, 1, 3)
        .reshape(row_total, -1)
    )


def tp_major(values, ep_count, tp_count):
    leading = values.shape[0]
    shaped = values.reshape(
        (ep_count, tp_count, leading // (ep_count * tp_count)) + values.shape[1:]
    )
    return jnp.swapaxes(shaped, 0, 1).reshape(values.shape)


def add_all(left_parts, right_parts):
    return tuple((left_part + right_part for left_part, right_part in zip(left_parts, right_parts)))


def reduce_grads(parts, ep_count, tp_count):
    (
        grad_gate_w,
        grad_up_w,
        grad_down_w,
        grad_gain_one,
        grad_gain_two,
        grad_route,
        grad_proj,
        grad_outw,
    ) = parts
    tp_sums = (
        lax.psum_scatter(
            grad_gate_w.astype(jnp.bfloat16), "tp", scatter_dimension=1, tiled=True
        ).astype(jnp.float32),
        lax.psum_scatter(
            grad_up_w.astype(jnp.bfloat16), "tp", scatter_dimension=1, tiled=True
        ).astype(jnp.float32),
        lax.psum_scatter(
            grad_down_w.astype(jnp.bfloat16), "tp", scatter_dimension=2, tiled=True
        ).astype(jnp.float32),
        lax.psum_scatter(
            tp_major(grad_gain_one, ep_count, tp_count).astype(jnp.bfloat16),
            "tp",
            scatter_dimension=0,
            tiled=True,
        ).astype(jnp.float32),
        lax.psum_scatter(
            tp_major(grad_gain_two, ep_count, tp_count).astype(jnp.bfloat16),
            "tp",
            scatter_dimension=0,
            tiled=True,
        ).astype(jnp.float32),
        lax.psum_scatter(
            tp_major(grad_route, ep_count, tp_count).astype(jnp.bfloat16),
            "tp",
            scatter_dimension=0,
            tiled=True,
        ).astype(jnp.float32),
    )
    ep_sums = (
        lax.psum_scatter(
            grad_proj.astype(jnp.bfloat16), "ep", scatter_dimension=0, tiled=True
        ).astype(jnp.float32),
        lax.psum_scatter(
            grad_outw.astype(jnp.bfloat16), "ep", scatter_dimension=1, tiled=True
        ).astype(jnp.float32),
        lax.psum_scatter(
            tp_sums[3].astype(jnp.bfloat16), "ep", scatter_dimension=0, tiled=True
        ).astype(jnp.float32),
        lax.psum_scatter(
            tp_sums[4].astype(jnp.bfloat16), "ep", scatter_dimension=0, tiled=True
        ).astype(jnp.float32),
        lax.psum_scatter(
            tp_sums[5].astype(jnp.bfloat16), "ep", scatter_dimension=0, tiled=True
        ).astype(jnp.float32),
    )
    return (
        tp_sums[0],
        tp_sums[1],
        tp_sums[2],
        ep_sums[2],
        ep_sums[3],
        ep_sums[4],
        ep_sums[0],
        ep_sums[1],
    )


def on_device_general(
    tokens,
    gain_attn,
    w_query,
    w_key,
    w_value,
    w_output,
    gain_moe,
    w_router,
    w_gate,
    w_up,
    w_down,
    routes,
    piece_starts,
    cotangent,
):
    ep_count = lax.axis_size("ep")
    tp_count = lax.axis_size("tp")
    micro_count, slice_rows, width = tokens.shape
    span_rows = slice_rows * tp_count
    seq_len = span_rows * ep_count
    q_cols = w_query.shape[1]
    kv_cols = w_key.shape[1]
    kv_here = kv_cols // HEAD_DIM
    group_size = q_cols // kv_cols
    query_rows = group_size * span_rows
    experts_here = w_gate.shape[0]
    experts_all = experts_here * ep_count
    top_count = routes.shape[2]
    capacity = max(2, slice_rows * top_count * 3 // (2 * experts_all))
    expert_rows = ep_count * capacity
    score_scale = HEAD_DIM ** (-0.5)
    key_block = math.gcd(seq_len, 512)
    block_count = seq_len // key_block
    local_pos = lax.axis_index("ep") * span_rows + jnp.arange(span_rows, dtype=jnp.int32)
    all_pos = jnp.arange(seq_len, dtype=jnp.int32)
    row_pos = jnp.tile(local_pos, group_size)
    cosine, sine = angle_tables(local_pos)
    slot_ids = jnp.arange(experts_all * capacity, dtype=jnp.int32)
    expert_ids = jnp.arange(experts_all, dtype=jnp.int32)
    gathered = (
        lax.all_gather(gain_attn, "ep", axis=0, tiled=True),
        lax.all_gather(w_query, "ep", axis=0, tiled=True),
        lax.all_gather(w_key, "ep", axis=0, tiled=True),
        lax.all_gather(w_value, "ep", axis=0, tiled=True),
        lax.all_gather(w_output, "ep", axis=1, tiled=True),
        lax.all_gather(gain_moe, "ep", axis=0, tiled=True),
        lax.all_gather(w_router, "ep", axis=0, tiled=True),
    )
    gain_one = gathered[0].astype(jnp.float32)
    w_proj = jnp.concatenate([gathered[1], gathered[2], gathered[3]], 1)
    w_out_full = gathered[4]
    gain_two = gathered[5].astype(jnp.float32)
    w_route_full = gathered[6]
    totals = None
    mixed_rows = []
    grad_rows = []
    for micro_index in range(micro_count):
        starts = piece_starts[micro_index]
        key_pieces = piece_index(starts, all_pos)
        row_piece = jnp.tile(piece_index(starts, local_pos), group_size)
        x_rows = tokens[micro_index].astype(jnp.float32)
        scale_one = rms_scale(x_rows)
        normed = (x_rows * scale_one * gain_one).astype(jnp.bfloat16)
        normed_all = lax.all_gather(normed, "tp", axis=0, tiled=True)
        projected = jnp.dot(normed_all, w_proj, preferred_element_type=jnp.float32)
        queries = rotate(
            projected[:, :q_cols].reshape(span_rows, -1, HEAD_DIM), cosine, sine
        ).astype(jnp.bfloat16)
        q_grouped = to_groups(queries.reshape(span_rows, q_cols), kv_here, group_size)
        keys_own = (
            rotate(
                projected[:, q_cols : q_cols + kv_cols].reshape(span_rows, kv_here, HEAD_DIM),
                cosine,
                sine,
            )
            .astype(jnp.bfloat16)
            .reshape(span_rows, kv_cols)
        )
        values_own = projected[:, q_cols + kv_cols :].astype(jnp.bfloat16)
        keys_all, values_all = (
            lax.all_gather(keys_own, "ep", axis=0, tiled=True),
            lax.all_gather(values_own, "ep", axis=0, tiled=True),
        )

        def block_scores(first_row, block_size):
            key_blk = lax.dynamic_slice_in_dim(keys_all, first_row, block_size, 0).reshape(
                block_size, kv_here, HEAD_DIM
            )
            value_blk = lax.dynamic_slice_in_dim(values_all, first_row, block_size, 0).reshape(
                block_size, kv_here, HEAD_DIM
            )
            key_pos = first_row + jnp.arange(block_size, dtype=jnp.int32)
            piece_blk = lax.dynamic_slice_in_dim(key_pieces, first_row, block_size, 0)
            allowed = allowed_mask(row_pos, row_piece, key_pos, piece_blk)[None]
            scores = (
                jnp.einsum("hrd,khd->hrk", q_grouped, key_blk, preferred_element_type=jnp.float32)
                * score_scale
            )
            return (scores, allowed, key_blk, value_blk)

        def forward_step(block_index, running):
            run_max, run_sum, run_acc = running
            scores, allowed, key_blk, value_blk = block_scores(block_index * key_block, key_block)
            scores = jnp.where(allowed, scores, NEG)
            new_max = jnp.maximum(run_max, jnp.max(scores, -1))
            weights = jnp.where(allowed, jnp.exp(scores - new_max[..., None]), 0.0)
            factor = jnp.exp(run_max - new_max)
            run_sum = run_sum * factor + jnp.sum(weights, -1)
            run_acc = run_acc * factor[..., None] + jnp.einsum(
                "hrk,khd->hrd",
                weights.astype(jnp.bfloat16),
                value_blk,
                preferred_element_type=jnp.float32,
            )
            return (new_max, run_sum, run_acc)

        start_state = (
            jnp.full((kv_here, query_rows), NEG, jnp.float32),
            jnp.zeros((kv_here, query_rows), jnp.float32),
            jnp.zeros((kv_here, query_rows, HEAD_DIM), jnp.float32),
        )
        run_max, run_sum, run_acc = lax.fori_loop(0, block_count, forward_step, start_state)
        log_total = run_max + jnp.log(run_sum)
        attended_f = run_acc / run_sum[..., None]
        attended = from_groups(attended_f.astype(jnp.bfloat16), span_rows)
        partial_attn = jnp.dot(attended, w_out_full, preferred_element_type=jnp.float32)
        attn_rows = lax.psum_scatter(
            partial_attn.astype(jnp.bfloat16), "tp", scatter_dimension=0, tiled=True
        ).astype(jnp.float32)
        resid = x_rows + attn_rows
        scale_two = rms_scale(resid)
        normed_two = (resid * scale_two * gain_two).astype(jnp.bfloat16)
        logits = jnp.dot(normed_two, w_route_full, preferred_element_type=jnp.float32)
        route_rows = routes[micro_index]
        route_hot = (route_rows[:, :, None] == expert_ids[None, None, :]).astype(jnp.float32)
        picked = jnp.sum(route_hot * logits[:, None, :], -1)
        highest = jnp.max(picked, -1, keepdims=True)
        raised = jnp.exp(picked - highest)
        gates = raised / jnp.sum(raised, -1, keepdims=True)
        flat_hot = route_hot.reshape(-1, experts_all)
        earlier = jnp.cumsum(flat_hot, 0) - flat_hot
        slot_of = jnp.sum(earlier * flat_hot, -1).astype(jnp.int32)
        target = route_rows.reshape(-1) * capacity + slot_of
        place_pairs = slot_ids[:, None] == target[None, :]
        place_pairs_b = place_pairs.astype(jnp.bfloat16)
        place_tokens = jnp.any(place_pairs.reshape(-1, slice_rows, top_count), -1).astype(
            jnp.bfloat16
        )
        send_rows = (
            jnp.dot(place_tokens, normed_two, preferred_element_type=jnp.float32)
            .astype(jnp.bfloat16)
            .reshape(ep_count, experts_here, capacity, width)
        )
        received = lax.all_to_all(send_rows, "ep", split_axis=0, concat_axis=0, tiled=True)
        expert_in = jnp.swapaxes(received, 0, 1).reshape(experts_here, expert_rows, width)
        gate_pre = jnp.einsum("erd,edf->erf", expert_in, w_gate, preferred_element_type=jnp.float32)
        up_pre = jnp.einsum("erd,edf->erf", expert_in, w_up, preferred_element_type=jnp.float32)
        sigmoid_val = jax.nn.sigmoid(gate_pre)
        silu_val = gate_pre * sigmoid_val
        hidden = (silu_val * up_pre).astype(jnp.bfloat16)
        expert_out = jnp.einsum(
            "erf,efd->erd", hidden, w_down, preferred_element_type=jnp.float32
        ).astype(jnp.bfloat16)
        returned = lax.all_to_all(
            jnp.swapaxes(expert_out.reshape(experts_here, ep_count, capacity, width), 0, 1),
            "ep",
            split_axis=0,
            concat_axis=0,
            tiled=True,
        )
        slot_rows = returned.reshape(-1, width)
        picked_rows = jnp.einsum(
            "sn,sd->nd", place_pairs_b, slot_rows, preferred_element_type=jnp.float32
        ).reshape(slice_rows, top_count, width)
        mixture = jnp.einsum("tk,tkd->td", gates, picked_rows)
        mixed_rows.append((resid + mixture).astype(jnp.bfloat16))
        grad_out = cotangent[micro_index].astype(jnp.float32)
        grad_gates = jnp.einsum("tkd,td->tk", picked_rows, grad_out)
        weighted = (
            (gates[:, :, None] * grad_out[:, None, :]).astype(jnp.bfloat16).reshape(-1, width)
        )
        grad_slots = (
            jnp.dot(place_pairs_b, weighted, preferred_element_type=jnp.float32)
            .astype(jnp.bfloat16)
            .reshape(ep_count, experts_here, capacity, width)
        )
        grad_recv = lax.all_to_all(grad_slots, "ep", split_axis=0, concat_axis=0, tiled=True)
        grad_expert = jnp.swapaxes(grad_recv, 0, 1).reshape(experts_here, expert_rows, width)
        grad_hidden = jnp.einsum(
            "erd,efd->erf", grad_expert, w_down, preferred_element_type=jnp.float32
        )
        grad_down_w = jnp.einsum(
            "erf,erd->efd", hidden, grad_expert, preferred_element_type=jnp.float32
        )
        silu_slope = sigmoid_val * (1.0 + gate_pre * (1.0 - sigmoid_val))
        grad_gate_pre = (grad_hidden * up_pre * silu_slope).astype(jnp.bfloat16)
        grad_up_pre = (grad_hidden * silu_val).astype(jnp.bfloat16)
        grad_gate_w = jnp.einsum(
            "erd,erf->edf", expert_in, grad_gate_pre, preferred_element_type=jnp.float32
        )
        grad_up_w = jnp.einsum(
            "erd,erf->edf", expert_in, grad_up_pre, preferred_element_type=jnp.float32
        )
        grad_copy = (
            jnp.einsum("erf,edf->erd", grad_gate_pre, w_gate, preferred_element_type=jnp.float32)
            + jnp.einsum("erf,edf->erd", grad_up_pre, w_up, preferred_element_type=jnp.float32)
        ).astype(jnp.bfloat16)
        grad_back = lax.all_to_all(
            jnp.swapaxes(grad_copy.reshape(experts_here, ep_count, capacity, width), 0, 1),
            "ep",
            split_axis=0,
            concat_axis=0,
            tiled=True,
        ).reshape(-1, width)
        grad_spread = gates * (grad_gates - jnp.sum(gates * grad_gates, -1, keepdims=True))
        grad_logits = jnp.einsum("tk,tke->te", grad_spread, route_hot).astype(jnp.bfloat16)
        grad_normed_two = jnp.einsum(
            "st,sd->td", place_tokens, grad_back, preferred_element_type=jnp.float32
        ) + jnp.einsum("te,de->td", grad_logits, w_route_full, preferred_element_type=jnp.float32)
        grad_route = jnp.einsum(
            "td,te->de", normed_two, grad_logits, preferred_element_type=jnp.float32
        )
        gained_two = grad_normed_two * gain_two
        grad_gain_two = jnp.sum(grad_normed_two * resid * scale_two, 0)
        grad_resid = (
            grad_out
            + scale_two * gained_two
            - resid * scale_two**3 * jnp.mean(resid * gained_two, -1, keepdims=True)
        )
        grad_attn = lax.all_gather(grad_resid.astype(jnp.bfloat16), "tp", axis=0, tiled=True)
        grad_outw = jnp.einsum("cq,cd->qd", attended, grad_attn, preferred_element_type=jnp.float32)
        grad_att_rows = jnp.einsum(
            "cd,qd->cq", grad_attn, w_out_full, preferred_element_type=jnp.float32
        ).astype(jnp.bfloat16)
        grad_grouped = to_groups(grad_att_rows, kv_here, group_size)
        delta = jnp.sum(grad_grouped.astype(jnp.float32) * attended_f, -1)

        def block_grads(first_row, block_size):
            scores, allowed, key_blk, value_blk = block_scores(first_row, block_size)
            probs = jnp.where(allowed, jnp.exp(scores - log_total[..., None]), 0.0)
            grad_probs = jnp.einsum(
                "hrd,khd->hrk", grad_grouped, value_blk, preferred_element_type=jnp.float32
            )
            grad_scores = (probs * (grad_probs - delta[..., None])).astype(jnp.bfloat16)
            return (probs, grad_scores, key_blk)

        def key_side(first_row, block_size):
            probs, grad_scores, key_blk = block_grads(first_row, block_size)
            grad_keys = (
                jnp.einsum(
                    "hrk,hrd->khd", grad_scores, q_grouped, preferred_element_type=jnp.float32
                ).reshape(block_size, kv_cols)
                * score_scale
            )
            grad_values = jnp.einsum(
                "hrk,hrd->khd",
                probs.astype(jnp.bfloat16),
                grad_grouped,
                preferred_element_type=jnp.float32,
            ).reshape(block_size, kv_cols)
            return (jnp.concatenate([grad_keys, grad_values], 1), grad_scores, key_blk)

        query_zero = jnp.zeros((kv_here, query_rows, HEAD_DIM), jnp.float32)

        def backward_step(block_index, running):
            grad_query, grad_kv = running
            first_row = block_index * key_block
            kv_terms, grad_scores, key_blk = key_side(first_row, key_block)
            grad_query = grad_query + jnp.einsum(
                "hrk,khd->hrd", grad_scores, key_blk, preferred_element_type=jnp.float32
            )
            grad_kv = lax.dynamic_update_slice_in_dim(grad_kv, kv_terms, first_row, 0)
            return (grad_query, grad_kv)

        grad_query, grad_kv = lax.fori_loop(
            0,
            block_count,
            backward_step,
            (query_zero, jnp.zeros((seq_len, 2 * kv_cols), jnp.float32)),
        )
        grad_kv_own = lax.psum_scatter(
            grad_kv.astype(jnp.bfloat16), "ep", scatter_dimension=0, tiled=True
        ).astype(jnp.float32)
        grad_query_rows = from_groups(grad_query * score_scale, span_rows).reshape(
            span_rows, -1, HEAD_DIM
        )
        grad_query_raw = (
            rotate(grad_query_rows, cosine, -sine).astype(jnp.bfloat16).reshape(span_rows, q_cols)
        )
        grad_key_raw = (
            rotate(grad_kv_own[:, :kv_cols].reshape(span_rows, kv_here, HEAD_DIM), cosine, -sine)
            .astype(jnp.bfloat16)
            .reshape(span_rows, kv_cols)
        )
        grad_value_raw = grad_kv_own[:, kv_cols:].astype(jnp.bfloat16)
        grad_proj_rows = jnp.concatenate([grad_query_raw, grad_key_raw, grad_value_raw], 1)
        grad_proj = jnp.einsum(
            "cd,cp->dp", normed_all, grad_proj_rows, preferred_element_type=jnp.float32
        )
        grad_normed_part = jnp.einsum(
            "cp,dp->cd", grad_proj_rows, w_proj, preferred_element_type=jnp.float32
        )
        grad_normed = lax.psum_scatter(
            grad_normed_part.astype(jnp.bfloat16), "tp", scatter_dimension=0, tiled=True
        ).astype(jnp.float32)
        gained_one = grad_normed * gain_one
        grad_gain_one = jnp.sum(grad_normed * x_rows * scale_one, 0)
        grad_rows.append(
            grad_resid
            + scale_one * gained_one
            - x_rows * scale_one**3 * jnp.mean(x_rows * gained_one, -1, keepdims=True)
        )
        parts = (
            grad_gate_w,
            grad_up_w,
            grad_down_w,
            grad_gain_one,
            grad_gain_two,
            grad_route,
            grad_proj,
            grad_outw,
        )
        reduced = reduce_grads(parts, ep_count, tp_count)
        totals = reduced if totals is None else add_all(totals, reduced)
    grad_qkv = totals[6]
    return (
        jnp.stack(mixed_rows),
        jnp.stack(grad_rows),
        totals[3],
        grad_qkv[:, :q_cols],
        grad_qkv[:, q_cols : q_cols + kv_cols],
        grad_qkv[:, q_cols + kv_cols :],
        totals[7],
        totals[4],
        totals[5],
        totals[0],
        totals[1],
        totals[2],
    )


def dot_f32(left, right, left_dim, right_dim):
    return lax.dot_general(
        left, right, (((left_dim,), (right_dim,)), ((), ())), preferred_element_type=jnp.float32
    )


def at_rows(first_row, count):
    return pl.ds(pl.multiple_of(first_row, count), count)


def whole_vmem():
    return pl.BlockSpec(memory_space=pltpu.VMEM)


def attend_kernel(
    tp_ref, own_ref, other_ref, limit_ref, out_ref, out_f_ref, log_ref, keys, queries, values,
    *, query_block, key_block
):
    core = tp_ref[0]
    blocks, _, rows = own_ref.shape
    seq_len = blocks * rows

    def fill(block, _):
        cols = at_rows(block * rows, rows)
        first, second = own_ref[block, HEAD_DIM:, :], other_ref[block]
        key_rows = jnp.where(core == 0, first, second)
        queries[:, cols] = own_ref[block, :HEAD_DIM, :]
        values[:HEAD_DIM, cols] = jnp.where(core == 0, second, first)
        values[HEAD_DIM:, cols] = jnp.ones((16, rows), jnp.bfloat16)
        keys[cols, :] = key_rows.astype(jnp.float32).T.astype(jnp.bfloat16)
        return 0

    lax.fori_loop(0, blocks, fill, 0)

    def update(scores, value_cols, carry):
        highest, total = carry
        new_highest = jnp.maximum(highest, jnp.max(scores, 0, keepdims=True) * EXP_SCALE)
        weights = jnp.exp2(scores * EXP_SCALE - new_highest).astype(jnp.bfloat16)
        factor = jnp.exp2(highest - new_highest)
        return (new_highest, total * factor + dot_f32(value_cols, weights, 1, 0))

    def query_step(index, _):
        first = index * query_block
        cols = at_rows(first, query_block)
        query = queries[:, cols]
        limit = limit_ref[:, cols]

        def full_step(step, carry):
            key_cols = at_rows(step * key_block, key_block)
            return update(
                dot_f32(keys[key_cols, :], query, 1, 0), values[:, key_cols], carry
            )

        carry = lax.fori_loop(
            0,
            first // key_block,
            full_step,
            (
                jnp.full((1, query_block), NEG, jnp.float32),
                jnp.zeros((HEAD_DIM + 16, query_block), jnp.float32),
            ),
        )
        scores = dot_f32(keys[cols, :], query, 1, 0)
        key_pos = first + lax.broadcasted_iota(jnp.int32, scores.shape, 0)
        highest, total = update(
            jnp.where(key_pos <= limit, scores, NEG), values[:, cols], carry
        )
        last = query_block - rows
        after = at_rows(jnp.minimum(first + query_block, seq_len - rows), rows)
        scores = dot_f32(keys[after, :], query[:, last:], 1, 0)
        key_pos = first + query_block + lax.broadcasted_iota(jnp.int32, scores.shape, 0)
        tail_highest, tail_total = update(
            jnp.where(key_pos <= limit[:, last:], scores, NEG),
            values[:, after],
            (highest[:, last:], total[:, last:]),
        )
        per_step = query_block // rows
        for piece in range(per_step):
            here = slice(piece * rows, (piece + 1) * rows)
            high, both = highest[:, here], total[:, here]
            if piece == per_step - 1:
                high, both = tail_highest, tail_total
            row_sum = both[HEAD_DIM : HEAD_DIM + 1, :]
            result = both[:HEAD_DIM, :] / row_sum
            block = index * per_step + piece
            out_ref[block] = result.astype(jnp.bfloat16)
            out_f_ref[block] = result
            log_ref[:, at_rows(first + piece * rows, rows)] = high + jnp.log2(row_sum)
        return 0

    lax.fori_loop(0, seq_len // query_block, query_step, 0)


def attend(core, own, other, limit):
    blocks, _, rows = own.shape
    seq_len = blocks * rows
    query_block = math.gcd(seq_len, 2048)
    key_block = math.gcd(query_block, 1024)
    block_shape = (blocks, HEAD_DIM, rows)
    return pl.pallas_call(
        functools.partial(attend_kernel, query_block=query_block, key_block=key_block),
        out_shape=(
            jax.ShapeDtypeStruct(block_shape, jnp.bfloat16),
            jax.ShapeDtypeStruct(block_shape, jnp.float32),
            jax.ShapeDtypeStruct((1, seq_len), jnp.float32),
        ),
        in_specs=[pl.BlockSpec(memory_space=pltpu.SMEM)] + [whole_vmem()] * 3,
        out_specs=(whole_vmem(),) * 3,
        scratch_shapes=[
            pltpu.VMEM((seq_len, HEAD_DIM), jnp.bfloat16),
            pltpu.VMEM((HEAD_DIM, seq_len), jnp.bfloat16),
            pltpu.VMEM((HEAD_DIM + 16, seq_len), jnp.bfloat16),
        ],
        cost_estimate=pl.CostEstimate(
            flops=seq_len * seq_len * 512, bytes_accessed=8 * MIB, transcendentals=0
        ),
        compiler_params=pltpu.CompilerParams(vmem_limit_bytes=56 * MIB),
        name="attend",
    )(core, own, other, limit)


def three_parts(values):
    high = values.astype(jnp.bfloat16).astype(jnp.float32)
    middle = (values - high).astype(jnp.bfloat16).astype(jnp.float32)
    low = values - high - middle
    row = lax.broadcasted_iota(jnp.int32, (16, values.shape[1]), 0)
    parts = jnp.where(
        row == 0, high, jnp.where(row == 1, middle, jnp.where(row == 2, low, 0.0))
    )
    return parts.astype(jnp.bfloat16)


def attend_back_kernel(
    tp_ref, own_ref, other_ref, limit_ref, out_f_ref, log_ref, grad_ref,
    grad_q_ref, keep_ref, send_ref,
    keys, keys_t, queries_t, queries, values, grads_t, grads, grad_k, grad_v,
    *, query_block, key_block
):
    core = tp_ref[0]
    blocks, _, rows = own_ref.shape
    seq_len = blocks * rows

    def fill(block, _):
        cols = at_rows(block * rows, rows)
        first, second = own_ref[block, HEAD_DIM:, :], other_ref[block]
        key_rows = jnp.where(core == 0, first, second)
        value_rows = jnp.where(core == 0, second, first)
        query, grad = own_ref[block, :HEAD_DIM, :], grad_ref[block]
        grad_f = grad.astype(jnp.float32)
        delta = jnp.sum(grad_f * out_f_ref[block], 0, keepdims=True)
        ones = jnp.ones((16, rows), jnp.float32)
        queries_t[:HEAD_DIM, cols] = query
        queries_t[HEAD_DIM:, cols] = three_parts(log_ref[:, cols] * (-1.0 / EXP_SCALE))
        queries[cols, :] = query.astype(jnp.float32).T.astype(jnp.bfloat16)
        keys_t[:, cols] = key_rows
        keys[cols, :] = (
            jnp.concatenate([key_rows.astype(jnp.float32), ones], 0).T.astype(jnp.bfloat16)
        )
        values[cols, :] = (
            jnp.concatenate([value_rows.astype(jnp.float32), ones], 0).T.astype(jnp.bfloat16)
        )
        grads_t[:HEAD_DIM, cols] = grad
        grads_t[HEAD_DIM:, cols] = three_parts(-delta)
        grads[cols, :] = grad_f.T.astype(jnp.bfloat16)
        grad_k[cols, :] = jnp.zeros((rows, HEAD_DIM), jnp.float32)
        grad_v[cols, :] = jnp.zeros((rows, HEAD_DIM), jnp.float32)
        return 0

    lax.fori_loop(0, blocks, fill, 0)

    def tile(operands, key_cols, allowed):
        query_t, query, grad_t, grad = operands
        probs = jnp.exp2(dot_f32(keys[key_cols, :], query_t, 1, 0) * EXP_SCALE)
        if allowed is not None:
            probs = jnp.where(allowed, probs, 0.0)
        grad_scores = (probs * dot_f32(values[key_cols, :], grad_t, 1, 0)).astype(jnp.bfloat16)
        grad_v[key_cols, :] += dot_f32(probs.astype(jnp.bfloat16), grad, 1, 0)
        grad_k[key_cols, :] += dot_f32(grad_scores, query, 1, 0)
        return dot_f32(keys_t[:, key_cols], grad_scores, 1, 0)

    def query_step(index, _):
        first = index * query_block
        cols = at_rows(first, query_block)
        limit = limit_ref[:, cols]
        operands = (queries_t[:, cols], queries[cols, :], grads_t[:, cols], grads[cols, :])

        def full_step(step, total):
            return total + tile(operands, at_rows(step * key_block, key_block), None)

        total = lax.fori_loop(
            0, first // key_block, full_step, jnp.zeros((HEAD_DIM, query_block), jnp.float32)
        )
        key_pos = first + lax.broadcasted_iota(jnp.int32, (query_block, query_block), 0)
        total = total + tile(operands, cols, key_pos <= limit)
        last = query_block - rows
        after = at_rows(jnp.minimum(first + query_block, seq_len - rows), rows)
        key_pos = first + query_block + lax.broadcasted_iota(jnp.int32, (rows, rows), 0)
        query_t, query, grad_t, grad = operands
        extra = tile(
            (query_t[:, last:], query[last:], grad_t[:, last:], grad[last:]),
            after,
            key_pos <= limit[:, last:],
        )
        per_step = query_block // rows
        for piece in range(per_step):
            here = total[:, piece * rows : (piece + 1) * rows]
            if piece == per_step - 1:
                here = here + extra
            grad_q_ref[index * per_step + piece] = (here * HEAD_DIM ** (-0.5)).astype(
                jnp.bfloat16
            )
        return 0

    lax.fori_loop(0, seq_len // query_block, query_step, 0)

    def finish(block, _):
        cols = at_rows(block * rows, rows)
        key_part = (grad_k[cols, :] * HEAD_DIM ** (-0.5)).T
        value_part = grad_v[cols, :].T
        keep_ref[block] = jnp.where(core == 0, key_part, value_part)
        send_ref[block] = jnp.where(core == 0, value_part, key_part).astype(jnp.bfloat16)
        return 0

    lax.fori_loop(0, blocks, finish, 0)


def attend_back(core, own, other, limit, out_f, log_total, grad):
    blocks, _, rows = own.shape
    seq_len = blocks * rows
    query_block = math.gcd(seq_len, 1024)
    key_block = math.gcd(query_block, 1024)
    block_shape = (blocks, HEAD_DIM, rows)
    wide = HEAD_DIM + 16
    return pl.pallas_call(
        functools.partial(attend_back_kernel, query_block=query_block, key_block=key_block),
        out_shape=(
            jax.ShapeDtypeStruct(block_shape, jnp.bfloat16),
            jax.ShapeDtypeStruct(block_shape, jnp.float32),
            jax.ShapeDtypeStruct(block_shape, jnp.bfloat16),
        ),
        in_specs=[pl.BlockSpec(memory_space=pltpu.SMEM)] + [whole_vmem()] * 6,
        out_specs=(whole_vmem(),) * 3,
        scratch_shapes=[
            pltpu.VMEM((seq_len, wide), jnp.bfloat16),
            pltpu.VMEM((HEAD_DIM, seq_len), jnp.bfloat16),
            pltpu.VMEM((wide, seq_len), jnp.bfloat16),
            pltpu.VMEM((seq_len, HEAD_DIM), jnp.bfloat16),
            pltpu.VMEM((seq_len, wide), jnp.bfloat16),
            pltpu.VMEM((wide, seq_len), jnp.bfloat16),
            pltpu.VMEM((seq_len, HEAD_DIM), jnp.bfloat16),
            pltpu.VMEM((seq_len, HEAD_DIM), jnp.float32),
            pltpu.VMEM((seq_len, HEAD_DIM), jnp.float32),
        ],
        cost_estimate=pl.CostEstimate(
            flops=seq_len * seq_len * 1024, bytes_accessed=12 * MIB, transcendentals=0
        ),
        compiler_params=pltpu.CompilerParams(vmem_limit_bytes=60 * MIB),
        name="attend_back",
    )(core, own, other, limit, out_f, log_total, grad)


def experts_kernel(
    tp_ref, x_ref, dy_ref, gate_ref, w_gate_ref, w_up_ref, w_down_ref, keep_in_ref, send_in_ref,
    mix_ref, grad_x_ref, grad_gate_ref, keep_ref, send_ref,
    x_t, dy_t, mix_sum, grad_x_sum, grad_w,
    *, tile_rows, first_call
):
    expert, expert_count = pl.program_id(0), pl.num_programs(0)
    rows, width = x_ref.shape
    half = width // 2
    core = tp_ref[0]
    tiles = rows // tile_rows

    @pl.when(expert == 0)
    def _():
        def turn(index, _):
            here = at_rows(index * tile_rows, tile_rows)
            x_t[:, here] = x_ref[here, :].T
            dy_t[:, here] = dy_ref[here, :].T
            mix_sum[here, :] = jnp.zeros((tile_rows, width), jnp.float32)
            grad_x_sum[here, :] = jnp.zeros((tile_rows, width), jnp.float32)
            return 0

        lax.fori_loop(0, tiles, turn, 0)

    if first_call:
        grad_w[...] = jnp.zeros_like(grad_w)
    else:
        for part in range(2):
            grad_w[part] = jnp.where(core == part, keep_in_ref[0], send_in_ref[0]).astype(
                jnp.float32
            )
    w_gate, w_up, w_down = w_gate_ref[0], w_up_ref[0], w_down_ref[0]

    def tile(index, _):
        here = at_rows(index * tile_rows, tile_rows)
        x = x_ref[here, :]
        dy = dy_ref[here, :].astype(jnp.float32)
        gate = gate_ref[0, here, :]
        gate_pre = dot_f32(x, w_gate, 1, 0)
        up_pre = dot_f32(x, w_up, 1, 0)
        sigmoid_val = 1.0 / (1.0 + jnp.exp(-gate_pre))
        silu_val = gate_pre * sigmoid_val
        hidden = (silu_val * up_pre).astype(jnp.bfloat16)
        out = dot_f32(hidden, w_down, 1, 0).astype(jnp.bfloat16).astype(jnp.float32)
        grad_gate_ref[0, here, :] = jnp.sum(out * dy, 1, keepdims=True)
        mix_sum[here, :] += gate * out
        grad_out = (gate * dy).astype(jnp.bfloat16)
        grad_hidden = dot_f32(grad_out, w_down, 1, 1)
        slope = sigmoid_val * (1.0 + gate_pre * (1.0 - sigmoid_val))
        grad_gate_pre = (grad_hidden * up_pre * slope).astype(jnp.bfloat16)
        grad_up_pre = (grad_hidden * silu_val).astype(jnp.bfloat16)
        grad_copy = dot_f32(grad_gate_pre, w_gate, 1, 1) + dot_f32(grad_up_pre, w_up, 1, 1)
        grad_x_sum[here, :] += grad_copy.astype(jnp.bfloat16).astype(jnp.float32)
        grad_out_t = (dy_t[:, here].astype(jnp.float32) * gate.T).astype(jnp.bfloat16)
        for part in range(2):
            cut = slice(part * half, (part + 1) * half)
            turned = x_t[cut, here]
            grad_w[part, 0] += dot_f32(turned, grad_gate_pre, 1, 0)
            grad_w[part, 1] += dot_f32(turned, grad_up_pre, 1, 0)
            grad_w[part, 2] += dot_f32(grad_out_t[cut], hidden, 1, 0)
        return 0

    lax.fori_loop(0, tiles, tile, 0)
    keep_ref[0] = grad_w[core].astype(jnp.bfloat16)
    send_ref[0] = grad_w[1 - core].astype(jnp.bfloat16)

    @pl.when(expert == expert_count - 1)
    def _():
        mix_ref[...] = mix_sum[...].astype(jnp.bfloat16)
        grad_x_ref[...] = grad_x_sum[...].astype(jnp.bfloat16)


def experts(core, x, dy, gates, w_gate, w_up, w_down, before):
    count, width, hidden_width = w_gate.shape
    rows = x.shape[0]
    half = width // 2
    first_call = before is None
    if first_call:
        before = (jnp.zeros((1, 3, 16, hidden_width), jnp.bfloat16),) * 2
        before_spec = pl.BlockSpec((1, 3, 16, hidden_width), lambda expert: (0, 0, 0, 0))
    else:
        before_spec = pl.BlockSpec((1, 3, half, hidden_width), lambda expert: (expert, 0, 0, 0))
    row_spec = pl.BlockSpec((rows, width), lambda expert: (0, 0))
    gate_spec = pl.BlockSpec((1, rows, 1), lambda expert: (expert, 0, 0))
    grad_spec = pl.BlockSpec((1, 3, half, hidden_width), lambda expert: (expert, 0, 0, 0))
    in_spec = pl.BlockSpec((1, width, hidden_width), lambda expert: (expert, 0, 0))
    out_spec = pl.BlockSpec((1, hidden_width, width), lambda expert: (expert, 0, 0))
    grad_shape = jax.ShapeDtypeStruct((count, 3, half, hidden_width), jnp.bfloat16)
    row_shape = jax.ShapeDtypeStruct((rows, width), jnp.bfloat16)
    return pl.pallas_call(
        functools.partial(
            experts_kernel, tile_rows=math.gcd(rows, 512), first_call=first_call
        ),
        grid=(count,),
        out_shape=(
            row_shape,
            row_shape,
            jax.ShapeDtypeStruct((count, rows, 1), jnp.float32),
            grad_shape,
            grad_shape,
        ),
        in_specs=[
            pl.BlockSpec(memory_space=pltpu.SMEM),
            row_spec,
            row_spec,
            gate_spec,
            in_spec,
            in_spec,
            out_spec,
            before_spec,
            before_spec,
        ],
        out_specs=(row_spec, row_spec, gate_spec, grad_spec, grad_spec),
        scratch_shapes=[
            pltpu.VMEM((width, rows), jnp.bfloat16),
            pltpu.VMEM((width, rows), jnp.bfloat16),
            pltpu.VMEM((rows, width), jnp.float32),
            pltpu.VMEM((rows, width), jnp.float32),
            pltpu.VMEM((2, 3, half, hidden_width), jnp.float32),
        ],
        cost_estimate=pl.CostEstimate(
            flops=count * rows * width * hidden_width * 18,
            bytes_accessed=count * width * hidden_width * 12,
            transcendentals=0,
        ),
        compiler_params=pltpu.CompilerParams(
            vmem_limit_bytes=60 * MIB, dimension_semantics=("arbitrary",)
        ),
        name="experts",
    )(core, x, dy, gates, w_gate, w_up, w_down, *before)


def flip(values, bits):
    count = lax.axis_size("ep")
    return lax.ppermute(values, "ep", [(index, index ^ bits) for index in range(count)])


def swap_cores(values):
    return lax.ppermute(values, "tp", [(0, 1), (1, 0)])


def every_device(values):
    return lax.all_to_all(values, ("ep", "tp"), 0, 0, tiled=True)


def head_tables(first_pos, rows):
    positions = first_pos + jnp.arange(rows, dtype=jnp.int32)
    halves = jnp.arange(HEAD_DIM // 2, dtype=jnp.float32)
    freqs = THETA ** (-2.0 * halves / HEAD_DIM)
    angles = freqs[:, None] * positions.astype(jnp.float32)[None, :]
    turned = jnp.array([[True, True], [True, False]])[:, :, None, None]
    cosine = jnp.where(turned, jnp.cos(angles), 1.0)
    sine = jnp.where(turned, jnp.sin(angles), 0.0)
    return cosine, sine


def rotate_heads(heads, cosine, sine):
    first_half, second_half = heads[..., 0, :, :], heads[..., 1, :, :]
    return jnp.stack(
        [first_half * cosine - second_half * sine, second_half * cosine + first_half * sine], -3
    )


def paired_layout(ep_count, tp_count, micro_count, slice_rows, width, q_cols, kv_cols, experts_here):
    group = q_cols // kv_cols
    kv_heads = kv_cols * tp_count // HEAD_DIM
    return (
        tp_count == 2
        and group == 2
        and ep_count == micro_count * kv_heads
        and ep_count == PLANE * PLANE
        and experts_here == 1
        and slice_rows >= PIECE
        and slice_rows % PIECE == 0
        and width % (2 * LANES) == 0
    )


def on_device_paired(
    tokens,
    gain_attn,
    w_query,
    w_key,
    w_value,
    w_output,
    gain_moe,
    w_router,
    w_gate,
    w_up,
    w_down,
    routes,
    piece_starts,
    cotangent,
):
    ep_count = lax.axis_size("ep")
    tp_count = lax.axis_size("tp")
    ep_index, tp_index = lax.axis_index("ep"), lax.axis_index("tp")
    micro_count, rows, width = tokens.shape
    devices = ep_count * tp_count
    seq_len = rows * devices
    all_rows = micro_count * rows
    shard = gain_attn.shape[0]
    q_cols, kv_cols = w_query.shape[1], w_key.shape[1]
    kv_here = kv_cols // HEAD_DIM
    half_cols = q_cols + 2 * kv_cols
    out_cols = w_output.shape[0]
    columns = ep_count // PLANE
    experts_all = ep_count
    core = tp_index.astype(jnp.int32).reshape(1)

    head_cols = jnp.stack(
        [
            w_query.reshape(shard, kv_here, 2, HEAD_DIM),
            jnp.stack(
                [
                    w_key.reshape(shard, kv_here, HEAD_DIM),
                    w_value.reshape(shard, kv_here, HEAD_DIM),
                ],
                2,
            ),
        ],
        3,
    ).reshape(shard, half_cols)
    small = jnp.concatenate([w_router, gain_attn[:, None], gain_moe[:, None]], 1)
    small = jnp.pad(small, ((0, 0), (0, LANES - small.shape[1])))
    packed = jnp.concatenate([head_cols, w_output.T, small], 1)
    gathered = lax.all_gather(packed, ("ep", "tp"), axis=0, tiled=False).reshape(
        ep_count, tp_count, shard, -1
    )
    w_heads = [gathered[:, part, :, :half_cols].reshape(width, half_cols) for part in range(2)]
    w_out_t = jnp.concatenate(
        [
            gathered[:, part, :, half_cols : half_cols + out_cols].reshape(width, out_cols)
            for part in range(2)
        ],
        1,
    )
    small_all = gathered[:, 0, :, half_cols + out_cols :].reshape(width, LANES)
    w_route_full = small_all[:, :experts_all]
    gain_one = small_all[:, experts_all].astype(jnp.float32)
    gain_two = small_all[:, experts_all + 1].astype(jnp.float32)

    half = width // 2
    expert_half = jnp.where(
        tp_index == 0,
        jnp.concatenate([w_gate[0, :half], w_up[0, :half], w_down[0, :, :half].T], 0),
        jnp.concatenate([w_gate[0, half:], w_up[0, half:], w_down[0, :, half:].T], 0),
    )
    column_halves = jnp.stack([flip(expert_half, PLANE * step) for step in range(1, columns)])
    column_others = swap_cores(column_halves)
    low = jnp.where(tp_index == 0, column_halves, column_others)
    high = jnp.where(tp_index == 0, column_others, column_halves)
    hidden_width = w_gate.shape[2]
    low = low.reshape(columns - 1, 3, half, hidden_width)
    high = high.reshape(columns - 1, 3, half, hidden_width)
    gate_cols = jnp.concatenate([w_gate, jnp.concatenate([low[:, 0], high[:, 0]], 1)], 0)
    up_cols = jnp.concatenate([w_up, jnp.concatenate([low[:, 1], high[:, 1]], 1)], 0)
    down_cols = jnp.concatenate(
        [
            w_down,
            jnp.concatenate([jnp.swapaxes(low[:, 2], 1, 2), jnp.swapaxes(high[:, 2], 1, 2)], 2),
        ],
        0,
    )

    dy_plane = [
        jnp.concatenate(
            [cotangent[micro]] + [flip(cotangent[micro], step) for step in range(1, PLANE)], 0
        )
        for micro in range(micro_count)
    ]

    x_rows = tokens.reshape(all_rows, width).astype(jnp.float32)
    scale_one = rms_scale(x_rows)
    normed = (x_rows * scale_one * gain_one).astype(jnp.bfloat16)
    device_index = ep_index * tp_count + tp_index
    cosine, sine = head_tables(device_index * rows, rows)
    sent = []
    for micro in range(micro_count):
        here = normed[micro * rows : (micro + 1) * rows]
        for part in range(tp_count):
            heads = dot_f32(w_heads[part], here, 0, 1).reshape(
                kv_here, 2, 2, 2, HEAD_DIM // 2, rows
            )
            sent.append(
                rotate_heads(heads, cosine, sine)
                .astype(jnp.bfloat16)
                .reshape(kv_here * 2, 2 * HEAD_DIM, rows)
            )
    own = every_device(jnp.concatenate(sent, 0))
    other = swap_cores(own[:, HEAD_DIM:, :])

    micro_here = ep_index // (ep_count // micro_count)
    starts = lax.dynamic_index_in_dim(piece_starts, micro_here, 0, keepdims=False)
    all_pos = jnp.arange(seq_len, dtype=jnp.int32)[None, :]
    inside = (all_pos >= starts[:, None]) & (all_pos < starts[:, None] + PIECE)
    piece_last = jnp.max(jnp.where(inside, starts[:, None] + (PIECE - 1), -1), 0, keepdims=True)
    limit = jnp.maximum(all_pos, piece_last).astype(jnp.int32)
    out_b, out_f, log_total = attend(core, own, other, limit)
    attended_t = every_device(out_b).reshape(micro_count, out_cols * tp_count, rows)

    attn_rows = jnp.concatenate(
        [dot_f32(attended_t[micro], w_out_t, 0, 1) for micro in range(micro_count)], 0
    )
    resid = x_rows + attn_rows
    scale_two = rms_scale(resid)
    normed_two = (resid * scale_two * gain_two).astype(jnp.bfloat16)
    plane_x = [
        jnp.concatenate(
            [normed_two[micro * rows : (micro + 1) * rows]]
            + [
                flip(normed_two[micro * rows : (micro + 1) * rows], step)
                for step in range(1, PLANE)
            ],
            0,
        )
        for micro in range(micro_count)
    ]
    logits = jnp.dot(normed_two, w_route_full, preferred_element_type=jnp.float32)
    route_rows = routes.reshape(all_rows, -1)
    expert_ids = jnp.arange(experts_all, dtype=jnp.int32)
    route_hot = (route_rows[:, :, None] == expert_ids[None, None, :]).astype(jnp.float32)
    picked = jnp.sum(route_hot * logits[:, None, :], -1)
    highest = jnp.max(picked, -1, keepdims=True)
    raised = jnp.exp(picked - highest)
    gates = raised / jnp.sum(raised, -1, keepdims=True)

    level, spot = ep_index // PLANE, ep_index % PLANE
    slot_ids = jnp.stack(
        [
            jnp.stack([(level ^ up) * PLANE + (spot ^ step) for up in range(columns)])
            for step in range(PLANE)
        ]
    )
    slot_hot = (route_rows[None, None, :, :] == slot_ids[:, :, None, None]).astype(jnp.float32)
    slot_gates = jnp.sum(slot_hot * gates[None, None], -1)
    plane_gates = jnp.stack(
        [slot_gates[0]] + [flip(slot_gates[step], step) for step in range(1, PLANE)], 1
    ).reshape(columns, PLANE, micro_count, rows)

    before = None
    mixes, grads_x, grads_gate = [], [], []
    for micro in range(micro_count):
        mix, grad_x, grad_gate, *before = experts(
            core,
            plane_x[micro],
            dy_plane[micro],
            plane_gates[:, :, micro].reshape(columns, PLANE * rows, 1),
            gate_cols,
            up_cols,
            down_cols,
            before,
        )

        def back_home(parts):
            parts = parts.reshape(PLANE, rows, width)
            total = parts[0].astype(jnp.float32)
            for step in range(1, PLANE):
                total = total + flip(parts[step], step).astype(jnp.float32)
            return total

        mixes.append(back_home(mix))
        grads_x.append(back_home(grad_x))
        grad_gate = grad_gate.reshape(columns, PLANE, rows)
        grads_gate.append(
            jnp.stack(
                [grad_gate[:, 0]]
                + [flip(grad_gate[:, step], step) for step in range(1, PLANE)]
            )
        )
    keep_w, send_w = before
    column_w = (keep_w.astype(jnp.float32) + swap_cores(send_w).astype(jnp.float32)).astype(
        jnp.bfloat16
    )
    grad_expert_w = column_w[0].astype(jnp.float32)
    for step in range(1, columns):
        grad_expert_w = grad_expert_w + flip(column_w[step], PLANE * step).astype(jnp.float32)

    mixed = (resid + jnp.concatenate(mixes, 0)).astype(jnp.bfloat16)
    grad_out = cotangent.reshape(all_rows, width).astype(jnp.float32)
    slot_grads = jnp.concatenate(grads_gate, 2)
    grad_gates = jnp.sum(slot_hot * slot_grads[:, :, :, None], (0, 1))
    grad_spread = gates * (grad_gates - jnp.sum(gates * grad_gates, -1, keepdims=True))
    grad_logits = jnp.sum(grad_spread[:, :, None] * route_hot, 1).astype(jnp.bfloat16)
    grad_normed_two = jnp.concatenate(grads_x, 0) + dot_f32(grad_logits, w_route_full, 1, 1)
    grad_route = dot_f32(normed_two, grad_logits, 0, 0)
    gained_two = grad_normed_two * gain_two
    grad_gain_two = jnp.sum(grad_normed_two * resid * scale_two, 0)
    grad_resid = (
        grad_out
        + scale_two * gained_two
        - resid * scale_two**3 * jnp.mean(resid * gained_two, -1, keepdims=True)
    )
    grad_branch = grad_resid.astype(jnp.bfloat16)
    grad_att = jnp.concatenate(
        [
            dot_f32(w_out_t, grad_branch[micro * rows : (micro + 1) * rows], 0, 1).astype(
                jnp.bfloat16
            )
            for micro in range(micro_count)
        ],
        0,
    ).reshape(devices, HEAD_DIM, rows)
    grad_heads = every_device(grad_att)
    grad_outw = sum(
        dot_f32(grad_branch[micro * rows : (micro + 1) * rows], attended_t[micro], 0, 1)
        for micro in range(micro_count)
    )

    grad_q, keep_kv, send_kv = attend_back(
        core, own, other, limit, out_f, log_total, grad_heads
    )
    grad_kv = (keep_kv + swap_cores(send_kv).astype(jnp.float32)).astype(jnp.bfloat16)
    grad_own = every_device(jnp.concatenate([grad_q, grad_kv], 1)).astype(jnp.float32)
    grad_proj_t = (
        rotate_heads(
            grad_own.reshape(
                micro_count, tp_count * kv_here, 2, 2, 2, HEAD_DIM // 2, rows
            ),
            cosine,
            -sine,
        )
        .astype(jnp.bfloat16)
        .reshape(micro_count, tp_count, half_cols, rows)
    )
    grad_normed = jnp.concatenate(
        [
            sum(dot_f32(grad_proj_t[micro, part], w_heads[part], 0, 1) for part in range(2))
            for micro in range(micro_count)
        ],
        0,
    )
    grad_proj = [
        sum(
            dot_f32(normed[micro * rows : (micro + 1) * rows], grad_proj_t[micro, part], 0, 1)
            for micro in range(micro_count)
        ).astype(jnp.bfloat16)
        for part in range(2)
    ]
    gained_one = grad_normed * gain_one
    grad_gain_one = jnp.sum(grad_normed * x_rows * scale_one, 0)
    grad_tokens = (
        grad_resid
        + scale_one * gained_one
        - x_rows * scale_one**3 * jnp.mean(x_rows * gained_one, -1, keepdims=True)
    )

    small_grads = jnp.concatenate([grad_route, grad_gain_one[:, None], grad_gain_two[:, None]], 1)
    small_grads = jnp.pad(small_grads, ((0, 0), (0, LANES - small_grads.shape[1]))).astype(
        jnp.bfloat16
    )
    grad_outw = grad_outw.astype(jnp.bfloat16)
    parts = [
        jnp.concatenate(
            [grad_proj[part], grad_outw[:, part * out_cols : (part + 1) * out_cols], small_grads],
            1,
        )
        for part in range(2)
    ]
    kept = jnp.where(tp_index == 0, parts[0], parts[1])
    given = jnp.where(tp_index == 0, parts[1], parts[0])
    core_sum = (kept.astype(jnp.float32) + swap_cores(given).astype(jnp.float32)).astype(
        jnp.bfloat16
    )
    shares = lax.all_to_all(
        core_sum.reshape(ep_count, shard, -1), "ep", split_axis=0, concat_axis=0, tiled=True
    )
    own_share = jnp.sum(shares.astype(jnp.float32), 0)
    head_grads = own_share[:, :half_cols].reshape(shard, kv_here, 2, 2, HEAD_DIM)
    small_share = lax.dynamic_slice_in_dim(
        own_share[:, half_cols + out_cols :], tp_index * (shard // 2), shard // 2, 0
    )
    return (
        mixed.reshape(micro_count, rows, width),
        grad_tokens.reshape(micro_count, rows, width),
        small_share[:, experts_all],
        head_grads[:, :, :, 0].reshape(shard, q_cols),
        head_grads[:, :, 0, 1].reshape(shard, kv_cols),
        head_grads[:, :, 1, 1].reshape(shard, kv_cols),
        own_share[:, half_cols : half_cols + out_cols].T,
        small_share[:, experts_all + 1],
        small_share[:, :experts_all],
        grad_expert_w[0][None],
        grad_expert_w[1][None],
        grad_expert_w[2].T[None],
    )


def on_device(*args):
    tokens, w_query, w_key, w_gate = args[0], args[2], args[3], args[8]
    paired = paired_layout(
        lax.axis_size("ep"),
        lax.axis_size("tp"),
        *tokens.shape,
        w_query.shape[1],
        w_key.shape[1],
        w_gate.shape[0],
    )
    return (on_device_paired if paired else on_device_general)(*args)


def solution(mesh):
    in_specs = (
        P(None, ("ep", "tp"), None),
        P("ep"),
        P("ep", "tp"),
        P("ep", "tp"),
        P("ep", "tp"),
        P("tp", "ep"),
        P("ep"),
        P("ep", None),
        P("ep", None, None),
        P("ep", None, None),
        P("ep", None, None),
        P(None, ("ep", "tp"), None),
        P(),
        P(None, ("ep", "tp"), None),
    )
    out_specs = (
        P(None, ("ep", "tp"), None),
        P(None, ("ep", "tp"), None),
        P(("ep", "tp")),
        P("ep", "tp"),
        P("ep", "tp"),
        P("ep", "tp"),
        P("tp", "ep"),
        P(("ep", "tp")),
        P(("ep", "tp"), None),
        P("ep", "tp", None),
        P("ep", "tp", None),
        P("ep", None, "tp"),
    )
    return jax.shard_map(
        on_device, mesh=mesh, in_specs=in_specs, out_specs=out_specs, check_vma=False
    )
```

```python
import functools
import math

import jax
import jax.numpy as jnp
from jax import lax
from jax.experimental import pallas as pl
from jax.experimental.pallas import tpu as pltpu
from jax.sharding import PartitionSpec as P

HEAD_DIM = 64
PIECE = 256
PLANE = 4
LANES = 128
MIB = 1 << 20


EPS = 1e-06
THETA = 10000.0
NEG = -1e30


def rms_scale(values):
    return lax.rsqrt(jnp.mean(values * values, -1, keepdims=True) + EPS)


def angle_tables(positions):
    halves = jnp.arange(HEAD_DIM // 2, dtype=jnp.float32)
    freqs = THETA ** (-2.0 * halves / HEAD_DIM)
    angles = positions.astype(jnp.float32)[:, None] * freqs[None, :]
    return (jnp.cos(angles)[:, None, :], jnp.sin(angles)[:, None, :])


def rotate(values, cosine, sine):
    half_dim = values.shape[-1] // 2
    first_half = values[..., :half_dim]
    second_half = values[..., half_dim:]
    return jnp.concatenate(
        [first_half * cosine - second_half * sine, second_half * cosine + first_half * sine], -1
    )


def piece_index(starts, positions):
    inside = (positions[:, None] >= starts[None, :]) & (
        positions[:, None] < starts[None, :] + PIECE
    )
    numbers = jnp.arange(1, starts.shape[0] + 1, dtype=jnp.int32)
    return jnp.sum(jnp.where(inside, numbers[None, :], 0), -1) - 1


def allowed_mask(query_pos, query_piece, key_pos, key_piece):
    return (key_pos[None, :] <= query_pos[:, None]) | (
        key_piece[None, :] == query_piece[:, None]
    ) & (query_piece[:, None] >= 0)


def to_groups(rows, kv_here, group_size):
    row_total = rows.shape[0]
    return (
        rows.reshape(row_total, kv_here, group_size, HEAD_DIM)
        .transpose(1, 2, 0, 3)
        .reshape(kv_here, group_size * row_total, HEAD_DIM)
    )


def from_groups(grouped, row_total):
    kv_here = grouped.shape[0]
    return (
        grouped.reshape(kv_here, -1, row_total, HEAD_DIM)
        .transpose(2, 0, 1, 3)
        .reshape(row_total, -1)
    )


def tp_major(values, ep_count, tp_count):
    leading = values.shape[0]
    shaped = values.reshape(
        (ep_count, tp_count, leading // (ep_count * tp_count)) + values.shape[1:]
    )
    return jnp.swapaxes(shaped, 0, 1).reshape(values.shape)


def add_all(left_parts, right_parts):
    return tuple((left_part + right_part for left_part, right_part in zip(left_parts, right_parts)))


def reduce_grads(parts, ep_count, tp_count):
    (
        grad_gate_w,
        grad_up_w,
        grad_down_w,
        grad_gain_one,
        grad_gain_two,
        grad_route,
        grad_proj,
        grad_outw,
    ) = parts
    tp_sums = (
        lax.psum_scatter(
            grad_gate_w.astype(jnp.bfloat16), "tp", scatter_dimension=1, tiled=True
        ).astype(jnp.float32),
        lax.psum_scatter(
            grad_up_w.astype(jnp.bfloat16), "tp", scatter_dimension=1, tiled=True
        ).astype(jnp.float32),
        lax.psum_scatter(
            grad_down_w.astype(jnp.bfloat16), "tp", scatter_dimension=2, tiled=True
        ).astype(jnp.float32),
        lax.psum_scatter(
            tp_major(grad_gain_one, ep_count, tp_count).astype(jnp.bfloat16),
            "tp",
            scatter_dimension=0,
            tiled=True,
        ).astype(jnp.float32),
        lax.psum_scatter(
            tp_major(grad_gain_two, ep_count, tp_count).astype(jnp.bfloat16),
            "tp",
            scatter_dimension=0,
            tiled=True,
        ).astype(jnp.float32),
        lax.psum_scatter(
            tp_major(grad_route, ep_count, tp_count).astype(jnp.bfloat16),
            "tp",
            scatter_dimension=0,
            tiled=True,
        ).astype(jnp.float32),
    )
    ep_sums = (
        lax.psum_scatter(
            grad_proj.astype(jnp.bfloat16), "ep", scatter_dimension=0, tiled=True
        ).astype(jnp.float32),
        lax.psum_scatter(
            grad_outw.astype(jnp.bfloat16), "ep", scatter_dimension=1, tiled=True
        ).astype(jnp.float32),
        lax.psum_scatter(
            tp_sums[3].astype(jnp.bfloat16), "ep", scatter_dimension=0, tiled=True
        ).astype(jnp.float32),
        lax.psum_scatter(
            tp_sums[4].astype(jnp.bfloat16), "ep", scatter_dimension=0, tiled=True
        ).astype(jnp.float32),
        lax.psum_scatter(
            tp_sums[5].astype(jnp.bfloat16), "ep", scatter_dimension=0, tiled=True
        ).astype(jnp.float32),
    )
    return (
        tp_sums[0],
        tp_sums[1],
        tp_sums[2],
        ep_sums[2],
        ep_sums[3],
        ep_sums[4],
        ep_sums[0],
        ep_sums[1],
    )


def on_device_general(
    tokens,
    gain_attn,
    w_query,
    w_key,
    w_value,
    w_output,
    gain_moe,
    w_router,
    w_gate,
    w_up,
    w_down,
    routes,
    piece_starts,
    cotangent,
):
    ep_count = lax.axis_size("ep")
    tp_count = lax.axis_size("tp")
    micro_count, slice_rows, width = tokens.shape
    span_rows = slice_rows * tp_count
    seq_len = span_rows * ep_count
    q_cols = w_query.shape[1]
    kv_cols = w_key.shape[1]
    kv_here = kv_cols // HEAD_DIM
    group_size = q_cols // kv_cols
    query_rows = group_size * span_rows
    experts_here = w_gate.shape[0]
    experts_all = experts_here * ep_count
    top_count = routes.shape[2]
    capacity = max(2, slice_rows * top_count * 3 // (2 * experts_all))
    expert_rows = ep_count * capacity
    score_scale = HEAD_DIM ** (-0.5)
    key_block = math.gcd(seq_len, 512)
    block_count = seq_len // key_block
    local_pos = lax.axis_index("ep") * span_rows + jnp.arange(span_rows, dtype=jnp.int32)
    all_pos = jnp.arange(seq_len, dtype=jnp.int32)
    row_pos = jnp.tile(local_pos, group_size)
    cosine, sine = angle_tables(local_pos)
    slot_ids = jnp.arange(experts_all * capacity, dtype=jnp.int32)
    expert_ids = jnp.arange(experts_all, dtype=jnp.int32)
    gathered = (
        lax.all_gather(gain_attn, "ep", axis=0, tiled=True),
        lax.all_gather(w_query, "ep", axis=0, tiled=True),
        lax.all_gather(w_key, "ep", axis=0, tiled=True),
        lax.all_gather(w_value, "ep", axis=0, tiled=True),
        lax.all_gather(w_output, "ep", axis=1, tiled=True),
        lax.all_gather(gain_moe, "ep", axis=0, tiled=True),
        lax.all_gather(w_router, "ep", axis=0, tiled=True),
    )
    gain_one = gathered[0].astype(jnp.float32)
    w_proj = jnp.concatenate([gathered[1], gathered[2], gathered[3]], 1)
    w_out_full = gathered[4]
    gain_two = gathered[5].astype(jnp.float32)
    w_route_full = gathered[6]
    totals = None
    mixed_rows = []
    grad_rows = []
    for micro_index in range(micro_count):
        starts = piece_starts[micro_index]
        key_pieces = piece_index(starts, all_pos)
        row_piece = jnp.tile(piece_index(starts, local_pos), group_size)
        x_rows = tokens[micro_index].astype(jnp.float32)
        scale_one = rms_scale(x_rows)
        normed = (x_rows * scale_one * gain_one).astype(jnp.bfloat16)
        normed_all = lax.all_gather(normed, "tp", axis=0, tiled=True)
        projected = jnp.dot(normed_all, w_proj, preferred_element_type=jnp.float32)
        queries = rotate(
            projected[:, :q_cols].reshape(span_rows, -1, HEAD_DIM), cosine, sine
        ).astype(jnp.bfloat16)
        q_grouped = to_groups(queries.reshape(span_rows, q_cols), kv_here, group_size)
        keys_own = (
            rotate(
                projected[:, q_cols : q_cols + kv_cols].reshape(span_rows, kv_here, HEAD_DIM),
                cosine,
                sine,
            )
            .astype(jnp.bfloat16)
            .reshape(span_rows, kv_cols)
        )
        values_own = projected[:, q_cols + kv_cols :].astype(jnp.bfloat16)
        keys_all, values_all = (
            lax.all_gather(keys_own, "ep", axis=0, tiled=True),
            lax.all_gather(values_own, "ep", axis=0, tiled=True),
        )

        def block_scores(first_row, block_size):
            key_blk = lax.dynamic_slice_in_dim(keys_all, first_row, block_size, 0).reshape(
                block_size, kv_here, HEAD_DIM
            )
            value_blk = lax.dynamic_slice_in_dim(values_all, first_row, block_size, 0).reshape(
                block_size, kv_here, HEAD_DIM
            )
            key_pos = first_row + jnp.arange(block_size, dtype=jnp.int32)
            piece_blk = lax.dynamic_slice_in_dim(key_pieces, first_row, block_size, 0)
            allowed = allowed_mask(row_pos, row_piece, key_pos, piece_blk)[None]
            scores = (
                jnp.einsum("hrd,khd->hrk", q_grouped, key_blk, preferred_element_type=jnp.float32)
                * score_scale
            )
            return (scores, allowed, key_blk, value_blk)

        def forward_step(block_index, running):
            run_max, run_sum, run_acc = running
            scores, allowed, key_blk, value_blk = block_scores(block_index * key_block, key_block)
            scores = jnp.where(allowed, scores, NEG)
            new_max = jnp.maximum(run_max, jnp.max(scores, -1))
            weights = jnp.where(allowed, jnp.exp(scores - new_max[..., None]), 0.0)
            factor = jnp.exp(run_max - new_max)
            run_sum = run_sum * factor + jnp.sum(weights, -1)
            run_acc = run_acc * factor[..., None] + jnp.einsum(
                "hrk,khd->hrd",
                weights.astype(jnp.bfloat16),
                value_blk,
                preferred_element_type=jnp.float32,
            )
            return (new_max, run_sum, run_acc)

        start_state = (
            jnp.full((kv_here, query_rows), NEG, jnp.float32),
            jnp.zeros((kv_here, query_rows), jnp.float32),
            jnp.zeros((kv_here, query_rows, HEAD_DIM), jnp.float32),
        )
        run_max, run_sum, run_acc = lax.fori_loop(0, block_count, forward_step, start_state)
        log_total = run_max + jnp.log(run_sum)
        attended_f = run_acc / run_sum[..., None]
        attended = from_groups(attended_f.astype(jnp.bfloat16), span_rows)
        partial_attn = jnp.dot(attended, w_out_full, preferred_element_type=jnp.float32)
        attn_rows = lax.psum_scatter(
            partial_attn.astype(jnp.bfloat16), "tp", scatter_dimension=0, tiled=True
        ).astype(jnp.float32)
        resid = x_rows + attn_rows
        scale_two = rms_scale(resid)
        normed_two = (resid * scale_two * gain_two).astype(jnp.bfloat16)
        logits = jnp.dot(normed_two, w_route_full, preferred_element_type=jnp.float32)
        route_rows = routes[micro_index]
        route_hot = (route_rows[:, :, None] == expert_ids[None, None, :]).astype(jnp.float32)
        picked = jnp.sum(route_hot * logits[:, None, :], -1)
        highest = jnp.max(picked, -1, keepdims=True)
        raised = jnp.exp(picked - highest)
        gates = raised / jnp.sum(raised, -1, keepdims=True)
        flat_hot = route_hot.reshape(-1, experts_all)
        earlier = jnp.cumsum(flat_hot, 0) - flat_hot
        slot_of = jnp.sum(earlier * flat_hot, -1).astype(jnp.int32)
        target = route_rows.reshape(-1) * capacity + slot_of
        place_pairs = slot_ids[:, None] == target[None, :]
        place_pairs_b = place_pairs.astype(jnp.bfloat16)
        place_tokens = jnp.any(place_pairs.reshape(-1, slice_rows, top_count), -1).astype(
            jnp.bfloat16
        )
        send_rows = (
            jnp.dot(place_tokens, normed_two, preferred_element_type=jnp.float32)
            .astype(jnp.bfloat16)
            .reshape(ep_count, experts_here, capacity, width)
        )
        received = lax.all_to_all(send_rows, "ep", split_axis=0, concat_axis=0, tiled=True)
        expert_in = jnp.swapaxes(received, 0, 1).reshape(experts_here, expert_rows, width)
        gate_pre = jnp.einsum("erd,edf->erf", expert_in, w_gate, preferred_element_type=jnp.float32)
        up_pre = jnp.einsum("erd,edf->erf", expert_in, w_up, preferred_element_type=jnp.float32)
        sigmoid_val = jax.nn.sigmoid(gate_pre)
        silu_val = gate_pre * sigmoid_val
        hidden = (silu_val * up_pre).astype(jnp.bfloat16)
        expert_out = jnp.einsum(
            "erf,efd->erd", hidden, w_down, preferred_element_type=jnp.float32
        ).astype(jnp.bfloat16)
        returned = lax.all_to_all(
            jnp.swapaxes(expert_out.reshape(experts_here, ep_count, capacity, width), 0, 1),
            "ep",
            split_axis=0,
            concat_axis=0,
            tiled=True,
        )
        slot_rows = returned.reshape(-1, width)
        picked_rows = jnp.einsum(
            "sn,sd->nd", place_pairs_b, slot_rows, preferred_element_type=jnp.float32
        ).reshape(slice_rows, top_count, width)
        mixture = jnp.einsum("tk,tkd->td", gates, picked_rows)
        mixed_rows.append((resid + mixture).astype(jnp.bfloat16))
        grad_out = cotangent[micro_index].astype(jnp.float32)
        grad_gates = jnp.einsum("tkd,td->tk", picked_rows, grad_out)
        weighted = (
            (gates[:, :, None] * grad_out[:, None, :]).astype(jnp.bfloat16).reshape(-1, width)
        )
        grad_slots = (
            jnp.dot(place_pairs_b, weighted, preferred_element_type=jnp.float32)
            .astype(jnp.bfloat16)
            .reshape(ep_count, experts_here, capacity, width)
        )
        grad_recv = lax.all_to_all(grad_slots, "ep", split_axis=0, concat_axis=0, tiled=True)
        grad_expert = jnp.swapaxes(grad_recv, 0, 1).reshape(experts_here, expert_rows, width)
        grad_hidden = jnp.einsum(
            "erd,efd->erf", grad_expert, w_down, preferred_element_type=jnp.float32
        )
        grad_down_w = jnp.einsum(
            "erf,erd->efd", hidden, grad_expert, preferred_element_type=jnp.float32
        )
        silu_slope = sigmoid_val * (1.0 + gate_pre * (1.0 - sigmoid_val))
        grad_gate_pre = (grad_hidden * up_pre * silu_slope).astype(jnp.bfloat16)
        grad_up_pre = (grad_hidden * silu_val).astype(jnp.bfloat16)
        grad_gate_w = jnp.einsum(
            "erd,erf->edf", expert_in, grad_gate_pre, preferred_element_type=jnp.float32
        )
        grad_up_w = jnp.einsum(
            "erd,erf->edf", expert_in, grad_up_pre, preferred_element_type=jnp.float32
        )
        grad_copy = (
            jnp.einsum("erf,edf->erd", grad_gate_pre, w_gate, preferred_element_type=jnp.float32)
            + jnp.einsum("erf,edf->erd", grad_up_pre, w_up, preferred_element_type=jnp.float32)
        ).astype(jnp.bfloat16)
        grad_back = lax.all_to_all(
            jnp.swapaxes(grad_copy.reshape(experts_here, ep_count, capacity, width), 0, 1),
            "ep",
            split_axis=0,
            concat_axis=0,
            tiled=True,
        ).reshape(-1, width)
        grad_spread = gates * (grad_gates - jnp.sum(gates * grad_gates, -1, keepdims=True))
        grad_logits = jnp.einsum("tk,tke->te", grad_spread, route_hot).astype(jnp.bfloat16)
        grad_normed_two = jnp.einsum(
            "st,sd->td", place_tokens, grad_back, preferred_element_type=jnp.float32
        ) + jnp.einsum("te,de->td", grad_logits, w_route_full, preferred_element_type=jnp.float32)
        grad_route = jnp.einsum(
            "td,te->de", normed_two, grad_logits, preferred_element_type=jnp.float32
        )
        gained_two = grad_normed_two * gain_two
        grad_gain_two = jnp.sum(grad_normed_two * resid * scale_two, 0)
        grad_resid = (
            grad_out
            + scale_two * gained_two
            - resid * scale_two**3 * jnp.mean(resid * gained_two, -1, keepdims=True)
        )
        grad_attn = lax.all_gather(grad_resid.astype(jnp.bfloat16), "tp", axis=0, tiled=True)
        grad_outw = jnp.einsum("cq,cd->qd", attended, grad_attn, preferred_element_type=jnp.float32)
        grad_att_rows = jnp.einsum(
            "cd,qd->cq", grad_attn, w_out_full, preferred_element_type=jnp.float32
        ).astype(jnp.bfloat16)
        grad_grouped = to_groups(grad_att_rows, kv_here, group_size)
        delta = jnp.sum(grad_grouped.astype(jnp.float32) * attended_f, -1)

        def block_grads(first_row, block_size):
            scores, allowed, key_blk, value_blk = block_scores(first_row, block_size)
            probs = jnp.where(allowed, jnp.exp(scores - log_total[..., None]), 0.0)
            grad_probs = jnp.einsum(
                "hrd,khd->hrk", grad_grouped, value_blk, preferred_element_type=jnp.float32
            )
            grad_scores = (probs * (grad_probs - delta[..., None])).astype(jnp.bfloat16)
            return (probs, grad_scores, key_blk)

        def key_side(first_row, block_size):
            probs, grad_scores, key_blk = block_grads(first_row, block_size)
            grad_keys = (
                jnp.einsum(
                    "hrk,hrd->khd", grad_scores, q_grouped, preferred_element_type=jnp.float32
                ).reshape(block_size, kv_cols)
                * score_scale
            )
            grad_values = jnp.einsum(
                "hrk,hrd->khd",
                probs.astype(jnp.bfloat16),
                grad_grouped,
                preferred_element_type=jnp.float32,
            ).reshape(block_size, kv_cols)
            return (jnp.concatenate([grad_keys, grad_values], 1), grad_scores, key_blk)

        query_zero = jnp.zeros((kv_here, query_rows, HEAD_DIM), jnp.float32)

        def backward_step(block_index, running):
            grad_query, grad_kv = running
            first_row = block_index * key_block
            kv_terms, grad_scores, key_blk = key_side(first_row, key_block)
            grad_query = grad_query + jnp.einsum(
                "hrk,khd->hrd", grad_scores, key_blk, preferred_element_type=jnp.float32
            )
            grad_kv = lax.dynamic_update_slice_in_dim(grad_kv, kv_terms, first_row, 0)
            return (grad_query, grad_kv)

        grad_query, grad_kv = lax.fori_loop(
            0,
            block_count,
            backward_step,
            (query_zero, jnp.zeros((seq_len, 2 * kv_cols), jnp.float32)),
        )
        grad_kv_own = lax.psum_scatter(
            grad_kv.astype(jnp.bfloat16), "ep", scatter_dimension=0, tiled=True
        ).astype(jnp.float32)
        grad_query_rows = from_groups(grad_query * score_scale, span_rows).reshape(
            span_rows, -1, HEAD_DIM
        )
        grad_query_raw = (
            rotate(grad_query_rows, cosine, -sine).astype(jnp.bfloat16).reshape(span_rows, q_cols)
        )
        grad_key_raw = (
            rotate(grad_kv_own[:, :kv_cols].reshape(span_rows, kv_here, HEAD_DIM), cosine, -sine)
            .astype(jnp.bfloat16)
            .reshape(span_rows, kv_cols)
        )
        grad_value_raw = grad_kv_own[:, kv_cols:].astype(jnp.bfloat16)
        grad_proj_rows = jnp.concatenate([grad_query_raw, grad_key_raw, grad_value_raw], 1)
        grad_proj = jnp.einsum(
            "cd,cp->dp", normed_all, grad_proj_rows, preferred_element_type=jnp.float32
        )
        grad_normed_part = jnp.einsum(
            "cp,dp->cd", grad_proj_rows, w_proj, preferred_element_type=jnp.float32
        )
        grad_normed = lax.psum_scatter(
            grad_normed_part.astype(jnp.bfloat16), "tp", scatter_dimension=0, tiled=True
        ).astype(jnp.float32)
        gained_one = grad_normed * gain_one
        grad_gain_one = jnp.sum(grad_normed * x_rows * scale_one, 0)
        grad_rows.append(
            grad_resid
            + scale_one * gained_one
            - x_rows * scale_one**3 * jnp.mean(x_rows * gained_one, -1, keepdims=True)
        )
        parts = (
            grad_gate_w,
            grad_up_w,
            grad_down_w,
            grad_gain_one,
            grad_gain_two,
            grad_route,
            grad_proj,
            grad_outw,
        )
        reduced = reduce_grads(parts, ep_count, tp_count)
        totals = reduced if totals is None else add_all(totals, reduced)
    grad_qkv = totals[6]
    return (
        jnp.stack(mixed_rows),
        jnp.stack(grad_rows),
        totals[3],
        grad_qkv[:, :q_cols],
        grad_qkv[:, q_cols : q_cols + kv_cols],
        grad_qkv[:, q_cols + kv_cols :],
        totals[7],
        totals[4],
        totals[5],
        totals[0],
        totals[1],
        totals[2],
    )


def dot_f32(left, right, left_dim, right_dim):
    return lax.dot_general(
        left, right, (((left_dim,), (right_dim,)), ((), ())), preferred_element_type=jnp.float32
    )


def at_rows(first_row, count):
    return pl.ds(pl.multiple_of(first_row, count), count)


def whole_vmem():
    return pl.BlockSpec(memory_space=pltpu.VMEM)


def attend_kernel(
    tp_ref, own_ref, other_ref, limit_ref, out_ref, out_f_ref, log_ref,
    keys, queries, values, highest, total,
    *, query_block, key_block, diagonal_block, chains
):
    core = tp_ref[0]
    blocks, _, rows = own_ref.shape
    seq_len = blocks * rows
    chain = query_block // chains

    def fill(block, _):
        cols = at_rows(block * rows, rows)
        first, second = own_ref[block, HEAD_DIM:, :], other_ref[block]
        key_rows = jnp.where(core == 0, first, second).astype(jnp.float32)
        queries[:, cols] = own_ref[block, :HEAD_DIM, :]
        values[:HEAD_DIM, cols] = jnp.where(core == 0, second, first)
        values[HEAD_DIM:, cols] = jnp.ones((16, rows), jnp.bfloat16)
        keys[cols, :] = (key_rows * HEAD_DIM ** (-0.5)).T.astype(jnp.bfloat16)
        return 0

    lax.fori_loop(0, blocks, fill, 0)

    def update(scores, value_cols, here):
        before = highest[:, here]
        after = jnp.maximum(before, jnp.max(scores, 0, keepdims=True))
        weights = jnp.exp(scores - after).astype(jnp.bfloat16)
        highest[:, here] = after
        total[:, here] = total[:, here] * jnp.exp(before - after) + dot_f32(
            value_cols, weights, 1, 0
        )

    def near_diagonal(key_rows, key_first, query_cols, here):
        scores = dot_f32(keys[key_rows, :], queries[:, query_cols], 1, 0)
        key_pos = key_first + lax.broadcasted_iota(jnp.int32, scores.shape, 0)
        allowed = key_pos <= limit_ref[:, query_cols]
        update(jnp.where(allowed, scores, NEG), values[:, key_rows], here)

    def query_step(index, _):
        first = index * query_block
        highest[...] = jnp.full_like(highest, NEG)
        total[...] = jnp.zeros_like(total)

        def full_step(step, _):
            key_rows = at_rows(step * key_block, key_block)
            scores = [
                dot_f32(keys[key_rows, :], queries[:, at_rows(first + part * chain, chain)], 1, 0)
                for part in range(chains)
            ]
            for part in range(chains):
                update(scores[part], values[:, key_rows], slice(part * chain, (part + 1) * chain))
            return 0

        lax.fori_loop(0, first // key_block, full_step, 0)
        for low in range(0, query_block, diagonal_block):
            here = pl.multiple_of(first + low, diagonal_block)
            if low:
                near_diagonal(
                    pl.ds(here, rows),
                    here,
                    pl.ds(pl.multiple_of(here - rows, rows), rows),
                    slice(low - rows, low),
                )
            near_diagonal(
                pl.ds(here, diagonal_block),
                here,
                pl.ds(here, query_block - low),
                slice(low, query_block),
            )
        near_diagonal(
            at_rows(jnp.minimum(first + query_block, seq_len - rows), rows),
            first + query_block,
            at_rows(first + query_block - rows, rows),
            slice(query_block - rows, query_block),
        )
        for piece in range(query_block // rows):
            here = slice(piece * rows, (piece + 1) * rows)
            row_sum = total[HEAD_DIM : HEAD_DIM + 1, here]
            result = total[:HEAD_DIM, here] / row_sum
            block = index * (query_block // rows) + piece
            out_ref[block] = result.astype(jnp.bfloat16)
            out_f_ref[block] = result
            log_ref[:, at_rows(first + piece * rows, rows)] = highest[:, here] + jnp.log(row_sum)
        return 0

    lax.fori_loop(0, seq_len // query_block, query_step, 0)


def attend(core, own, other, limit):
    blocks, _, rows = own.shape
    seq_len = blocks * rows
    query_block = math.gcd(seq_len, 2048)
    key_block = math.gcd(query_block, 1024)
    block_shape = (blocks, HEAD_DIM, rows)
    return pl.pallas_call(
        functools.partial(
            attend_kernel,
            query_block=query_block,
            key_block=key_block,
            diagonal_block=math.gcd(query_block, 512),
            chains=query_block // math.gcd(query_block, 512),
        ),
        out_shape=(
            jax.ShapeDtypeStruct(block_shape, jnp.bfloat16),
            jax.ShapeDtypeStruct(block_shape, jnp.float32),
            jax.ShapeDtypeStruct((1, seq_len), jnp.float32),
        ),
        in_specs=[pl.BlockSpec(memory_space=pltpu.SMEM)] + [whole_vmem()] * 3,
        out_specs=(whole_vmem(),) * 3,
        scratch_shapes=[
            pltpu.VMEM((seq_len, HEAD_DIM), jnp.bfloat16),
            pltpu.VMEM((HEAD_DIM, seq_len), jnp.bfloat16),
            pltpu.VMEM((HEAD_DIM + 16, seq_len), jnp.bfloat16),
            pltpu.VMEM((1, query_block), jnp.float32),
            pltpu.VMEM((HEAD_DIM + 16, query_block), jnp.float32),
        ],
        cost_estimate=pl.CostEstimate(
            flops=seq_len * seq_len * 512, bytes_accessed=8 * MIB, transcendentals=0
        ),
        compiler_params=pltpu.CompilerParams(vmem_limit_bytes=56 * MIB),
        name="attend",
    )(core, own, other, limit)


def three_parts(values):
    high = values.astype(jnp.bfloat16).astype(jnp.float32)
    middle = (values - high).astype(jnp.bfloat16).astype(jnp.float32)
    low = values - high - middle
    row = lax.broadcasted_iota(jnp.int32, (16, values.shape[1]), 0)
    parts = jnp.where(
        row == 0, high, jnp.where(row == 1, middle, jnp.where(row == 2, low, 0.0))
    )
    return parts.astype(jnp.bfloat16)


def attend_back_kernel(
    tp_ref, own_ref, other_ref, limit_ref, out_f_ref, log_ref, grad_ref,
    grad_q_ref, keep_ref, send_ref,
    keys, keys_t, queries_t, queries, values, grads_t, grads, grad_k, grad_v, grad_q,
    *, query_block, key_block, diagonal_block
):
    core = tp_ref[0]
    blocks, _, rows = own_ref.shape
    seq_len = blocks * rows

    def fill(block, _):
        cols = at_rows(block * rows, rows)
        first, second = own_ref[block, HEAD_DIM:, :], other_ref[block]
        key_rows = jnp.where(core == 0, first, second).astype(jnp.float32)
        key_rows = key_rows * HEAD_DIM ** (-0.5)
        value_rows = jnp.where(core == 0, second, first).astype(jnp.float32)
        query, grad = own_ref[block, :HEAD_DIM, :], grad_ref[block]
        grad_f = grad.astype(jnp.float32)
        delta = jnp.sum(grad_f * out_f_ref[block], 0, keepdims=True)
        ones = jnp.ones((16, rows), jnp.float32)
        queries_t[:HEAD_DIM, cols] = query
        queries_t[HEAD_DIM:, cols] = three_parts(-log_ref[:, cols])
        queries[cols, :] = query.astype(jnp.float32).T.astype(jnp.bfloat16)
        keys_t[:, cols] = key_rows.astype(jnp.bfloat16)
        keys[cols, :] = jnp.concatenate([key_rows, ones], 0).T.astype(jnp.bfloat16)
        values[cols, :] = jnp.concatenate([value_rows, ones], 0).T.astype(jnp.bfloat16)
        grads_t[:HEAD_DIM, cols] = grad
        grads_t[HEAD_DIM:, cols] = three_parts(-delta)
        grads[cols, :] = grad_f.T.astype(jnp.bfloat16)
        grad_k[cols, :] = jnp.zeros((rows, HEAD_DIM), jnp.float32)
        grad_v[cols, :] = jnp.zeros((rows, HEAD_DIM), jnp.float32)
        return 0

    lax.fori_loop(0, blocks, fill, 0)

    def tile(key_rows, key_first, query_cols, here):
        probs = jnp.exp(dot_f32(keys[key_rows, :], queries_t[:, query_cols], 1, 0))
        if key_first is not None:
            key_pos = key_first + lax.broadcasted_iota(jnp.int32, probs.shape, 0)
            probs = jnp.where(key_pos <= limit_ref[:, query_cols], probs, 0.0)
        grad_probs = dot_f32(values[key_rows, :], grads_t[:, query_cols], 1, 0)
        grad_scores = (probs * grad_probs).astype(jnp.bfloat16)
        grad_v[key_rows, :] += dot_f32(probs.astype(jnp.bfloat16), grads[query_cols, :], 1, 0)
        grad_k[key_rows, :] += dot_f32(grad_scores, queries[query_cols, :], 1, 0)
        grad_q[:, here] += dot_f32(keys_t[:, key_rows], grad_scores, 1, 0)

    def query_step(index, _):
        first = index * query_block
        whole = slice(0, query_block)
        grad_q[...] = jnp.zeros_like(grad_q)

        def full_step(step, _):
            tile(at_rows(step * key_block, key_block), None, at_rows(first, query_block), whole)
            return 0

        lax.fori_loop(0, first // key_block, full_step, 0)
        for low in range(0, query_block, diagonal_block):
            here = pl.multiple_of(first + low, diagonal_block)
            if low:
                tile(
                    pl.ds(here, rows),
                    here,
                    pl.ds(pl.multiple_of(here - rows, rows), rows),
                    slice(low - rows, low),
                )
            tile(
                pl.ds(here, diagonal_block),
                here,
                pl.ds(here, query_block - low),
                slice(low, query_block),
            )
        tile(
            at_rows(jnp.minimum(first + query_block, seq_len - rows), rows),
            first + query_block,
            at_rows(first + query_block - rows, rows),
            slice(query_block - rows, query_block),
        )
        for piece in range(query_block // rows):
            here = slice(piece * rows, (piece + 1) * rows)
            grad_q_ref[index * (query_block // rows) + piece] = grad_q[:, here].astype(
                jnp.bfloat16
            )
        return 0

    lax.fori_loop(0, seq_len // query_block, query_step, 0)

    def finish(block, _):
        cols = at_rows(block * rows, rows)
        key_part = (grad_k[cols, :] * HEAD_DIM ** (-0.5)).T
        value_part = grad_v[cols, :].T
        keep_ref[block] = jnp.where(core == 0, key_part, value_part)
        send_ref[block] = jnp.where(core == 0, value_part, key_part).astype(jnp.bfloat16)
        return 0

    lax.fori_loop(0, blocks, finish, 0)


def attend_back(core, own, other, limit, out_f, log_total, grad):
    blocks, _, rows = own.shape
    seq_len = blocks * rows
    query_block = math.gcd(seq_len, 1024)
    key_block = math.gcd(query_block, 1024)
    block_shape = (blocks, HEAD_DIM, rows)
    wide = HEAD_DIM + 16
    return pl.pallas_call(
        functools.partial(
            attend_back_kernel,
            query_block=query_block,
            key_block=key_block,
            diagonal_block=math.gcd(query_block, 512),
        ),
        out_shape=(
            jax.ShapeDtypeStruct(block_shape, jnp.bfloat16),
            jax.ShapeDtypeStruct(block_shape, jnp.float32),
            jax.ShapeDtypeStruct(block_shape, jnp.bfloat16),
        ),
        in_specs=[pl.BlockSpec(memory_space=pltpu.SMEM)] + [whole_vmem()] * 6,
        out_specs=(whole_vmem(),) * 3,
        scratch_shapes=[
            pltpu.VMEM((seq_len, wide), jnp.bfloat16),
            pltpu.VMEM((HEAD_DIM, seq_len), jnp.bfloat16),
            pltpu.VMEM((wide, seq_len), jnp.bfloat16),
            pltpu.VMEM((seq_len, HEAD_DIM), jnp.bfloat16),
            pltpu.VMEM((seq_len, wide), jnp.bfloat16),
            pltpu.VMEM((wide, seq_len), jnp.bfloat16),
            pltpu.VMEM((seq_len, HEAD_DIM), jnp.bfloat16),
            pltpu.VMEM((seq_len, HEAD_DIM), jnp.float32),
            pltpu.VMEM((seq_len, HEAD_DIM), jnp.float32),
            pltpu.VMEM((HEAD_DIM, query_block), jnp.float32),
        ],
        cost_estimate=pl.CostEstimate(
            flops=seq_len * seq_len * 1024, bytes_accessed=12 * MIB, transcendentals=0
        ),
        compiler_params=pltpu.CompilerParams(vmem_limit_bytes=60 * MIB),
        name="attend_back",
    )(core, own, other, limit, out_f, log_total, grad)


def project_kernel(*refs, count):
    place_ref, x_ref, cosine_ref, sine_ref = refs[:4]
    mine_refs, other_refs = refs[4 : 4 + count], refs[4 + count : 4 + 2 * count]
    normed_ref, sent_ref, heads_ref, small_ref = refs[4 + 2 * count :]
    core, level, spot = place_ref[0], place_ref[1], place_ref[2]
    micro_count, rows, width = x_ref.shape
    columns, shard, _ = mine_refs[0].shape
    half_cols = heads_ref.shape[2]
    half_dim = HEAD_DIM // 2
    units = half_cols // (2 * HEAD_DIM)
    for step in range(count):
        for up in range(columns):
            here = at_rows(((level ^ up) * count + (spot ^ step)) * shard, shard)
            heads_ref[core, here, :] = mine_refs[step][up, :, :half_cols]
            heads_ref[1 - core, here, :] = other_refs[step][up, :, :half_cols]
            small_ref[here, :] = mine_refs[step][up, :, half_cols:]
    cosine, sine = cosine_ref[...], sine_ref[...]
    gain_row = small_ref.shape[1] // 2
    gain = small_ref[...].astype(jnp.float32).T[gain_row : gain_row + 1]

    def rotated(heads):
        first, second = heads[:half_dim], heads[half_dim:]
        return jnp.concatenate(
            [first * cosine - second * sine, second * cosine + first * sine], 0
        ).astype(jnp.bfloat16)

    for micro in range(micro_count):
        x = x_ref[micro].astype(jnp.float32)
        scale = lax.rsqrt(jnp.mean(x * x, -1, keepdims=True) + EPS)
        normed = (x * scale * gain).astype(jnp.bfloat16)
        normed_ref[micro * rows : (micro + 1) * rows, :] = normed
        for part in range(2):
            heads = dot_f32(normed, heads_ref[part], 1, 0).T
            for unit in range(units):
                first = unit * 2 * HEAD_DIM
                block = (micro * 2 + part) * units + unit
                second = heads[first + HEAD_DIM : first + 2 * HEAD_DIM]
                sent_ref[block, :HEAD_DIM, :] = rotated(heads[first : first + HEAD_DIM])
                sent_ref[block, HEAD_DIM:, :] = (
                    rotated(second) if unit % 2 == 0 else second.astype(jnp.bfloat16)
                )


def project(place, x, cosine, sine, mine, other, devices):
    micro_count, rows, width = x.shape
    half_cols = mine[0].shape[2] - LANES
    return pl.pallas_call(
        functools.partial(project_kernel, count=len(mine)),
        out_shape=(
            jax.ShapeDtypeStruct((micro_count * rows, width), jnp.bfloat16),
            jax.ShapeDtypeStruct((devices, 2 * HEAD_DIM, rows), jnp.bfloat16),
            jax.ShapeDtypeStruct((2, width, half_cols), jnp.bfloat16),
            jax.ShapeDtypeStruct((width, LANES), jnp.bfloat16),
        ),
        in_specs=[pl.BlockSpec(memory_space=pltpu.SMEM)]
        + [whole_vmem()] * (3 + len(mine) + len(other)),
        out_specs=(whole_vmem(),) * 4,
        compiler_params=pltpu.CompilerParams(vmem_limit_bytes=48 * MIB),
        name="project",
    )(place, x, cosine, sine, *mine, *other)


def project_back_kernel(
    tp_ref, grad_ref, heads_ref, normed_ref, x_ref, grad_resid_ref, gain_ref, cosine_ref,
    sine_ref, grad_x_ref, kept_ref, given_ref, grad_rows
):
    core = tp_ref[0]
    micro_count, rows, width = x_ref.shape
    half_cols = heads_ref.shape[2]
    half_dim = HEAD_DIM // 2
    units = half_cols // (2 * HEAD_DIM)
    cosine, sine = cosine_ref[...], sine_ref[...]

    def turned_back(heads):
        first, second = heads[:half_dim].astype(jnp.float32), heads[half_dim:].astype(jnp.float32)
        return [first * cosine + second * sine, second * cosine - first * sine]

    for micro in range(micro_count):
        for part in range(2):
            pieces = []
            for unit in range(units):
                block = (micro * 2 + part) * units + unit
                second = grad_ref[block, HEAD_DIM:, :]
                pieces += turned_back(grad_ref[block, :HEAD_DIM, :])
                pieces += turned_back(second) if unit % 2 == 0 else [second.astype(jnp.float32)]
            grad_rows[part, micro * rows : (micro + 1) * rows, :] = (
                jnp.concatenate(pieces, 0).T.astype(jnp.bfloat16)
            )
    gain = gain_ref[...]
    grad_gain = jnp.zeros((1, width), jnp.float32)
    for micro in range(micro_count):
        here = slice(micro * rows, (micro + 1) * rows)
        grad_normed = dot_f32(grad_rows[0, here, :], heads_ref[0], 1, 1) + dot_f32(
            grad_rows[1, here, :], heads_ref[1], 1, 1
        )
        x = x_ref[micro].astype(jnp.float32)
        scale = lax.rsqrt(jnp.mean(x * x, -1, keepdims=True) + EPS)
        gained = grad_normed * gain
        grad_gain = grad_gain + jnp.sum(grad_normed * x * scale, 0, keepdims=True)
        grad_x_ref[micro] = (
            grad_resid_ref[here, :]
            + scale * gained
            - x * scale**3 * jnp.mean(x * gained, -1, keepdims=True)
        )
    normed_t = normed_ref[...].T
    gain_cols = jnp.broadcast_to(grad_gain, (LANES, width)).T.astype(jnp.bfloat16)
    for ref, part in ((kept_ref, core), (given_ref, 1 - core)):
        ref[:, :half_cols] = dot_f32(normed_t, grad_rows[part], 1, 0).astype(jnp.bfloat16)
        ref[:, half_cols:] = gain_cols


def project_back(core, grad_own, heads, normed, x, grad_resid, gain, cosine, sine):
    micro_count, rows, width = x.shape
    half_cols = heads.shape[2]
    share = jax.ShapeDtypeStruct((width, half_cols + LANES), jnp.bfloat16)
    return pl.pallas_call(
        project_back_kernel,
        out_shape=(jax.ShapeDtypeStruct(x.shape, jnp.float32), share, share),
        in_specs=[pl.BlockSpec(memory_space=pltpu.SMEM)] + [whole_vmem()] * 8,
        out_specs=(whole_vmem(),) * 3,
        scratch_shapes=[pltpu.VMEM((2, micro_count * rows, half_cols), jnp.bfloat16)],
        compiler_params=pltpu.CompilerParams(vmem_limit_bytes=56 * MIB),
        name="project_back",
    )(core, grad_own, heads, normed, x, grad_resid, gain, cosine, sine)


def experts_kernel(*refs, slots, first_call, pieces, piece_count):
    place_ref, refs = refs[0], refs[1:]
    x_refs, dy_refs = refs[:slots], refs[slots : 2 * slots]
    w_route_ref, weight_refs = refs[2 * slots], refs[2 * slots + 1 : 2 * slots + 1 + piece_count]
    refs = refs[2 * slots + 1 + piece_count :]
    if not first_call:
        keep_in_ref, send_in_ref = refs[:2]
        refs = refs[2:]
    mix_refs, grad_x_refs = refs[:slots], refs[slots : 2 * slots]
    grad_gate_ref, keep_ref, send_ref = refs[2 * slots : 2 * slots + 3]
    (
        x_all, x_t, dy_all, dy_t, gates, grad_gates, mix_sum, grad_x_sum, grad_w, weights, sems
    ) = refs[2 * slots + 3 :]
    expert, expert_count = pl.program_id(0), pl.num_programs(0)
    rows, width = x_refs[0].shape
    total = slots * rows
    half = width // 2
    core = place_ref[0]

    def moves(index):
        copies = []
        for number, (array, whose, first, last) in enumerate(pieces[index]):
            target = weights.at[index % 2, pl.ds(first, last - first)]
            if whose is not None:
                part = core if whose == 0 else 1 - core
                target = weights.at[
                    index % 2, pl.ds(first, last - first), pl.ds(pl.multiple_of(part * half, half), half)
                ]
            copies.append(
                pltpu.make_async_copy(weight_refs[array], target, sems.at[index, number])
            )
        return copies

    @pl.when(expert == 0)
    def _():
        for copy in moves(0) + moves(1):
            copy.start()
        for slot in range(slots):
            here = slice(slot * rows, (slot + 1) * rows)
            x, dy = x_refs[slot][...], dy_refs[slot][:, :width]
            x_all[here, :] = x
            x_t[:, here] = x.T
            dy_all[here, :] = dy
            dy_t[:, here] = dy.T
            chosen = dy_refs[slot][:, width:].astype(jnp.float32)
            logits = jnp.where(chosen > 0.0, dot_f32(x, w_route_ref[...], 1, 0), NEG)
            raised = jnp.exp(logits - jnp.max(logits, 1, keepdims=True)) * chosen
            gates[here, :] = raised / jnp.sum(raised, 1, keepdims=True)
        mix_sum[...] = jnp.zeros_like(mix_sum)
        grad_x_sum[...] = jnp.zeros_like(grad_x_sum)

    for index in range(len(pieces)):

        @pl.when(expert == index)
        def _():
            if 1 <= index < len(pieces) - 1:
                for copy in moves(index + 1):
                    copy.start()
            for copy in moves(index):
                copy.wait()

    if first_call:
        grad_w[...] = jnp.zeros_like(grad_w)
    else:
        for part in range(2):
            grad_w[part] = jnp.where(core == part, keep_in_ref[0], send_in_ref[0]).astype(
                jnp.float32
            )
    buffer = lax.rem(expert, 2)
    w_gate, w_up, w_down_t = weights[buffer, 0], weights[buffer, 1], weights[buffer, 2]
    x = x_all[...]
    dy = dy_all[...].astype(jnp.float32)
    lane = lax.broadcasted_iota(jnp.int32, (total, LANES), 1)
    gate = jnp.sum(jnp.where(lane == place_ref[1 + expert], gates[...], 0.0), 1, keepdims=True)
    gate_row = jnp.broadcast_to(gate, (total, LANES)).T[:1]
    gate_pre = dot_f32(x, w_gate, 1, 0)
    up_pre = dot_f32(x, w_up, 1, 0)
    sigmoid_val = 1.0 / (1.0 + jnp.exp(-gate_pre))
    silu_val = gate_pre * sigmoid_val
    hidden = (silu_val * up_pre).astype(jnp.bfloat16)
    out = dot_f32(hidden, w_down_t, 1, 1).astype(jnp.bfloat16).astype(jnp.float32)
    grad_gate = jnp.sum(out * dy, 1, keepdims=True)
    grad_gates[pl.ds(expert, 1), :] = jnp.broadcast_to(grad_gate, (total, LANES)).T[:1]
    mix_sum[...] += gate * out
    grad_out = (gate * dy).astype(jnp.bfloat16)
    grad_hidden = dot_f32(grad_out, w_down_t, 1, 0)
    slope = sigmoid_val * (1.0 + gate_pre * (1.0 - sigmoid_val))
    grad_gate_pre = (grad_hidden * up_pre * slope).astype(jnp.bfloat16)
    grad_up_pre = (grad_hidden * silu_val).astype(jnp.bfloat16)
    grad_copy = dot_f32(grad_gate_pre, w_gate, 1, 1) + dot_f32(grad_up_pre, w_up, 1, 1)
    grad_x_sum[...] += grad_copy.astype(jnp.bfloat16).astype(jnp.float32)
    grad_out_t = (dy_t[...].astype(jnp.float32) * gate_row).astype(jnp.bfloat16)
    terms = (
        dot_f32(x_t[...], grad_gate_pre, 1, 0),
        dot_f32(x_t[...], grad_up_pre, 1, 0),
        dot_f32(grad_out_t, hidden, 1, 0),
    )
    for part in range(2):
        for matrix, term in enumerate(terms):
            grad_w[part, matrix] += term[part * half : (part + 1) * half]
    keep_ref[0] = grad_w[core].astype(jnp.bfloat16)
    send_ref[0] = grad_w[1 - core].astype(jnp.bfloat16)

    @pl.when(expert == expert_count - 1)
    def _():
        for slot in range(slots):
            here = slice(slot * rows, (slot + 1) * rows)
            mix_refs[slot][...] = mix_sum[here, :].astype(jnp.bfloat16)
            grad_x_refs[slot][...] = grad_x_sum[here, :].astype(jnp.bfloat16)
            grad_gate_ref[slot] = grad_gates[: grad_gate_ref.shape[1], here]


def experts(place, x_parts, dy_parts, w_route, weights, pieces, before):
    rows = dy_parts[0][0].shape[1]
    width, hidden_width = weights[0].shape[-2:]
    count, slots = len(pieces), len(x_parts)
    total = slots * rows
    half = width // 2
    first_call = before is None
    before = () if first_call else tuple(before)

    def at_block(shape, index):
        return pl.BlockSpec(
            shape,
            lambda expert: (index,) + (0,) * (len(shape) - 1),
            pipeline_mode=pl.Buffered(1),
        )

    row_spec = pl.BlockSpec((rows, width), lambda expert: (0, 0))
    grad_spec = pl.BlockSpec((1, 3, half, hidden_width), lambda expert: (expert, 0, 0, 0))
    grad_shape = jax.ShapeDtypeStruct((count, 3, half, hidden_width), jnp.bfloat16)
    row_shape = jax.ShapeDtypeStruct((rows, width), jnp.bfloat16)
    outs = pl.pallas_call(
        functools.partial(
            experts_kernel,
            slots=slots,
            first_call=first_call,
            pieces=pieces,
            piece_count=len(weights),
        ),
        grid=(count,),
        out_shape=(row_shape,) * (2 * slots)
        + (jax.ShapeDtypeStruct((slots, count, rows), jnp.float32), grad_shape, grad_shape),
        in_specs=[pl.BlockSpec(memory_space=pltpu.SMEM)]
        + [at_block((rows, width), index) for _, index in x_parts]
        + [at_block((None, rows, width + LANES), index) for _, index in dy_parts]
        + [at_block((width, LANES), 0)]
        + [pl.BlockSpec(memory_space=pl.ANY)] * len(weights)
        + [grad_spec] * len(before),
        out_specs=(row_spec,) * (2 * slots)
        + (pl.BlockSpec((slots, count, rows), lambda expert: (0, 0, 0)), grad_spec, grad_spec),
        scratch_shapes=[
            pltpu.VMEM((total, width), jnp.bfloat16),
            pltpu.VMEM((width, total), jnp.bfloat16),
            pltpu.VMEM((total, width), jnp.bfloat16),
            pltpu.VMEM((width, total), jnp.bfloat16),
            pltpu.VMEM((total, LANES), jnp.float32),
            pltpu.VMEM((8, total), jnp.float32),
            pltpu.VMEM((total, width), jnp.float32),
            pltpu.VMEM((total, width), jnp.float32),
            pltpu.VMEM((2, 3, half, hidden_width), jnp.float32),
            pltpu.VMEM((2, 3, width, hidden_width), jnp.bfloat16),
            pltpu.SemaphoreType.DMA((count, max(len(group) for group in pieces))),
        ],
        cost_estimate=pl.CostEstimate(
            flops=count * total * width * hidden_width * 18,
            bytes_accessed=count * width * hidden_width * 12,
            transcendentals=0,
        ),
        compiler_params=pltpu.CompilerParams(
            vmem_limit_bytes=62 * MIB, dimension_semantics=("arbitrary",)
        ),
        name="experts",
    )(
        place,
        *[array for array, _ in (*x_parts, *dy_parts)],
        w_route,
        *weights,
        *before,
    )
    return outs[:slots], outs[slots : 2 * slots], outs[2 * slots], outs[2 * slots + 1 :]


def together(*values):
    return lax.optimization_barrier(values)


def flip(values, bits):
    count = lax.axis_size("ep")
    return lax.ppermute(values, "ep", [(index, index ^ bits) for index in range(count)])


def swap_cores(values):
    return lax.ppermute(values, "tp", [(0, 1), (1, 0)])


def after(values, *earlier):
    return together(values, *earlier)[0]


def every_device(values):
    return lax.all_to_all(values, ("ep", "tp"), 0, 0, tiled=True)


def head_tables(first_pos, rows):
    positions = first_pos + jnp.arange(rows, dtype=jnp.int32)
    halves = jnp.arange(HEAD_DIM // 2, dtype=jnp.float32)
    freqs = THETA ** (-2.0 * halves / HEAD_DIM)
    angles = freqs[:, None] * positions.astype(jnp.float32)[None, :]
    return jnp.cos(angles), jnp.sin(angles)


def paired_layout(ep_count, tp_count, micro_count, slice_rows, width, q_cols, kv_cols, experts_here):
    group = q_cols // kv_cols
    kv_heads = kv_cols * tp_count // HEAD_DIM
    return (
        tp_count == 2
        and group == 2
        and ep_count == micro_count * kv_heads
        and ep_count == PLANE * PLANE
        and experts_here == 1
        and slice_rows >= PIECE
        and slice_rows % PIECE == 0
        and width % (2 * LANES) == 0
    )


def on_device_paired(
    tokens,
    gain_attn,
    w_query,
    w_key,
    w_value,
    w_output,
    gain_moe,
    w_router,
    w_gate,
    w_up,
    w_down,
    routes,
    piece_starts,
    cotangent,
):
    ep_count = lax.axis_size("ep")
    tp_count = lax.axis_size("tp")
    ep_index, tp_index = lax.axis_index("ep"), lax.axis_index("tp")
    micro_count, rows, width = tokens.shape
    devices = ep_count * tp_count
    seq_len = rows * devices
    all_rows = micro_count * rows
    shard = gain_attn.shape[0]
    q_cols, kv_cols = w_query.shape[1], w_key.shape[1]
    kv_here = kv_cols // HEAD_DIM
    half_cols = q_cols + 2 * kv_cols
    out_cols = w_output.shape[0]
    columns = ep_count // PLANE
    experts_all = ep_count
    core = tp_index.astype(jnp.int32).reshape(1)

    level, spot = ep_index // PLANE, ep_index % PLANE
    half = width // 2
    micros = range(micro_count)

    head_cols = jnp.stack(
        [
            w_query.reshape(shard, kv_here, 2, HEAD_DIM),
            jnp.stack(
                [
                    w_key.reshape(shard, kv_here, HEAD_DIM),
                    w_value.reshape(shard, kv_here, HEAD_DIM),
                ],
                2,
            ),
        ],
        3,
    ).reshape(shard, half_cols)
    small = jnp.concatenate([w_router, jnp.zeros((shard, LANES - experts_all), w_router.dtype)], 1)
    lanes = jnp.arange(LANES, dtype=jnp.int32)
    small = jnp.where(lanes == LANES // 2, gain_attn[:, None], small)
    small = jnp.where(lanes == LANES // 2 + 1, gain_moe[:, None], small)
    packed = jnp.concatenate([head_cols, small], 1)
    levels = [packed] + [flip(packed, PLANE * step) for step in range(1, columns)]
    mine = jnp.stack(levels)
    mine = [mine] + [flip(mine, step) for step in range(1, PLANE)]

    w_down_t = w_down[0].T
    first_half = tp_index * half
    expert_half = jnp.stack(
        [
            lax.dynamic_slice_in_dim(whole, first_half, half, 0)
            for whole in (w_gate[0], w_up[0], w_down_t)
        ]
    )
    expert_half, levels = together(expert_half, levels)
    far_out = flip(expert_half[2:], 2 * PLANE)
    mine, far_out = together(mine, far_out)
    other = [swap_cores(part) for part in mine]
    near_all = flip(expert_half, PLANE)

    x_rows = tokens.reshape(all_rows, width).astype(jnp.float32)
    device_index = ep_index * tp_count + tp_index
    cosine, sine = head_tables(device_index * rows, rows)
    spot_here = jnp.stack([tp_index, level, spot]).astype(jnp.int32)
    normed, sent, w_heads, small_all = project(
        spot_here, tokens, cosine, sine, mine, other, devices
    )
    w_route_full = small_all[:, :experts_all]
    gain_one = small_all[:, LANES // 2].astype(jnp.float32)
    gain_two = small_all[:, LANES // 2 + 1].astype(jnp.float32)
    own = every_device(sent)
    other = swap_cores(own[:, HEAD_DIM:, :])

    chosen = jnp.any(routes[:, :, :, None] == lanes, 2).astype(jnp.bfloat16)
    own_dy = jnp.concatenate([cotangent, chosen], 2)
    last_dy = flip(after(own_dy, sent), PLANE - 1)
    other, last_dy = together(other, last_dy)
    w_output_t, expert_late, far_out, dy_late, other = together(
        w_output.T, expert_half, far_out, own_dy, other
    )
    far_in = flip(expert_late[:2], 2 * PLANE)
    plane_dy = [flip(dy_late, step) for step in range(1, PLANE - 1)] + [last_dy]
    nearfar_out = flip(far_out, PLANE)
    gathered_out = lax.all_gather(w_output_t, ("ep", "tp"), axis=0, tiled=False)

    micro_here = ep_index // (ep_count // micro_count)
    starts = lax.dynamic_index_in_dim(piece_starts, micro_here, 0, keepdims=False)
    all_pos = jnp.arange(seq_len, dtype=jnp.int32)[None, :]
    inside = (all_pos >= starts[:, None]) & (all_pos < starts[:, None] + PIECE)
    piece_last = jnp.max(jnp.where(inside, starts[:, None] + (PIECE - 1), -1), 0, keepdims=True)
    limit = jnp.maximum(all_pos, piece_last).astype(jnp.int32)
    out_b, out_f, log_total = attend(core, own, other, limit)
    out_b, far_in, plane_dy, nearfar_out, near_all = together(
        out_b, far_in, plane_dy, nearfar_out, near_all
    )
    nearfar_in = flip(far_in, PLANE)
    attended_t = every_device(out_b).reshape(micro_count, out_cols * tp_count, rows)
    gathered_out = gathered_out.reshape(ep_count, tp_count, shard, out_cols)
    w_out_t = jnp.concatenate(
        [gathered_out[:, part].reshape(width, out_cols) for part in range(2)], 1
    )

    attn_rows = jnp.concatenate(
        [dot_f32(attended_t[micro], w_out_t, 0, 1) for micro in micros], 0
    )
    resid = x_rows + attn_rows
    scale_two = rms_scale(resid)
    normed_two = (resid * scale_two * gain_two).astype(jnp.bfloat16)
    normed_parts = [normed_two[micro * rows : (micro + 1) * rows] for micro in micros]
    plane_x = [[flip(normed_parts[0], step) for step in range(1, PLANE)]]

    column_weights = [w_gate, w_up, w_down_t[None]]
    for piece in (near_all, far_in, far_out, after(nearfar_in, normed_two), nearfar_out):
        column_weights += [piece, swap_cores(piece)]
    pieces = [[(0, None, 0, 1), (1, None, 1, 2), (2, None, 2, 3)]]
    pieces.append([(5, 0, 0, 2), (6, 1, 0, 2), (7, 0, 2, 3), (8, 1, 2, 3)])
    pieces.append([(3, 0, 0, 3), (4, 1, 0, 3)])
    pieces.append([(9, 0, 0, 2), (10, 1, 0, 2), (11, 0, 2, 3), (12, 1, 2, 3)])

    logits = jnp.dot(normed_two, w_route_full, preferred_element_type=jnp.float32)
    route_rows = routes.reshape(all_rows, -1)
    expert_ids = jnp.arange(experts_all, dtype=jnp.int32)
    route_hot = (route_rows[:, :, None] == expert_ids[None, None, :]).astype(jnp.float32)
    picked = jnp.sum(route_hot * logits[:, None, :], -1)
    highest = jnp.max(picked, -1, keepdims=True)
    raised = jnp.exp(picked - highest)
    gates = raised / jnp.sum(raised, -1, keepdims=True)

    slot_ids = jnp.stack(
        [
            jnp.stack([(level ^ up) * PLANE + (spot ^ step) for up in (0, 2, 1, 3)])
            for step in range(PLANE)
        ]
    )
    slot_hot = (route_rows[None, None, :, :] == slot_ids[:, :, None, None]).astype(jnp.float32)

    place = jnp.concatenate([core, slot_ids[0]])
    own_mix, own_grad_x, own_grad_gate, before = experts(
        place,
        [(normed_two, micro) for micro in micros],
        [(own_dy, micro) for micro in micros],
        small_all,
        column_weights,
        pieces,
        None,
    )
    leaving = normed_parts[1:]
    leaving, own_grad_gate = together(leaving, own_grad_gate)
    plane_x += [[flip(part, step) for step in range(1, PLANE)] for part in leaving]
    far_mix, late_mix, far_grad_x, far_grad_gate = [], [], [], []
    for micro in micros:
        mix, grad_x, grad_gate, before = experts(
            place,
            [(part, 0) for part in plane_x[micro]],
            [(part, micro) for part in plane_dy],
            small_all,
            column_weights,
            pieces,
            before,
        )
        if micro:
            grad_x, mix, grad_gate, before, far_grad_x, far_mix = together(
                grad_x, mix, grad_gate, before, far_grad_x, far_mix
            )
        far_grad_x.append([flip(grad_x[step - 1], step) for step in range(1, PLANE)])
        far_grad_gate.append(grad_gate)
        early = PLANE - 2 if micro < micro_count - 1 else 0
        far_mix.append([flip(mix[step - 1], step) for step in range(1, early + 1)])
        late_mix.append([(mix[step - 1], step) for step in range(early + 1, PLANE)])
    far_grad_gate = jnp.concatenate(far_grad_gate, 2)
    far_grad_gate = [flip(far_grad_gate[step - 1], step) for step in range(1, PLANE)]
    keep_w, send_w = before
    given_w = swap_cores(send_w)

    def column_sum(first, last, low, high):
        kept = keep_w[first:last, low:high].astype(jnp.float32)
        return (kept + given_w[first:last, low:high].astype(jnp.float32)).astype(jnp.bfloat16)

    own_w = keep_w[0].astype(jnp.float32) + given_w[0].astype(jnp.float32)
    far_in_w, near_in_w, last_in_w = [column_sum(slot, slot + 1, 0, 2) for slot in (1, 2, 3)]
    far_out_w, near_out_w = column_sum(1, 2, 2, 3), column_sum(2, 4, 2, 3)
    near_out_w, far_grad_x[-1] = together(near_out_w, far_grad_x[-1])
    near_out_w = flip(near_out_w, PLANE)

    def at_home(own_parts, far_parts):
        return jnp.concatenate(
            [
                own_parts[micro].astype(jnp.float32)
                + sum(part.astype(jnp.float32) for part in far_parts[micro])
                for micro in micros
            ],
            0,
        )

    grad_out = cotangent.reshape(all_rows, width).astype(jnp.float32)
    slot_grads = jnp.stack(
        [jnp.concatenate([own_grad_gate[micro] for micro in micros], 1)]
        + far_grad_gate
    )
    grad_gates = jnp.sum(slot_hot * slot_grads[:, :, :, None], (0, 1))
    grad_spread = gates * (grad_gates - jnp.sum(gates * grad_gates, -1, keepdims=True))
    grad_logits = jnp.sum(grad_spread[:, :, None] * route_hot, 1).astype(jnp.bfloat16)
    grad_normed_two = at_home(own_grad_x, far_grad_x) + dot_f32(
        grad_logits, w_route_full, 1, 1
    )
    grad_route = dot_f32(normed_two, grad_logits, 0, 0)
    gained_two = grad_normed_two * gain_two
    grad_gain_two = jnp.sum(grad_normed_two * resid * scale_two, 0)
    grad_resid = (
        grad_out
        + scale_two * gained_two
        - resid * scale_two**3 * jnp.mean(resid * gained_two, -1, keepdims=True)
    )
    grad_branch = grad_resid.astype(jnp.bfloat16)
    grad_att = jnp.concatenate(
        [
            dot_f32(w_out_t, grad_branch[micro * rows : (micro + 1) * rows], 0, 1).astype(
                jnp.bfloat16
            )
            for micro in micros
        ],
        0,
    ).reshape(devices, HEAD_DIM, rows)
    grad_outw = sum(
        dot_f32(grad_branch[micro * rows : (micro + 1) * rows], attended_t[micro], 0, 1)
        for micro in micros
    )
    grad_att, near_out_w = together(grad_att, near_out_w)
    near_out_w = near_out_w.astype(jnp.float32)
    grad_heads = every_device(grad_att)
    grad_heads, near_out_w, far_in_w, near_in_w, last_in_w, far_out_w = together(
        grad_heads, near_out_w, far_in_w, near_in_w, last_in_w, far_out_w
    )
    far_in_w = flip(far_in_w, 2 * PLANE)
    near_in_w = flip(near_in_w, PLANE)
    last_in_w = flip(last_in_w, 3 * PLANE)
    far_out_w = flip(
        (far_out_w[0].astype(jnp.float32) + near_out_w[1]).astype(jnp.bfloat16), 2 * PLANE
    )

    def to_shards(kept, given):
        core_sum = kept.astype(jnp.float32) + swap_cores(given).astype(jnp.float32)
        shares = lax.all_to_all(
            core_sum.astype(jnp.bfloat16).reshape(ep_count, shard, -1), "ep", 0, 0, tiled=True
        )
        return jnp.sum(shares.astype(jnp.float32), 0)

    def in_lanes(columns_f):
        small = jnp.concatenate(columns_f, 1)
        return jnp.pad(small, ((0, 0), (0, LANES - small.shape[1]))).astype(jnp.bfloat16)

    def own_rows(values):
        return lax.dynamic_slice_in_dim(values, tp_index * (shard // 2), shard // 2, 0)

    grad_heads, grad_outw, grad_route, grad_gain_two = together(
        grad_heads, grad_outw.astype(jnp.bfloat16), grad_route, grad_gain_two
    )
    late_small = in_lanes([grad_route, grad_gain_two[:, None]])
    out_parts = [
        jnp.concatenate([grad_outw[:, part * out_cols : (part + 1) * out_cols], late_small], 1)
        for part in range(2)
    ]
    out_kept = jnp.where(tp_index == 0, out_parts[0], out_parts[1])
    out_given = jnp.where(tp_index == 0, out_parts[1], out_parts[0])
    out_sum = out_kept.astype(jnp.float32) + swap_cores(out_given).astype(jnp.float32)
    plane_groups = [
        [up * PLANE + step for step in range(PLANE)] for up in range(columns)
    ]
    column_groups = [
        [up * PLANE + step for up in range(columns)] for step in range(PLANE)
    ]
    out_spots = lax.all_to_all(
        jnp.swapaxes(
            out_sum.astype(jnp.bfloat16).reshape(columns, PLANE, shard, -1), 0, 1
        ),
        "ep",
        0,
        0,
        tiled=True,
        axis_index_groups=plane_groups,
    )

    grad_q, keep_kv, send_kv = attend_back(
        core, own, other, limit, out_f, log_total, grad_heads
    )
    grad_q, keep_kv, send_kv, far_in_w, near_in_w, last_in_w, far_out_w, out_spots = together(
        grad_q, keep_kv, send_kv, far_in_w, near_in_w, last_in_w, far_out_w, out_spots
    )
    for micro in micros:
        far_mix[micro] = far_mix[micro] + [
            flip(after(part, grad_q), step) for part, step in late_mix[micro]
        ]
    grad_kv = (keep_kv + swap_cores(send_kv).astype(jnp.float32)).astype(jnp.bfloat16)
    grad_own = every_device(jnp.concatenate([grad_q, grad_kv], 1))
    grad_own, far_mix = together(grad_own, far_mix)

    out_levels = jnp.sum(out_spots.astype(jnp.float32), 0).astype(jnp.bfloat16)
    out_levels = lax.all_to_all(
        out_levels, "ep", 0, 0, tiled=True, axis_index_groups=column_groups
    )
    out_share = jnp.sum(out_levels.astype(jnp.float32), 0)
    out_small = own_rows(out_share[:, out_cols:])
    grad_tokens, kept, given = project_back(
        core, grad_own, w_heads, normed, tokens, grad_resid, gain_one[None, :], cosine, sine
    )
    kept, given, far_in_w, near_in_w, last_in_w, far_out_w = together(
        kept, given, far_in_w, near_in_w, last_in_w, far_out_w
    )
    grad_in_w = own_w[:2] + sum(
        part[0].astype(jnp.float32) for part in (far_in_w, near_in_w, last_in_w)
    )
    grad_out_w = own_w[2] + near_out_w[0, 0] + far_out_w[0].astype(jnp.float32)
    mixed = (resid + at_home(own_mix, far_mix)).astype(jnp.bfloat16)

    own_share = to_shards(kept, given)
    head_grads = own_share[:, :half_cols].reshape(shard, kv_here, 2, 2, HEAD_DIM)
    return (
        mixed.reshape(micro_count, rows, width),
        grad_tokens,
        own_rows(own_share[:, half_cols:])[:, 0],
        head_grads[:, :, :, 0].reshape(shard, q_cols),
        head_grads[:, :, 0, 1].reshape(shard, kv_cols),
        head_grads[:, :, 1, 1].reshape(shard, kv_cols),
        out_share[:, :out_cols].T,
        out_small[:, experts_all],
        out_small[:, :experts_all],
        grad_in_w[0][None],
        grad_in_w[1][None],
        grad_out_w.T[None],
    )


def on_device(*args):
    tokens, w_query, w_key, w_gate = args[0], args[2], args[3], args[8]
    paired = paired_layout(
        lax.axis_size("ep"),
        lax.axis_size("tp"),
        *tokens.shape,
        w_query.shape[1],
        w_key.shape[1],
        w_gate.shape[0],
    )
    return (on_device_paired if paired else on_device_general)(*args)


def solution(mesh):
    in_specs = (
        P(None, ("ep", "tp"), None),
        P("ep"),
        P("ep", "tp"),
        P("ep", "tp"),
        P("ep", "tp"),
        P("tp", "ep"),
        P("ep"),
        P("ep", None),
        P("ep", None, None),
        P("ep", None, None),
        P("ep", None, None),
        P(None, ("ep", "tp"), None),
        P(),
        P(None, ("ep", "tp"), None),
    )
    out_specs = (
        P(None, ("ep", "tp"), None),
        P(None, ("ep", "tp"), None),
        P(("ep", "tp")),
        P("ep", "tp"),
        P("ep", "tp"),
        P("ep", "tp"),
        P("tp", "ep"),
        P(("ep", "tp")),
        P(("ep", "tp"), None),
        P("ep", "tp", None),
        P("ep", "tp", None),
        P("ep", None, "tp"),
    )
    return jax.shard_map(
        on_device, mesh=mesh, in_specs=in_specs, out_specs=out_specs, check_vma=False
    )
```

```python
import functools
import math

import jax
import jax.numpy as jnp
from jax import lax
from jax.experimental import pallas as pl
from jax.experimental.pallas import tpu as pltpu
from jax.sharding import PartitionSpec as P

HEAD_DIM = 64
PIECE = 256
PLANE = 4
LANES = 128
MIB = 1 << 20


EPS = 1e-06
THETA = 10000.0
NEG = -1e30


def rms_scale(values):
    return lax.rsqrt(jnp.mean(values * values, -1, keepdims=True) + EPS)


def angle_tables(positions):
    halves = jnp.arange(HEAD_DIM // 2, dtype=jnp.float32)
    freqs = THETA ** (-2.0 * halves / HEAD_DIM)
    angles = positions.astype(jnp.float32)[:, None] * freqs[None, :]
    return (jnp.cos(angles)[:, None, :], jnp.sin(angles)[:, None, :])


def rotate(values, cosine, sine):
    half_dim = values.shape[-1] // 2
    first_half = values[..., :half_dim]
    second_half = values[..., half_dim:]
    return jnp.concatenate(
        [first_half * cosine - second_half * sine, second_half * cosine + first_half * sine], -1
    )


def piece_index(starts, positions):
    inside = (positions[:, None] >= starts[None, :]) & (
        positions[:, None] < starts[None, :] + PIECE
    )
    numbers = jnp.arange(1, starts.shape[0] + 1, dtype=jnp.int32)
    return jnp.sum(jnp.where(inside, numbers[None, :], 0), -1) - 1


def allowed_mask(query_pos, query_piece, key_pos, key_piece):
    return (key_pos[None, :] <= query_pos[:, None]) | (
        key_piece[None, :] == query_piece[:, None]
    ) & (query_piece[:, None] >= 0)


def to_groups(rows, kv_here, group_size):
    row_total = rows.shape[0]
    return (
        rows.reshape(row_total, kv_here, group_size, HEAD_DIM)
        .transpose(1, 2, 0, 3)
        .reshape(kv_here, group_size * row_total, HEAD_DIM)
    )


def from_groups(grouped, row_total):
    kv_here = grouped.shape[0]
    return (
        grouped.reshape(kv_here, -1, row_total, HEAD_DIM)
        .transpose(2, 0, 1, 3)
        .reshape(row_total, -1)
    )


def tp_major(values, ep_count, tp_count):
    leading = values.shape[0]
    shaped = values.reshape(
        (ep_count, tp_count, leading // (ep_count * tp_count)) + values.shape[1:]
    )
    return jnp.swapaxes(shaped, 0, 1).reshape(values.shape)


def add_all(left_parts, right_parts):
    return tuple((left_part + right_part for left_part, right_part in zip(left_parts, right_parts)))


def reduce_grads(parts, ep_count, tp_count):
    (
        grad_gate_w,
        grad_up_w,
        grad_down_w,
        grad_gain_one,
        grad_gain_two,
        grad_route,
        grad_proj,
        grad_outw,
    ) = parts
    tp_sums = (
        lax.psum_scatter(
            grad_gate_w.astype(jnp.bfloat16), "tp", scatter_dimension=1, tiled=True
        ).astype(jnp.float32),
        lax.psum_scatter(
            grad_up_w.astype(jnp.bfloat16), "tp", scatter_dimension=1, tiled=True
        ).astype(jnp.float32),
        lax.psum_scatter(
            grad_down_w.astype(jnp.bfloat16), "tp", scatter_dimension=2, tiled=True
        ).astype(jnp.float32),
        lax.psum_scatter(
            tp_major(grad_gain_one, ep_count, tp_count).astype(jnp.bfloat16),
            "tp",
            scatter_dimension=0,
            tiled=True,
        ).astype(jnp.float32),
        lax.psum_scatter(
            tp_major(grad_gain_two, ep_count, tp_count).astype(jnp.bfloat16),
            "tp",
            scatter_dimension=0,
            tiled=True,
        ).astype(jnp.float32),
        lax.psum_scatter(
            tp_major(grad_route, ep_count, tp_count).astype(jnp.bfloat16),
            "tp",
            scatter_dimension=0,
            tiled=True,
        ).astype(jnp.float32),
    )
    ep_sums = (
        lax.psum_scatter(
            grad_proj.astype(jnp.bfloat16), "ep", scatter_dimension=0, tiled=True
        ).astype(jnp.float32),
        lax.psum_scatter(
            grad_outw.astype(jnp.bfloat16), "ep", scatter_dimension=1, tiled=True
        ).astype(jnp.float32),
        lax.psum_scatter(
            tp_sums[3].astype(jnp.bfloat16), "ep", scatter_dimension=0, tiled=True
        ).astype(jnp.float32),
        lax.psum_scatter(
            tp_sums[4].astype(jnp.bfloat16), "ep", scatter_dimension=0, tiled=True
        ).astype(jnp.float32),
        lax.psum_scatter(
            tp_sums[5].astype(jnp.bfloat16), "ep", scatter_dimension=0, tiled=True
        ).astype(jnp.float32),
    )
    return (
        tp_sums[0],
        tp_sums[1],
        tp_sums[2],
        ep_sums[2],
        ep_sums[3],
        ep_sums[4],
        ep_sums[0],
        ep_sums[1],
    )


def on_device_general(
    tokens,
    gain_attn,
    w_query,
    w_key,
    w_value,
    w_output,
    gain_moe,
    w_router,
    w_gate,
    w_up,
    w_down,
    routes,
    piece_starts,
    cotangent,
):
    ep_count = lax.axis_size("ep")
    tp_count = lax.axis_size("tp")
    micro_count, slice_rows, width = tokens.shape
    span_rows = slice_rows * tp_count
    seq_len = span_rows * ep_count
    q_cols = w_query.shape[1]
    kv_cols = w_key.shape[1]
    kv_here = kv_cols // HEAD_DIM
    group_size = q_cols // kv_cols
    query_rows = group_size * span_rows
    experts_here = w_gate.shape[0]
    experts_all = experts_here * ep_count
    top_count = routes.shape[2]
    capacity = max(2, slice_rows * top_count * 3 // (2 * experts_all))
    expert_rows = ep_count * capacity
    score_scale = HEAD_DIM ** (-0.5)
    key_block = math.gcd(seq_len, 512)
    block_count = seq_len // key_block
    local_pos = lax.axis_index("ep") * span_rows + jnp.arange(span_rows, dtype=jnp.int32)
    all_pos = jnp.arange(seq_len, dtype=jnp.int32)
    row_pos = jnp.tile(local_pos, group_size)
    cosine, sine = angle_tables(local_pos)
    slot_ids = jnp.arange(experts_all * capacity, dtype=jnp.int32)
    expert_ids = jnp.arange(experts_all, dtype=jnp.int32)
    gathered = (
        lax.all_gather(gain_attn, "ep", axis=0, tiled=True),
        lax.all_gather(w_query, "ep", axis=0, tiled=True),
        lax.all_gather(w_key, "ep", axis=0, tiled=True),
        lax.all_gather(w_value, "ep", axis=0, tiled=True),
        lax.all_gather(w_output, "ep", axis=1, tiled=True),
        lax.all_gather(gain_moe, "ep", axis=0, tiled=True),
        lax.all_gather(w_router, "ep", axis=0, tiled=True),
    )
    gain_one = gathered[0].astype(jnp.float32)
    w_proj = jnp.concatenate([gathered[1], gathered[2], gathered[3]], 1)
    w_out_full = gathered[4]
    gain_two = gathered[5].astype(jnp.float32)
    w_route_full = gathered[6]
    totals = None
    mixed_rows = []
    grad_rows = []
    for micro_index in range(micro_count):
        starts = piece_starts[micro_index]
        key_pieces = piece_index(starts, all_pos)
        row_piece = jnp.tile(piece_index(starts, local_pos), group_size)
        x_rows = tokens[micro_index].astype(jnp.float32)
        scale_one = rms_scale(x_rows)
        normed = (x_rows * scale_one * gain_one).astype(jnp.bfloat16)
        normed_all = lax.all_gather(normed, "tp", axis=0, tiled=True)
        projected = jnp.dot(normed_all, w_proj, preferred_element_type=jnp.float32)
        queries = rotate(
            projected[:, :q_cols].reshape(span_rows, -1, HEAD_DIM), cosine, sine
        ).astype(jnp.bfloat16)
        q_grouped = to_groups(queries.reshape(span_rows, q_cols), kv_here, group_size)
        keys_own = (
            rotate(
                projected[:, q_cols : q_cols + kv_cols].reshape(span_rows, kv_here, HEAD_DIM),
                cosine,
                sine,
            )
            .astype(jnp.bfloat16)
            .reshape(span_rows, kv_cols)
        )
        values_own = projected[:, q_cols + kv_cols :].astype(jnp.bfloat16)
        keys_all, values_all = (
            lax.all_gather(keys_own, "ep", axis=0, tiled=True),
            lax.all_gather(values_own, "ep", axis=0, tiled=True),
        )

        def block_scores(first_row, block_size):
            key_blk = lax.dynamic_slice_in_dim(keys_all, first_row, block_size, 0).reshape(
                block_size, kv_here, HEAD_DIM
            )
            value_blk = lax.dynamic_slice_in_dim(values_all, first_row, block_size, 0).reshape(
                block_size, kv_here, HEAD_DIM
            )
            key_pos = first_row + jnp.arange(block_size, dtype=jnp.int32)
            piece_blk = lax.dynamic_slice_in_dim(key_pieces, first_row, block_size, 0)
            allowed = allowed_mask(row_pos, row_piece, key_pos, piece_blk)[None]
            scores = (
                jnp.einsum("hrd,khd->hrk", q_grouped, key_blk, preferred_element_type=jnp.float32)
                * score_scale
            )
            return (scores, allowed, key_blk, value_blk)

        def forward_step(block_index, running):
            run_max, run_sum, run_acc = running
            scores, allowed, key_blk, value_blk = block_scores(block_index * key_block, key_block)
            scores = jnp.where(allowed, scores, NEG)
            new_max = jnp.maximum(run_max, jnp.max(scores, -1))
            weights = jnp.where(allowed, jnp.exp(scores - new_max[..., None]), 0.0)
            factor = jnp.exp(run_max - new_max)
            run_sum = run_sum * factor + jnp.sum(weights, -1)
            run_acc = run_acc * factor[..., None] + jnp.einsum(
                "hrk,khd->hrd",
                weights.astype(jnp.bfloat16),
                value_blk,
                preferred_element_type=jnp.float32,
            )
            return (new_max, run_sum, run_acc)

        start_state = (
            jnp.full((kv_here, query_rows), NEG, jnp.float32),
            jnp.zeros((kv_here, query_rows), jnp.float32),
            jnp.zeros((kv_here, query_rows, HEAD_DIM), jnp.float32),
        )
        run_max, run_sum, run_acc = lax.fori_loop(0, block_count, forward_step, start_state)
        log_total = run_max + jnp.log(run_sum)
        attended_f = run_acc / run_sum[..., None]
        attended = from_groups(attended_f.astype(jnp.bfloat16), span_rows)
        partial_attn = jnp.dot(attended, w_out_full, preferred_element_type=jnp.float32)
        attn_rows = lax.psum_scatter(
            partial_attn.astype(jnp.bfloat16), "tp", scatter_dimension=0, tiled=True
        ).astype(jnp.float32)
        resid = x_rows + attn_rows
        scale_two = rms_scale(resid)
        normed_two = (resid * scale_two * gain_two).astype(jnp.bfloat16)
        logits = jnp.dot(normed_two, w_route_full, preferred_element_type=jnp.float32)
        route_rows = routes[micro_index]
        route_hot = (route_rows[:, :, None] == expert_ids[None, None, :]).astype(jnp.float32)
        picked = jnp.sum(route_hot * logits[:, None, :], -1)
        highest = jnp.max(picked, -1, keepdims=True)
        raised = jnp.exp(picked - highest)
        gates = raised / jnp.sum(raised, -1, keepdims=True)
        flat_hot = route_hot.reshape(-1, experts_all)
        earlier = jnp.cumsum(flat_hot, 0) - flat_hot
        slot_of = jnp.sum(earlier * flat_hot, -1).astype(jnp.int32)
        target = route_rows.reshape(-1) * capacity + slot_of
        place_pairs = slot_ids[:, None] == target[None, :]
        place_pairs_b = place_pairs.astype(jnp.bfloat16)
        place_tokens = jnp.any(place_pairs.reshape(-1, slice_rows, top_count), -1).astype(
            jnp.bfloat16
        )
        send_rows = (
            jnp.dot(place_tokens, normed_two, preferred_element_type=jnp.float32)
            .astype(jnp.bfloat16)
            .reshape(ep_count, experts_here, capacity, width)
        )
        received = lax.all_to_all(send_rows, "ep", split_axis=0, concat_axis=0, tiled=True)
        expert_in = jnp.swapaxes(received, 0, 1).reshape(experts_here, expert_rows, width)
        gate_pre = jnp.einsum("erd,edf->erf", expert_in, w_gate, preferred_element_type=jnp.float32)
        up_pre = jnp.einsum("erd,edf->erf", expert_in, w_up, preferred_element_type=jnp.float32)
        sigmoid_val = jax.nn.sigmoid(gate_pre)
        silu_val = gate_pre * sigmoid_val
        hidden = (silu_val * up_pre).astype(jnp.bfloat16)
        expert_out = jnp.einsum(
            "erf,efd->erd", hidden, w_down, preferred_element_type=jnp.float32
        ).astype(jnp.bfloat16)
        returned = lax.all_to_all(
            jnp.swapaxes(expert_out.reshape(experts_here, ep_count, capacity, width), 0, 1),
            "ep",
            split_axis=0,
            concat_axis=0,
            tiled=True,
        )
        slot_rows = returned.reshape(-1, width)
        picked_rows = jnp.einsum(
            "sn,sd->nd", place_pairs_b, slot_rows, preferred_element_type=jnp.float32
        ).reshape(slice_rows, top_count, width)
        mixture = jnp.einsum("tk,tkd->td", gates, picked_rows)
        mixed_rows.append((resid + mixture).astype(jnp.bfloat16))
        grad_out = cotangent[micro_index].astype(jnp.float32)
        grad_gates = jnp.einsum("tkd,td->tk", picked_rows, grad_out)
        weighted = (
            (gates[:, :, None] * grad_out[:, None, :]).astype(jnp.bfloat16).reshape(-1, width)
        )
        grad_slots = (
            jnp.dot(place_pairs_b, weighted, preferred_element_type=jnp.float32)
            .astype(jnp.bfloat16)
            .reshape(ep_count, experts_here, capacity, width)
        )
        grad_recv = lax.all_to_all(grad_slots, "ep", split_axis=0, concat_axis=0, tiled=True)
        grad_expert = jnp.swapaxes(grad_recv, 0, 1).reshape(experts_here, expert_rows, width)
        grad_hidden = jnp.einsum(
            "erd,efd->erf", grad_expert, w_down, preferred_element_type=jnp.float32
        )
        grad_down_w = jnp.einsum(
            "erf,erd->efd", hidden, grad_expert, preferred_element_type=jnp.float32
        )
        silu_slope = sigmoid_val * (1.0 + gate_pre * (1.0 - sigmoid_val))
        grad_gate_pre = (grad_hidden * up_pre * silu_slope).astype(jnp.bfloat16)
        grad_up_pre = (grad_hidden * silu_val).astype(jnp.bfloat16)
        grad_gate_w = jnp.einsum(
            "erd,erf->edf", expert_in, grad_gate_pre, preferred_element_type=jnp.float32
        )
        grad_up_w = jnp.einsum(
            "erd,erf->edf", expert_in, grad_up_pre, preferred_element_type=jnp.float32
        )
        grad_copy = (
            jnp.einsum("erf,edf->erd", grad_gate_pre, w_gate, preferred_element_type=jnp.float32)
            + jnp.einsum("erf,edf->erd", grad_up_pre, w_up, preferred_element_type=jnp.float32)
        ).astype(jnp.bfloat16)
        grad_back = lax.all_to_all(
            jnp.swapaxes(grad_copy.reshape(experts_here, ep_count, capacity, width), 0, 1),
            "ep",
            split_axis=0,
            concat_axis=0,
            tiled=True,
        ).reshape(-1, width)
        grad_spread = gates * (grad_gates - jnp.sum(gates * grad_gates, -1, keepdims=True))
        grad_logits = jnp.einsum("tk,tke->te", grad_spread, route_hot).astype(jnp.bfloat16)
        grad_normed_two = jnp.einsum(
            "st,sd->td", place_tokens, grad_back, preferred_element_type=jnp.float32
        ) + jnp.einsum("te,de->td", grad_logits, w_route_full, preferred_element_type=jnp.float32)
        grad_route = jnp.einsum(
            "td,te->de", normed_two, grad_logits, preferred_element_type=jnp.float32
        )
        gained_two = grad_normed_two * gain_two
        grad_gain_two = jnp.sum(grad_normed_two * resid * scale_two, 0)
        grad_resid = (
            grad_out
            + scale_two * gained_two
            - resid * scale_two**3 * jnp.mean(resid * gained_two, -1, keepdims=True)
        )
        grad_attn = lax.all_gather(grad_resid.astype(jnp.bfloat16), "tp", axis=0, tiled=True)
        grad_outw = jnp.einsum("cq,cd->qd", attended, grad_attn, preferred_element_type=jnp.float32)
        grad_att_rows = jnp.einsum(
            "cd,qd->cq", grad_attn, w_out_full, preferred_element_type=jnp.float32
        ).astype(jnp.bfloat16)
        grad_grouped = to_groups(grad_att_rows, kv_here, group_size)
        delta = jnp.sum(grad_grouped.astype(jnp.float32) * attended_f, -1)

        def block_grads(first_row, block_size):
            scores, allowed, key_blk, value_blk = block_scores(first_row, block_size)
            probs = jnp.where(allowed, jnp.exp(scores - log_total[..., None]), 0.0)
            grad_probs = jnp.einsum(
                "hrd,khd->hrk", grad_grouped, value_blk, preferred_element_type=jnp.float32
            )
            grad_scores = (probs * (grad_probs - delta[..., None])).astype(jnp.bfloat16)
            return (probs, grad_scores, key_blk)

        def key_side(first_row, block_size):
            probs, grad_scores, key_blk = block_grads(first_row, block_size)
            grad_keys = (
                jnp.einsum(
                    "hrk,hrd->khd", grad_scores, q_grouped, preferred_element_type=jnp.float32
                ).reshape(block_size, kv_cols)
                * score_scale
            )
            grad_values = jnp.einsum(
                "hrk,hrd->khd",
                probs.astype(jnp.bfloat16),
                grad_grouped,
                preferred_element_type=jnp.float32,
            ).reshape(block_size, kv_cols)
            return (jnp.concatenate([grad_keys, grad_values], 1), grad_scores, key_blk)

        query_zero = jnp.zeros((kv_here, query_rows, HEAD_DIM), jnp.float32)

        def backward_step(block_index, running):
            grad_query, grad_kv = running
            first_row = block_index * key_block
            kv_terms, grad_scores, key_blk = key_side(first_row, key_block)
            grad_query = grad_query + jnp.einsum(
                "hrk,khd->hrd", grad_scores, key_blk, preferred_element_type=jnp.float32
            )
            grad_kv = lax.dynamic_update_slice_in_dim(grad_kv, kv_terms, first_row, 0)
            return (grad_query, grad_kv)

        grad_query, grad_kv = lax.fori_loop(
            0,
            block_count,
            backward_step,
            (query_zero, jnp.zeros((seq_len, 2 * kv_cols), jnp.float32)),
        )
        grad_kv_own = lax.psum_scatter(
            grad_kv.astype(jnp.bfloat16), "ep", scatter_dimension=0, tiled=True
        ).astype(jnp.float32)
        grad_query_rows = from_groups(grad_query * score_scale, span_rows).reshape(
            span_rows, -1, HEAD_DIM
        )
        grad_query_raw = (
            rotate(grad_query_rows, cosine, -sine).astype(jnp.bfloat16).reshape(span_rows, q_cols)
        )
        grad_key_raw = (
            rotate(grad_kv_own[:, :kv_cols].reshape(span_rows, kv_here, HEAD_DIM), cosine, -sine)
            .astype(jnp.bfloat16)
            .reshape(span_rows, kv_cols)
        )
        grad_value_raw = grad_kv_own[:, kv_cols:].astype(jnp.bfloat16)
        grad_proj_rows = jnp.concatenate([grad_query_raw, grad_key_raw, grad_value_raw], 1)
        grad_proj = jnp.einsum(
            "cd,cp->dp", normed_all, grad_proj_rows, preferred_element_type=jnp.float32
        )
        grad_normed_part = jnp.einsum(
            "cp,dp->cd", grad_proj_rows, w_proj, preferred_element_type=jnp.float32
        )
        grad_normed = lax.psum_scatter(
            grad_normed_part.astype(jnp.bfloat16), "tp", scatter_dimension=0, tiled=True
        ).astype(jnp.float32)
        gained_one = grad_normed * gain_one
        grad_gain_one = jnp.sum(grad_normed * x_rows * scale_one, 0)
        grad_rows.append(
            grad_resid
            + scale_one * gained_one
            - x_rows * scale_one**3 * jnp.mean(x_rows * gained_one, -1, keepdims=True)
        )
        parts = (
            grad_gate_w,
            grad_up_w,
            grad_down_w,
            grad_gain_one,
            grad_gain_two,
            grad_route,
            grad_proj,
            grad_outw,
        )
        reduced = reduce_grads(parts, ep_count, tp_count)
        totals = reduced if totals is None else add_all(totals, reduced)
    grad_qkv = totals[6]
    return (
        jnp.stack(mixed_rows),
        jnp.stack(grad_rows),
        totals[3],
        grad_qkv[:, :q_cols],
        grad_qkv[:, q_cols : q_cols + kv_cols],
        grad_qkv[:, q_cols + kv_cols :],
        totals[7],
        totals[4],
        totals[5],
        totals[0],
        totals[1],
        totals[2],
    )


RAISE_AT = 40.0


def dot_f32(left, right, left_dim, right_dim):
    return lax.dot_general(
        left, right, (((left_dim,), (right_dim,)), ((), ())), preferred_element_type=jnp.float32
    )


def at_rows(first_row, count):
    return pl.ds(pl.multiple_of(first_row, count), count)


def whole_vmem():
    return pl.BlockSpec(memory_space=pltpu.VMEM)


def attend_kernel(
    tp_ref, own_ref, other_ref, limit_ref, out_ref, out_f_ref, log_ref,
    keys, queries, values, highest, total,
    *, query_block, key_block, chain
):
    core = tp_ref[0]
    blocks, _, rows = own_ref.shape
    seq_len = blocks * rows
    chains = query_block // chain

    def fill(block, _):
        cols = at_rows(block * rows, rows)
        first, second = own_ref[block, HEAD_DIM:, :], other_ref[block]
        key_rows = jnp.where(core == 0, first, second).astype(jnp.float32)
        queries[:, cols] = own_ref[block, :HEAD_DIM, :]
        values[:HEAD_DIM, cols] = jnp.where(core == 0, second, first)
        values[HEAD_DIM:, cols] = jnp.ones((16, rows), jnp.bfloat16)
        keys[cols, :] = (key_rows * HEAD_DIM ** (-0.5)).T.astype(jnp.bfloat16)
        return 0

    lax.fori_loop(0, blocks, fill, 0)
    keys[seq_len:, :] = jnp.zeros((rows, HEAD_DIM), jnp.bfloat16)
    values[:, seq_len:] = jnp.zeros((HEAD_DIM + 16, rows), jnp.bfloat16)

    def diagonal_step(index, _):
        firsts = [pl.multiple_of((index * chains + part) * chain, chain) for part in range(chains)]
        spans = [pl.ds(first, chain + rows) for first in firsts]
        scores = [
            dot_f32(keys[span, :], queries[:, pl.ds(first, chain)], 1, 0)
            for first, span in zip(firsts, spans)
        ]
        for first, span, score in zip(firsts, spans, scores):
            here = pl.ds(first, chain)
            key_pos = first + lax.broadcasted_iota(jnp.int32, score.shape, 0)
            score = jnp.where(key_pos <= limit_ref[:, here], score, NEG)
            most = jnp.max(score, 0, keepdims=True)
            highest[:, here] = most
            total[:, here] = dot_f32(
                values[:, span], jnp.exp(score - most).astype(jnp.bfloat16), 1, 0
            )
        return 0

    lax.fori_loop(0, seq_len // query_block, diagonal_step, 0)

    def earlier_keys(span, firsts):
        terms, over = [], []
        for first in firsts:
            here = pl.ds(first, chain)
            score = dot_f32(keys[span, :], queries[:, here], 1, 0)
            most = highest[:, here]
            over.append(jnp.max(score, 0, keepdims=True) - most)
            weights = jnp.exp(score - most).astype(jnp.bfloat16)
            terms.append(dot_f32(values[:, span], weights, 1, 0))
        most_over = jnp.max(functools.reduce(jnp.maximum, over))

        @pl.when(most_over <= RAISE_AT)
        def _():
            for first, term in zip(firsts, terms):
                total[:, pl.ds(first, chain)] += term

        @pl.when(most_over > RAISE_AT)
        def _():
            for first in firsts:
                here = pl.ds(first, chain)
                score = dot_f32(keys[span, :], queries[:, here], 1, 0)
                before = highest[:, here]
                after_all = jnp.maximum(before, jnp.max(score, 0, keepdims=True))
                weights = jnp.exp(score - after_all).astype(jnp.bfloat16)
                highest[:, here] = after_all
                total[:, here] = total[:, here] * jnp.exp(before - after_all) + dot_f32(
                    values[:, span], weights, 1, 0
                )

    def query_step(index, _):
        first = index * query_block
        firsts = [pl.multiple_of(first + part * chain, chain) for part in range(chains)]

        def full_step(step, _):
            earlier_keys(at_rows(step * key_block, key_block), firsts)
            return 0

        lax.fori_loop(0, first // key_block, full_step, 0)
        for part in range(1, chains):
            earlier_keys(pl.ds(firsts[part - 1], chain), firsts[part:])
        for piece in range(query_block // rows):
            here = at_rows(first + piece * rows, rows)
            row_sum = total[HEAD_DIM : HEAD_DIM + 1, here]
            result = total[:HEAD_DIM, here] / row_sum
            block = index * (query_block // rows) + piece
            out_ref[block] = result.astype(jnp.bfloat16)
            out_f_ref[block] = result
            log_ref[:, here] = highest[:, here] + jnp.log(row_sum)
        return 0

    lax.fori_loop(0, seq_len // query_block, query_step, 0)


def attend(core, own, other, limit):
    blocks, _, rows = own.shape
    seq_len = blocks * rows
    query_block = math.gcd(seq_len, 2048)
    key_block = math.gcd(query_block, 2048)
    block_shape = (blocks, HEAD_DIM, rows)
    return pl.pallas_call(
        functools.partial(
            attend_kernel,
            query_block=query_block,
            key_block=key_block,
            chain=math.gcd(query_block, 512),
        ),
        out_shape=(
            jax.ShapeDtypeStruct(block_shape, jnp.bfloat16),
            jax.ShapeDtypeStruct(block_shape, jnp.float32),
            jax.ShapeDtypeStruct((1, seq_len), jnp.float32),
        ),
        in_specs=[pl.BlockSpec(memory_space=pltpu.SMEM)] + [whole_vmem()] * 3,
        out_specs=(whole_vmem(),) * 3,
        scratch_shapes=[
            pltpu.VMEM((seq_len + rows, HEAD_DIM), jnp.bfloat16),
            pltpu.VMEM((HEAD_DIM, seq_len), jnp.bfloat16),
            pltpu.VMEM((HEAD_DIM + 16, seq_len + rows), jnp.bfloat16),
            pltpu.VMEM((1, seq_len), jnp.float32),
            pltpu.VMEM((HEAD_DIM + 16, seq_len), jnp.float32),
        ],
        cost_estimate=pl.CostEstimate(
            flops=seq_len * seq_len * 512, bytes_accessed=8 * MIB, transcendentals=0
        ),
        compiler_params=pltpu.CompilerParams(vmem_limit_bytes=56 * MIB),
        name="attend",
    )(core, own, other, limit)


def split_three(values):
    high = values.astype(jnp.bfloat16).astype(jnp.float32)
    middle = (values - high).astype(jnp.bfloat16).astype(jnp.float32)
    return high, middle, values - high - middle


def three_parts(values):
    high, middle, low = split_three(values)
    row = lax.broadcasted_iota(jnp.int32, (16, values.shape[1]), 0)
    return jnp.where(
        row == 0, high, jnp.where(row == 1, middle, jnp.where(row == 2, low, 0.0))
    )


def attend_back_kernel(
    tp_ref, own_ref, other_ref, limit_ref, out_f_ref, log_ref, grad_ref,
    grad_q_ref, keep_ref, send_ref,
    queries, queries_t, keys_t, values_t, grads, grads_t, grad_k, grad_v, grad_q,
    *, query_block, key_block, chain
):
    core = tp_ref[0]
    blocks, _, rows = own_ref.shape
    seq_len = blocks * rows
    chains = query_block // chain

    def fill(block, _):
        cols = at_rows(block * rows, rows)
        first, second = own_ref[block, HEAD_DIM:, :], other_ref[block]
        key_rows = jnp.where(core == 0, first, second).astype(jnp.float32)
        key_rows = key_rows * HEAD_DIM ** (-0.5)
        query, grad = own_ref[block, :HEAD_DIM, :], grad_ref[block]
        grad_f = grad.astype(jnp.float32)
        delta = jnp.sum(grad_f * out_f_ref[block], 0, keepdims=True)
        ones = jnp.ones((16, rows), jnp.bfloat16)
        query_parts = [query.astype(jnp.float32), three_parts(-log_ref[:, cols])]
        queries[cols, :] = jnp.concatenate(query_parts, 0).T.astype(jnp.bfloat16)
        queries_t[:, cols] = query
        keys_t[:HEAD_DIM, cols] = key_rows.astype(jnp.bfloat16)
        keys_t[HEAD_DIM:, cols] = ones
        values_t[:HEAD_DIM, cols] = jnp.where(core == 0, second, first)
        values_t[HEAD_DIM:, cols] = ones
        grads[cols, :] = jnp.concatenate([grad_f, three_parts(-delta)], 0).T.astype(jnp.bfloat16)
        grads_t[:, cols] = grad
        grad_k[:, cols] = jnp.zeros((HEAD_DIM, rows), jnp.float32)
        grad_v[:, cols] = jnp.zeros((HEAD_DIM, rows), jnp.float32)
        return 0

    lax.fori_loop(0, blocks, fill, 0)

    def tile(query_rows, here, key_cols, key_first):
        probs = jnp.exp(dot_f32(queries[query_rows, :], keys_t[:, key_cols], 1, 0))
        if key_first is not None:
            limit = limit_ref[:, query_rows].astype(jnp.float32)
            limit = jnp.broadcast_to(limit, (8, limit.shape[1])).T[:, :1]
            key_pos = key_first + lax.broadcasted_iota(jnp.int32, probs.shape, 1)
            probs = jnp.where(key_pos.astype(jnp.float32) <= limit, probs, 0.0)
        grad_probs = dot_f32(grads[query_rows, :], values_t[:, key_cols], 1, 0)
        grad_scores = (probs * grad_probs).astype(jnp.bfloat16)
        grad_v[:, key_cols] += dot_f32(grads_t[:, query_rows], probs.astype(jnp.bfloat16), 1, 0)
        grad_k[:, key_cols] += dot_f32(queries_t[:, query_rows], grad_scores, 1, 0)
        grad_q[:, here] += dot_f32(keys_t[:HEAD_DIM, key_cols], grad_scores, 1, 1)

    def query_step(index, _):
        first = index * query_block
        grad_q[...] = jnp.zeros_like(grad_q)

        def full_step(step, _):
            tile(
                at_rows(first, query_block),
                slice(0, query_block),
                at_rows(step * key_block, key_block),
                None,
            )
            return 0

        lax.fori_loop(0, first // key_block, full_step, 0)
        for low in range(0, query_block, chain):
            here = pl.multiple_of(first + low, chain)
            if low:
                tile(
                    pl.ds(here, query_block - low),
                    slice(low, query_block),
                    pl.ds(pl.multiple_of(here - chain, chain), chain),
                    None,
                )
            tile(pl.ds(here, chain), slice(low, low + chain), pl.ds(here, chain), here)
            tile(
                at_rows(here + chain - rows, rows),
                slice(low + chain - rows, low + chain),
                at_rows(jnp.minimum(here + chain, seq_len - rows), rows),
                here + chain,
            )
        for piece in range(query_block // rows):
            here = grad_q[:, piece * rows : (piece + 1) * rows]
            grad_q_ref[index * (query_block // rows) + piece] = here.astype(jnp.bfloat16)
        return 0

    lax.fori_loop(0, seq_len // query_block, query_step, 0)

    def finish(block, _):
        cols = at_rows(block * rows, rows)
        key_part = grad_k[:, cols] * HEAD_DIM ** (-0.5)
        value_part = grad_v[:, cols]
        keep_ref[block] = jnp.where(core == 0, key_part, value_part)
        send_ref[block] = jnp.where(core == 0, value_part, key_part).astype(jnp.bfloat16)
        return 0

    lax.fori_loop(0, blocks, finish, 0)


def attend_back(core, own, other, limit, out_f, log_total, grad):
    blocks, _, rows = own.shape
    seq_len = blocks * rows
    query_block = math.gcd(seq_len, 2048)
    key_block = math.gcd(query_block, 1024)
    block_shape = (blocks, HEAD_DIM, rows)
    wide = HEAD_DIM + 16
    return pl.pallas_call(
        functools.partial(
            attend_back_kernel,
            query_block=query_block,
            key_block=key_block,
            chain=math.gcd(query_block, 512),
        ),
        out_shape=(
            jax.ShapeDtypeStruct(block_shape, jnp.bfloat16),
            jax.ShapeDtypeStruct(block_shape, jnp.float32),
            jax.ShapeDtypeStruct(block_shape, jnp.bfloat16),
        ),
        in_specs=[pl.BlockSpec(memory_space=pltpu.SMEM)] + [whole_vmem()] * 6,
        out_specs=(whole_vmem(),) * 3,
        scratch_shapes=[
            pltpu.VMEM((seq_len, wide), jnp.bfloat16),
            pltpu.VMEM((HEAD_DIM, seq_len), jnp.bfloat16),
            pltpu.VMEM((wide, seq_len), jnp.bfloat16),
            pltpu.VMEM((wide, seq_len), jnp.bfloat16),
            pltpu.VMEM((seq_len, wide), jnp.bfloat16),
            pltpu.VMEM((HEAD_DIM, seq_len), jnp.bfloat16),
            pltpu.VMEM((HEAD_DIM, seq_len), jnp.float32),
            pltpu.VMEM((HEAD_DIM, seq_len), jnp.float32),
            pltpu.VMEM((HEAD_DIM, query_block), jnp.float32),
        ],
        cost_estimate=pl.CostEstimate(
            flops=seq_len * seq_len * 1024, bytes_accessed=12 * MIB, transcendentals=0
        ),
        compiler_params=pltpu.CompilerParams(vmem_limit_bytes=60 * MIB),
        name="attend_back",
    )(core, own, other, limit, out_f, log_total, grad)


def project_kernel(*refs, count):
    place_ref, x_ref, cosine_ref, sine_ref = refs[:4]
    mine_refs, other_refs = refs[4 : 4 + count], refs[4 + count : 4 + 2 * count]
    normed_ref, sent_ref, heads_ref, small_ref = refs[4 + 2 * count :]
    core, level, spot = place_ref[0], place_ref[1], place_ref[2]
    micro_count, rows, width = x_ref.shape
    columns, shard, _ = mine_refs[0].shape
    half_cols = heads_ref.shape[2]
    half_dim = HEAD_DIM // 2
    units = half_cols // (2 * HEAD_DIM)
    kv_heads = units // 2
    for step in range(count):
        for up in range(columns):
            here = at_rows(((level ^ up) * count + (spot ^ step)) * shard, shard)
            heads_ref[core, here, :] = mine_refs[step][up, :, :half_cols]
            heads_ref[1 - core, here, :] = other_refs[step][up, :, :half_cols]
            small_ref[here, :] = mine_refs[step][up, :, half_cols:]
    cosine, sine = cosine_ref[...], sine_ref[...]
    gain_row = small_ref.shape[1] // 2
    gain = small_ref[...].astype(jnp.float32).T[gain_row : gain_row + 1]

    def rotated(heads):
        first, second = heads[:half_dim], heads[half_dim:]
        return jnp.concatenate(
            [first * cosine - second * sine, second * cosine + first * sine], 0
        ).astype(jnp.bfloat16)

    for micro in range(micro_count):
        x = x_ref[micro].astype(jnp.float32)
        scale = lax.rsqrt(jnp.mean(x * x, -1, keepdims=True) + EPS)
        normed = (x * scale * gain).astype(jnp.bfloat16)
        normed_ref[micro * rows : (micro + 1) * rows, :] = normed
        for part in range(2):
            heads = dot_f32(normed, heads_ref[part], 1, 0).T
            for unit in range(units):
                first = unit * HEAD_DIM
                paired = (units + unit // 2 + unit % 2 * kv_heads) * HEAD_DIM
                block = (micro * 2 + part) * units + unit
                second = heads[paired : paired + HEAD_DIM]
                sent_ref[block, :HEAD_DIM, :] = rotated(heads[first : first + HEAD_DIM])
                sent_ref[block, HEAD_DIM:, :] = (
                    rotated(second) if unit % 2 == 0 else second.astype(jnp.bfloat16)
                )


def project(place, x, cosine, sine, mine, other, devices):
    micro_count, rows, width = x.shape
    half_cols = mine[0].shape[2] - LANES
    return pl.pallas_call(
        functools.partial(project_kernel, count=len(mine)),
        out_shape=(
            jax.ShapeDtypeStruct((micro_count * rows, width), jnp.bfloat16),
            jax.ShapeDtypeStruct((devices, 2 * HEAD_DIM, rows), jnp.bfloat16),
            jax.ShapeDtypeStruct((2, width, half_cols), jnp.bfloat16),
            jax.ShapeDtypeStruct((width, LANES), jnp.bfloat16),
        ),
        in_specs=[pl.BlockSpec(memory_space=pltpu.SMEM)]
        + [whole_vmem()] * (3 + len(mine) + len(other)),
        out_specs=(whole_vmem(),) * 4,
        compiler_params=pltpu.CompilerParams(vmem_limit_bytes=48 * MIB),
        name="project",
    )(place, x, cosine, sine, *mine, *other)


def project_back_kernel(
    tp_ref, grad_ref, heads_ref, normed_ref, x_ref, grad_resid_ref, gain_ref, cosine_ref,
    sine_ref, grad_x_ref, kept_ref, given_ref, grad_rows
):
    core = tp_ref[0]
    micro_count, rows, width = x_ref.shape
    half_cols = heads_ref.shape[2]
    half_dim = HEAD_DIM // 2
    units = half_cols // (2 * HEAD_DIM)
    cosine, sine = cosine_ref[...], sine_ref[...]

    def turned_back(heads):
        first, second = heads[:half_dim].astype(jnp.float32), heads[half_dim:].astype(jnp.float32)
        return [first * cosine + second * sine, second * cosine - first * sine]

    for micro in range(micro_count):
        for part in range(2):
            first_block = (micro * 2 + part) * units
            pieces = []
            for block in range(first_block, first_block + units):
                pieces += turned_back(grad_ref[block, :HEAD_DIM, :])
            for block in range(first_block, first_block + units, 2):
                pieces += turned_back(grad_ref[block, HEAD_DIM:, :])
            for block in range(first_block + 1, first_block + units, 2):
                pieces.append(grad_ref[block, HEAD_DIM:, :].astype(jnp.float32))
            grad_rows[part, micro * rows : (micro + 1) * rows, :] = (
                jnp.concatenate(pieces, 0).T.astype(jnp.bfloat16)
            )
    gain = gain_ref[...]
    grad_gain = jnp.zeros((1, width), jnp.float32)
    for micro in range(micro_count):
        here = slice(micro * rows, (micro + 1) * rows)
        grad_normed = dot_f32(grad_rows[0, here, :], heads_ref[0], 1, 1) + dot_f32(
            grad_rows[1, here, :], heads_ref[1], 1, 1
        )
        x = x_ref[micro].astype(jnp.float32)
        scale = lax.rsqrt(jnp.mean(x * x, -1, keepdims=True) + EPS)
        gained = grad_normed * gain
        grad_gain = grad_gain + jnp.sum(grad_normed * x * scale, 0, keepdims=True)
        grad_x_ref[micro] = (
            grad_resid_ref[here, :]
            + scale * gained
            - x * scale**3 * jnp.mean(x * gained, -1, keepdims=True)
        )
    normed_t = normed_ref[...].T
    gain_cols = jnp.broadcast_to(grad_gain, (LANES, width)).T.astype(jnp.bfloat16)
    for ref, part in ((kept_ref, core), (given_ref, 1 - core)):
        ref[:, :half_cols] = dot_f32(normed_t, grad_rows[part], 1, 0).astype(jnp.bfloat16)
        ref[:, half_cols:] = gain_cols


def project_back(core, grad_own, heads, normed, x, grad_resid, gain, cosine, sine):
    micro_count, rows, width = x.shape
    half_cols = heads.shape[2]
    share = jax.ShapeDtypeStruct((width, half_cols + LANES), jnp.bfloat16)
    return pl.pallas_call(
        project_back_kernel,
        out_shape=(jax.ShapeDtypeStruct(x.shape, jnp.float32), share, share),
        in_specs=[pl.BlockSpec(memory_space=pltpu.SMEM)] + [whole_vmem()] * 8,
        out_specs=(whole_vmem(),) * 3,
        scratch_shapes=[pltpu.VMEM((2, micro_count * rows, half_cols), jnp.bfloat16)],
        compiler_params=pltpu.CompilerParams(vmem_limit_bytes=56 * MIB),
        name="project_back",
    )(core, grad_own, heads, normed, x, grad_resid, gain, cosine, sine)


def experts_kernel(*refs, slots, first_call, pieces, piece_count, spread):
    place_ref, refs = refs[0], refs[1:]
    x_refs, dy_refs = refs[:slots], refs[slots : 2 * slots]
    w_route_ref, weight_refs = refs[2 * slots], refs[2 * slots + 1 : 2 * slots + 1 + piece_count]
    refs = refs[2 * slots + 1 + piece_count :]
    if not first_call:
        before_refs, refs = refs[:3], refs[3:]
    mix_ref, grad_x_refs, refs = refs[0], refs[1 : 1 + slots], refs[1 + slots :]
    keep_ref, send_in_ref, send_out_ref = refs[:3]
    (
        x_all, x_t, dy_all, dy_t, gates, grad_gates, mix_sum, grad_x_sum, grad_w, weights, sems,
        hidden, grad_gate_pre, grad_up_pre,
    ) = refs[3:]
    expert, expert_count = pl.program_id(0), pl.num_programs(0)
    rows, width = x_refs[0].shape
    total = slots * rows
    half = width // 2
    core = place_ref[0]

    def moves(index):
        copies = []
        for number, (array, whose, first, last) in enumerate(pieces[index]):
            target = weights.at[index % 2, pl.ds(first, last - first)]
            if whose is not None:
                part = core if whose == 0 else 1 - core
                target = weights.at[
                    index % 2, pl.ds(first, last - first), pl.ds(pl.multiple_of(part * half, half), half)
                ]
            copies.append(
                pltpu.make_async_copy(weight_refs[array], target, sems.at[index, number])
            )
        return copies

    @pl.when(expert == 0)
    def _():
        for copy in moves(0) + moves(1):
            copy.start()
        for slot in range(slots):
            here = slice(slot * rows, (slot + 1) * rows)
            x, dy = x_refs[slot][...], dy_refs[slot][:, :width]
            x_all[here, :] = x
            x_t[:, here] = x.T
            dy_all[here, :] = dy
            dy_t[:, here] = dy.T
            chosen = dy_refs[slot][:, width:].astype(jnp.float32)
            logits = jnp.where(chosen > 0.0, dot_f32(x, w_route_ref[...], 1, 0), NEG)
            raised = jnp.exp(logits - jnp.max(logits, 1, keepdims=True)) * chosen
            gates[here, :] = raised / jnp.sum(raised, 1, keepdims=True)
        grad_gates[...] = jnp.zeros_like(grad_gates)
        mix_sum[...] = jnp.zeros_like(mix_sum)
        grad_x_sum[...] = jnp.zeros_like(grad_x_sum)

    for index in range(len(pieces)):

        @pl.when(expert == index)
        def _():
            if 1 <= index < len(pieces) - 1:
                for copy in moves(index + 1):
                    copy.start()
            for copy in moves(index):
                copy.wait()

    if first_call:
        grad_w[...] = jnp.zeros_like(grad_w)
    else:
        keep_before, in_before, out_before = before_refs
        grad_w[core] = keep_before[0].astype(jnp.float32)
        grad_w[1 - core, :2] = in_before[0].astype(jnp.float32)
        grad_w[1 - core, 2:] = out_before[0].astype(jnp.float32)
    buffer = lax.rem(expert, 2)
    w_gate, w_up, w_down_t = weights[buffer, 0], weights[buffer, 1], weights[buffer, 2]
    lane = lax.broadcasted_iota(jnp.int32, (total, LANES), 1)
    gate = jnp.sum(jnp.where(lane == place_ref[1 + expert], gates[...], 0.0), 1, keepdims=True)
    gate_row = jnp.broadcast_to(gate, (total, LANES)).T[:1]
    x = x_all[...]
    dy = dy_all[...].astype(jnp.float32)
    gate_pre = dot_f32(x, w_gate, 1, 0)
    up_pre = dot_f32(x, w_up, 1, 0)
    sigmoid_val = 0.5 + 0.5 * jnp.tanh(0.5 * gate_pre)
    silu_val = gate_pre * sigmoid_val
    up_slope = up_pre * (sigmoid_val * (1.0 + gate_pre * (1.0 - sigmoid_val)))
    hidden[...] = (silu_val * up_pre).astype(jnp.bfloat16)
    grad_hidden = dot_f32((gate * dy).astype(jnp.bfloat16), w_down_t, 1, 0)
    grad_gate_pre[...] = (grad_hidden * up_slope).astype(jnp.bfloat16)
    grad_up_pre[...] = (grad_hidden * silu_val).astype(jnp.bfloat16)
    out = dot_f32(hidden[...], w_down_t, 1, 1).astype(jnp.bfloat16).astype(jnp.float32)
    grad_gate = jnp.sum(out * dy, 1, keepdims=True)
    grad_gates[pl.ds(expert, 1), :] = jnp.broadcast_to(grad_gate, (total, LANES)).T[:1]
    mix_sum[...] += gate * out
    grad_copy = dot_f32(grad_gate_pre[...], w_gate, 1, 1) + dot_f32(
        grad_up_pre[...], w_up, 1, 1
    )
    grad_x_sum[...] += grad_copy.astype(jnp.bfloat16).astype(jnp.float32)
    grad_out_t = (dy_t[...].astype(jnp.float32) * gate_row).astype(jnp.bfloat16)
    terms = (
        dot_f32(x_t[...], grad_gate_pre[...], 1, 0),
        dot_f32(x_t[...], grad_up_pre[...], 1, 0),
        dot_f32(grad_out_t, hidden[...], 1, 0),
    )
    for part in range(2):
        for matrix, term in enumerate(terms):
            grad_w[part, matrix] += term[part * half : (part + 1) * half]
    keep_ref[0] = grad_w[core].astype(jnp.bfloat16)
    send_in_ref[0] = grad_w[1 - core, :2].astype(jnp.bfloat16)
    send_out_ref[0] = grad_w[1 - core, 2:].astype(jnp.bfloat16)

    @pl.when(expert == expert_count - 1)
    def _():
        for slot in range(slots):
            here = slice(slot * rows, (slot + 1) * rows)
            block = (place_ref[place_ref.shape[0] - 1] ^ (slot + 1)) if spread else slot
            mix_ref[block] = mix_sum[here, :].astype(jnp.bfloat16)
            grad_x_refs[slot][:, :width] = grad_x_sum[here, :].astype(jnp.bfloat16)
            parts = split_three(grad_gates[:, here])
            rest = jnp.zeros((LANES - 3 * parts[0].shape[0], rows), jnp.float32)
            grad_x_refs[slot][:, width:] = (
                jnp.concatenate([*parts, rest], 0).T.astype(jnp.bfloat16)
            )
        if spread:
            own_block = place_ref[place_ref.shape[0] - 1]
            mix_ref[own_block] = jnp.zeros((rows, width), jnp.bfloat16)


def experts(place, x_parts, dy_parts, w_route, weights, pieces, before, spread):
    rows = dy_parts[0][0].shape[1]
    width, hidden_width = x_parts[0][0].shape[1], weights[0].shape[-1]
    count, slots = len(pieces), len(x_parts)
    total = slots * rows
    half = width // 2
    mix_slots = slots + 1 if spread else slots
    first_call = before is None
    before = () if first_call else tuple(before)

    def at_block(shape, index):
        return pl.BlockSpec(
            shape,
            lambda expert: (index,) + (0,) * (len(shape) - 1),
            pipeline_mode=pl.Buffered(1),
        )

    row_spec = pl.BlockSpec((rows, width + LANES), lambda expert: (0, 0))
    grad_specs = [
        pl.BlockSpec((1, size, half, hidden_width), lambda expert: (expert, 0, 0, 0))
        for size in (3, 2, 1)
    ]
    grad_shapes = tuple(
        jax.ShapeDtypeStruct((count, size, half, hidden_width), jnp.bfloat16) for size in (3, 2, 1)
    )
    row_shape = jax.ShapeDtypeStruct((rows, width + LANES), jnp.bfloat16)
    outs = pl.pallas_call(
        functools.partial(
            experts_kernel,
            slots=slots,
            first_call=first_call,
            pieces=pieces,
            piece_count=len(weights),
            spread=spread,
        ),
        grid=(count,),
        out_shape=(jax.ShapeDtypeStruct((mix_slots, rows, width), jnp.bfloat16),)
        + (row_shape,) * slots
        + grad_shapes,
        in_specs=[pl.BlockSpec(memory_space=pltpu.SMEM)]
        + [at_block((rows, width), index) for _, index in x_parts]
        + [at_block((None, rows, width + LANES), index) for _, index in dy_parts]
        + [at_block((width, LANES), 0)]
        + [pl.BlockSpec(memory_space=pl.ANY)] * len(weights)
        + grad_specs[: len(before)],
        out_specs=(pl.BlockSpec((mix_slots, rows, width), lambda expert: (0, 0, 0)),)
        + (row_spec,) * slots
        + tuple(grad_specs),
        scratch_shapes=[
            pltpu.VMEM((total, width), jnp.bfloat16),
            pltpu.VMEM((width, total), jnp.bfloat16),
            pltpu.VMEM((total, width), jnp.bfloat16),
            pltpu.VMEM((width, total), jnp.bfloat16),
            pltpu.VMEM((total, LANES), jnp.float32),
            pltpu.VMEM((8, total), jnp.float32),
            pltpu.VMEM((total, width), jnp.float32),
            pltpu.VMEM((total, width), jnp.float32),
            pltpu.VMEM((2, 3, half, hidden_width), jnp.float32),
            pltpu.VMEM((2, 3, width, hidden_width), jnp.bfloat16),
            pltpu.SemaphoreType.DMA((count, max(len(group) for group in pieces))),
        ]
        + [pltpu.VMEM((total, hidden_width), jnp.bfloat16)] * 3,
        cost_estimate=pl.CostEstimate(
            flops=count * total * width * hidden_width * 18,
            bytes_accessed=count * width * hidden_width * 12,
            transcendentals=0,
        ),
        compiler_params=pltpu.CompilerParams(
            vmem_limit_bytes=62 * MIB, dimension_semantics=("arbitrary",)
        ),
        name="experts",
    )(
        place,
        *[array for array, _ in (*x_parts, *dy_parts)],
        w_route,
        *weights,
        *before,
    )
    return outs[0], outs[1 : 1 + slots], outs[1 + slots :]


def together(*values):
    return lax.optimization_barrier(values)


def flip(values, bits):
    count = lax.axis_size("ep")
    return lax.ppermute(values, "ep", [(index, index ^ bits) for index in range(count)])


def swap_cores(values):
    return lax.ppermute(values, "tp", [(0, 1), (1, 0)])


def every_device(values):
    return lax.all_to_all(values, ("ep", "tp"), 0, 0, tiled=True)


def head_tables(first_pos, rows):
    positions = first_pos + jnp.arange(rows, dtype=jnp.int32)
    halves = jnp.arange(HEAD_DIM // 2, dtype=jnp.float32)
    freqs = THETA ** (-2.0 * halves / HEAD_DIM)
    angles = freqs[:, None] * positions.astype(jnp.float32)[None, :]
    return jnp.cos(angles), jnp.sin(angles)


def paired_layout(ep_count, tp_count, micro_count, slice_rows, width, q_cols, kv_cols, experts_here):
    group = q_cols // kv_cols
    kv_heads = kv_cols * tp_count // HEAD_DIM
    return (
        tp_count == 2
        and group == 2
        and ep_count == micro_count * kv_heads
        and ep_count == PLANE * PLANE
        and experts_here == 1
        and slice_rows >= PIECE
        and slice_rows % PIECE == 0
        and width % (2 * LANES) == 0
    )


def on_device_paired(
    tokens,
    gain_attn,
    w_query,
    w_key,
    w_value,
    w_output,
    gain_moe,
    w_router,
    w_gate,
    w_up,
    w_down,
    routes,
    piece_starts,
    cotangent,
):
    ep_count = lax.axis_size("ep")
    tp_count = lax.axis_size("tp")
    ep_index, tp_index = lax.axis_index("ep"), lax.axis_index("tp")
    micro_count, rows, width = tokens.shape
    devices = ep_count * tp_count
    seq_len = rows * devices
    all_rows = micro_count * rows
    shard = gain_attn.shape[0]
    q_cols, kv_cols = w_query.shape[1], w_key.shape[1]
    kv_here = kv_cols // HEAD_DIM
    half_cols = q_cols + 2 * kv_cols
    out_cols = w_output.shape[0]
    columns = ep_count // PLANE
    experts_all = ep_count
    core = tp_index.astype(jnp.int32).reshape(1)

    level, spot = ep_index // PLANE, ep_index % PLANE
    half = width // 2
    micros = range(micro_count)

    small = jnp.concatenate([w_router, jnp.zeros((shard, LANES - experts_all), w_router.dtype)], 1)
    lanes = jnp.arange(LANES, dtype=jnp.int32)
    small = jnp.where(lanes == LANES // 2, gain_attn[:, None], small)
    small = jnp.where(lanes == LANES // 2 + 1, gain_moe[:, None], small)
    packed = jnp.concatenate([w_query, w_key, w_value, small], 1)
    levels = [packed] + [flip(packed, PLANE * step) for step in range(1, columns)]
    mine = jnp.stack(levels)
    mine = [mine] + [flip(mine, step) for step in range(1, PLANE)]

    w_down_t = w_down[0].T
    first_half = tp_index * half
    expert_half = jnp.stack(
        [
            lax.dynamic_slice_in_dim(whole, first_half, half, 0)
            for whole in (w_gate[0], w_up[0], w_down_t)
        ]
    )
    expert_half, levels = together(expert_half, levels)
    far_out = flip(expert_half[2:], 2 * PLANE)
    near_out = flip(expert_half[2:], PLANE)
    mine, far_out, near_out = together(mine, far_out, near_out)
    other = [swap_cores(part) for part in mine]

    x_rows = tokens.reshape(all_rows, width).astype(jnp.float32)
    device_index = ep_index * tp_count + tp_index
    cosine, sine = head_tables(device_index * rows, rows)
    spot_here = jnp.stack([tp_index, level, spot]).astype(jnp.int32)
    normed, sent, w_heads, small_all = project(
        spot_here, tokens, cosine, sine, mine, other, devices
    )
    w_route_full = small_all[:, :experts_all]
    gain_one = small_all[:, LANES // 2].astype(jnp.float32)
    gain_two = small_all[:, LANES // 2 + 1].astype(jnp.float32)
    nearfar_out = flip(far_out, PLANE)
    sent, nearfar_out = together(sent, nearfar_out)
    own = every_device(sent)
    other = swap_cores(own[:, HEAD_DIM:, :])

    chosen = jnp.any(routes[:, :, :, None] == lanes, 2).astype(jnp.bfloat16)
    own_dy = jnp.concatenate([cotangent, chosen], 2)
    w_output_t, expert_late, far_out, dy_late, other = together(
        w_output.T, expert_half, far_out, own_dy, other
    )
    far_in = flip(expert_late[:2], 2 * PLANE)
    near_in = flip(expert_late[:2], PLANE)
    plane_dy = [flip(dy_late, step) for step in range(1, PLANE)]
    gathered_out = lax.all_gather(w_output_t, ("ep", "tp"), axis=0, tiled=False)

    micro_here = ep_index // (ep_count // micro_count)
    starts = lax.dynamic_index_in_dim(piece_starts, micro_here, 0, keepdims=False)
    all_pos = jnp.arange(seq_len, dtype=jnp.int32)[None, :]
    inside = (all_pos >= starts[:, None]) & (all_pos < starts[:, None] + PIECE)
    piece_last = jnp.max(jnp.where(inside, starts[:, None] + (PIECE - 1), -1), 0, keepdims=True)
    limit = jnp.maximum(all_pos, piece_last).astype(jnp.int32)
    out_b, out_f, log_total = attend(core, own, other, limit)
    out_b, near_in, far_in, plane_dy = together(out_b, near_in, far_in, plane_dy)
    nearfar_in = flip(far_in, PLANE)
    attended_t = every_device(out_b).reshape(micro_count, out_cols * tp_count, rows)
    gathered_out = gathered_out.reshape(ep_count, tp_count, shard, out_cols)
    w_out_t = jnp.concatenate(
        [gathered_out[:, part].reshape(width, out_cols) for part in range(2)], 1
    )

    attn_rows = jnp.concatenate(
        [dot_f32(attended_t[micro], w_out_t, 0, 1) for micro in micros], 0
    )
    resid = x_rows + attn_rows
    scale_two = rms_scale(resid)
    normed_two = (resid * scale_two * gain_two).astype(jnp.bfloat16)
    normed_parts = [normed_two[micro * rows : (micro + 1) * rows] for micro in micros]
    plane_x = [[flip(normed_parts[0], step) for step in range(1, PLANE)]]

    weights = [w_gate, w_up, w_down_t[None]]
    nearfar_in, normed_late = together(nearfar_in, normed_two)
    for piece in (near_in, near_out, far_in, far_out, nearfar_in, nearfar_out):
        weights += [piece, swap_cores(piece)]
    pieces = [[(0, None, 0, 1), (1, None, 1, 2), (2, None, 2, 3)]]
    for first in (3, 7, 11):
        pieces.append(
            [(first, 0, 0, 2), (first + 1, 1, 0, 2), (first + 2, 0, 2, 3), (first + 3, 1, 2, 3)]
        )

    logits = jnp.dot(normed_two, w_route_full, preferred_element_type=jnp.float32)
    route_rows = routes.reshape(all_rows, -1)
    expert_ids = jnp.arange(experts_all, dtype=jnp.int32)
    route_hot = (route_rows[:, :, None] == expert_ids[None, None, :]).astype(jnp.float32)
    picked = jnp.sum(route_hot * logits[:, None, :], -1)
    highest = jnp.max(picked, -1, keepdims=True)
    raised = jnp.exp(picked - highest)
    gates = raised / jnp.sum(raised, -1, keepdims=True)

    slot_ids = jnp.stack(
        [
            jnp.stack([(level ^ up) * PLANE + (spot ^ step) for up in range(columns)])
            for step in range(PLANE)
        ]
    )
    slot_hot = (route_rows[None, None, :, :] == slot_ids[:, :, None, None]).astype(jnp.float32)

    spot_here = spot.astype(jnp.int32).reshape(1)
    column_ids = jnp.stack([(level ^ up) * PLANE + spot for up in range(columns)])
    place = jnp.concatenate([core, column_ids.astype(jnp.int32), spot_here])
    own_mix, own_grad_x, before = experts(
        place,
        [(normed_two, micro) for micro in micros],
        [(own_dy, micro) for micro in micros],
        small_all,
        weights,
        pieces,
        None,
        False,
    )
    leaving = normed_parts[1:]
    leaving, own_mix = together(leaving, own_mix)
    plane_x += [[flip(part, step) for step in range(1, PLANE)] for part in leaving]
    plane_groups = [[up * PLANE + step for step in range(PLANE)] for up in range(columns)]
    column_groups = [[up * PLANE + step for up in range(columns)] for step in range(PLANE)]

    def within_plane(parts):
        return lax.all_to_all(parts, "ep", 0, 0, tiled=True, axis_index_groups=plane_groups)

    far_mix, far_grad_x = [], []
    for micro in micros:
        mix, grad_x, before = experts(
            place,
            [(part, 0) for part in plane_x[micro]],
            [(part, micro) for part in plane_dy],
            small_all,
            weights,
            pieces,
            before,
            True,
        )
        if micro:
            grad_x, before, far_grad_x, far_mix = together(grad_x, before, far_grad_x, far_mix)
        far_grad_x.append([flip(grad_x[step - 1], step) for step in range(1, PLANE)])
        if micro < micro_count - 1:
            far_mix.append(within_plane(mix))
    last_mix = mix
    keep_w, send_in_w, send_out_w = before
    given_out = swap_cores(send_out_w)[:, 0]
    out_w = keep_w[:, 2].astype(jnp.float32) + given_out.astype(jnp.float32)
    near_out_w = flip(out_w[1::2].astype(jnp.bfloat16), PLANE)
    far_grad_x[-1], near_out_w = together(far_grad_x[-1], near_out_w)
    near_out_w = near_out_w.astype(jnp.float32)

    def at_home(own_parts, far_parts):
        return jnp.concatenate(
            [
                sum(part.astype(jnp.float32) for part in (own_parts[micro], *far_parts[micro]))
                for micro in micros
            ],
            0,
        )

    grad_out = cotangent.reshape(all_rows, width).astype(jnp.float32)
    home_grad_x = [
        [own_grad_x[micro], *far_grad_x[micro]] for micro in micros
    ]
    slot_grads = jnp.concatenate(
        [
            jnp.stack(
                [
                    sum(
                        part[:, width + low : width + low + columns].astype(jnp.float32)
                        for low in (0, 8, 16)
                    ).T
                    for part in parts
                ]
            )
            for parts in home_grad_x
        ],
        2,
    )
    grad_gates = jnp.sum(slot_hot * slot_grads[:, :, :, None], (0, 1))
    grad_spread = gates * (grad_gates - jnp.sum(gates * grad_gates, -1, keepdims=True))
    grad_logits = jnp.sum(grad_spread[:, :, None] * route_hot, 1).astype(jnp.bfloat16)
    grad_normed_two = jnp.concatenate(
        [sum(part[:, :width].astype(jnp.float32) for part in parts) for parts in home_grad_x], 0
    ) + dot_f32(grad_logits, w_route_full, 1, 1)
    grad_route = dot_f32(normed_late, grad_logits, 0, 0)
    gained_two = grad_normed_two * gain_two
    grad_gain_two = jnp.sum(grad_normed_two * resid * scale_two, 0)
    grad_resid = (
        grad_out
        + scale_two * gained_two
        - resid * scale_two**3 * jnp.mean(resid * gained_two, -1, keepdims=True)
    )
    grad_branch = grad_resid.astype(jnp.bfloat16)
    grad_att = jnp.concatenate(
        [
            dot_f32(w_out_t, grad_branch[micro * rows : (micro + 1) * rows], 0, 1).astype(
                jnp.bfloat16
            )
            for micro in micros
        ],
        0,
    ).reshape(devices, HEAD_DIM, rows)
    grad_outw = sum(
        dot_f32(grad_branch[micro * rows : (micro + 1) * rows], attended_t[micro], 0, 1)
        for micro in micros
    ).astype(jnp.bfloat16)
    grad_heads = every_device(grad_att)
    far_out_w = (out_w[2] + near_out_w[1]).astype(jnp.bfloat16)
    given_in = swap_cores(send_in_w)

    def column_sum(slot):
        kept = keep_w[slot, :2].astype(jnp.float32)
        return (kept + given_in[slot].astype(jnp.float32)).astype(jnp.bfloat16)

    own_w = keep_w[0, :2].astype(jnp.float32) + given_in[0].astype(jnp.float32)
    near_in_w, far_in_w, last_in_w = column_sum(1), column_sum(2), column_sum(3)
    grad_heads, near_in_w, last_in_w, far_in_w, far_out_w, own_w = together(
        grad_heads, near_in_w, last_in_w, far_in_w, far_out_w, own_w
    )
    last_mix = within_plane(last_mix)
    near_in_w = flip(near_in_w, PLANE)
    last_in_w = flip(last_in_w, 3 * PLANE)
    far_in_w = flip(far_in_w, 2 * PLANE)
    far_out_w = flip(far_out_w, 2 * PLANE)

    def to_shards(kept, given):
        core_sum = kept.astype(jnp.float32) + swap_cores(given).astype(jnp.float32)
        shares = lax.all_to_all(
            core_sum.astype(jnp.bfloat16).reshape(ep_count, shard, -1), "ep", 0, 0, tiled=True
        )
        return jnp.sum(shares.astype(jnp.float32), 0)

    def in_lanes(columns_f):
        small = jnp.concatenate(columns_f, 1)
        return jnp.pad(small, ((0, 0), (0, LANES - small.shape[1]))).astype(jnp.bfloat16)

    def own_rows(values):
        return lax.dynamic_slice_in_dim(values, tp_index * (shard // 2), shard // 2, 0)

    late_small = in_lanes([grad_route, grad_gain_two[:, None]])
    out_parts = [
        jnp.concatenate([grad_outw[:, part * out_cols : (part + 1) * out_cols], late_small], 1)
        for part in range(2)
    ]
    out_kept = jnp.where(tp_index == 0, out_parts[0], out_parts[1])
    out_given = jnp.where(tp_index == 0, out_parts[1], out_parts[0])
    grad_q, keep_kv, send_kv = attend_back(
        core, own, other, limit, out_f, log_total, grad_heads
    )
    grad_q, keep_kv, send_kv, near_in_w, last_in_w, far_in_w, far_out_w, last_mix = together(
        grad_q, keep_kv, send_kv, near_in_w, last_in_w, far_in_w, far_out_w, last_mix
    )
    far_mix.append(last_mix)
    grad_kv = (keep_kv + swap_cores(send_kv).astype(jnp.float32)).astype(jnp.bfloat16)
    sent_back = jnp.concatenate([grad_q, grad_kv], 1)
    grad_own = every_device(sent_back)
    out_sum = out_kept.astype(jnp.float32) + swap_cores(out_given).astype(jnp.float32)
    out_sum = out_sum.astype(jnp.bfloat16).reshape(columns, PLANE, shard, -1)

    def summed(values, axis, place_here, stride):
        own_part = lax.dynamic_index_in_dim(values, place_here, axis, False).astype(jnp.float32)
        return own_part, [
            flip(lax.dynamic_index_in_dim(values, place_here ^ step, axis, False), stride * step)
            for step in range(1, values.shape[axis])
        ]

    out_own, out_far = summed(out_sum, 1, spot, 1)
    out_levels = out_own + sum(part.astype(jnp.float32) for part in out_far)
    out_own, out_far = summed(out_levels.astype(jnp.bfloat16), 0, level, PLANE)
    grad_own, out_far = together(grad_own, out_far)
    out_share = out_own + sum(part.astype(jnp.float32) for part in out_far)
    out_small = own_rows(out_share[:, out_cols:])
    grad_tokens, kept, given = project_back(
        core, grad_own, w_heads, normed, tokens, grad_resid, gain_one[None, :], cosine, sine
    )
    kept, given, near_in_w, last_in_w, far_in_w, far_out_w = together(
        kept, given, near_in_w, last_in_w, far_in_w, far_out_w
    )
    grad_w = [
        own_w[matrix]
        + sum(part[matrix].astype(jnp.float32) for part in (near_in_w, last_in_w, far_in_w))
        for matrix in range(2)
    ]
    grad_w.append(out_w[0] + near_out_w[0] + far_out_w.astype(jnp.float32))
    mixed = (resid + at_home(own_mix, far_mix)).astype(jnp.bfloat16)

    own_share = to_shards(kept, given)
    return (
        mixed.reshape(micro_count, rows, width),
        grad_tokens,
        own_rows(own_share[:, half_cols:])[:, 0],
        own_share[:, :q_cols],
        own_share[:, q_cols : q_cols + kv_cols],
        own_share[:, q_cols + kv_cols : half_cols],
        out_share[:, :out_cols].T,
        out_small[:, experts_all],
        out_small[:, :experts_all],
        grad_w[0][None],
        grad_w[1][None],
        grad_w[2].T[None],
    )


def on_device(*args):
    tokens, w_query, w_key, w_gate = args[0], args[2], args[3], args[8]
    paired = paired_layout(
        lax.axis_size("ep"),
        lax.axis_size("tp"),
        *tokens.shape,
        w_query.shape[1],
        w_key.shape[1],
        w_gate.shape[0],
    )
    return (on_device_paired if paired else on_device_general)(*args)


def solution(mesh):
    in_specs = (
        P(None, ("ep", "tp"), None),
        P("ep"),
        P("ep", "tp"),
        P("ep", "tp"),
        P("ep", "tp"),
        P("tp", "ep"),
        P("ep"),
        P("ep", None),
        P("ep", None, None),
        P("ep", None, None),
        P("ep", None, None),
        P(None, ("ep", "tp"), None),
        P(),
        P(None, ("ep", "tp"), None),
    )
    out_specs = (
        P(None, ("ep", "tp"), None),
        P(None, ("ep", "tp"), None),
        P(("ep", "tp")),
        P("ep", "tp"),
        P("ep", "tp"),
        P("ep", "tp"),
        P("tp", "ep"),
        P(("ep", "tp")),
        P(("ep", "tp"), None),
        P("ep", "tp", None),
        P("ep", "tp", None),
        P("ep", None, "tp"),
    )
    return jax.shard_map(
        on_device, mesh=mesh, in_specs=in_specs, out_specs=out_specs, check_vma=False
    )
```

```python
import functools
import math

import jax
import jax.numpy as jnp
from jax import lax
from jax.experimental import pallas as pl
from jax.experimental.pallas import tpu as pltpu
from jax.sharding import PartitionSpec as P

HEAD_DIM = 64
PIECE = 256
PLANE = 4
LANES = 128
MIB = 1 << 20


EPS = 1e-06
THETA = 10000.0
NEG = -1e30


def rms_scale(values):
    return lax.rsqrt(jnp.mean(values * values, -1, keepdims=True) + EPS)


def angle_tables(positions):
    halves = jnp.arange(HEAD_DIM // 2, dtype=jnp.float32)
    freqs = THETA ** (-2.0 * halves / HEAD_DIM)
    angles = positions.astype(jnp.float32)[:, None] * freqs[None, :]
    return (jnp.cos(angles)[:, None, :], jnp.sin(angles)[:, None, :])


def rotate(values, cosine, sine):
    half_dim = values.shape[-1] // 2
    first_half = values[..., :half_dim]
    second_half = values[..., half_dim:]
    return jnp.concatenate(
        [first_half * cosine - second_half * sine, second_half * cosine + first_half * sine], -1
    )


def piece_index(starts, positions):
    inside = (positions[:, None] >= starts[None, :]) & (
        positions[:, None] < starts[None, :] + PIECE
    )
    numbers = jnp.arange(1, starts.shape[0] + 1, dtype=jnp.int32)
    return jnp.sum(jnp.where(inside, numbers[None, :], 0), -1) - 1


def allowed_mask(query_pos, query_piece, key_pos, key_piece):
    return (key_pos[None, :] <= query_pos[:, None]) | (
        key_piece[None, :] == query_piece[:, None]
    ) & (query_piece[:, None] >= 0)


def to_groups(rows, kv_here, group_size):
    row_total = rows.shape[0]
    return (
        rows.reshape(row_total, kv_here, group_size, HEAD_DIM)
        .transpose(1, 2, 0, 3)
        .reshape(kv_here, group_size * row_total, HEAD_DIM)
    )


def from_groups(grouped, row_total):
    kv_here = grouped.shape[0]
    return (
        grouped.reshape(kv_here, -1, row_total, HEAD_DIM)
        .transpose(2, 0, 1, 3)
        .reshape(row_total, -1)
    )


def tp_major(values, ep_count, tp_count):
    leading = values.shape[0]
    shaped = values.reshape(
        (ep_count, tp_count, leading // (ep_count * tp_count)) + values.shape[1:]
    )
    return jnp.swapaxes(shaped, 0, 1).reshape(values.shape)


def add_all(left_parts, right_parts):
    return tuple((left_part + right_part for left_part, right_part in zip(left_parts, right_parts)))


def reduce_grads(parts, ep_count, tp_count):
    (
        grad_gate_w,
        grad_up_w,
        grad_down_w,
        grad_gain_one,
        grad_gain_two,
        grad_route,
        grad_proj,
        grad_outw,
    ) = parts
    tp_sums = (
        lax.psum_scatter(
            grad_gate_w.astype(jnp.bfloat16), "tp", scatter_dimension=1, tiled=True
        ).astype(jnp.float32),
        lax.psum_scatter(
            grad_up_w.astype(jnp.bfloat16), "tp", scatter_dimension=1, tiled=True
        ).astype(jnp.float32),
        lax.psum_scatter(
            grad_down_w.astype(jnp.bfloat16), "tp", scatter_dimension=2, tiled=True
        ).astype(jnp.float32),
        lax.psum_scatter(
            tp_major(grad_gain_one, ep_count, tp_count).astype(jnp.bfloat16),
            "tp",
            scatter_dimension=0,
            tiled=True,
        ).astype(jnp.float32),
        lax.psum_scatter(
            tp_major(grad_gain_two, ep_count, tp_count).astype(jnp.bfloat16),
            "tp",
            scatter_dimension=0,
            tiled=True,
        ).astype(jnp.float32),
        lax.psum_scatter(
            tp_major(grad_route, ep_count, tp_count).astype(jnp.bfloat16),
            "tp",
            scatter_dimension=0,
            tiled=True,
        ).astype(jnp.float32),
    )
    ep_sums = (
        lax.psum_scatter(
            grad_proj.astype(jnp.bfloat16), "ep", scatter_dimension=0, tiled=True
        ).astype(jnp.float32),
        lax.psum_scatter(
            grad_outw.astype(jnp.bfloat16), "ep", scatter_dimension=1, tiled=True
        ).astype(jnp.float32),
        lax.psum_scatter(
            tp_sums[3].astype(jnp.bfloat16), "ep", scatter_dimension=0, tiled=True
        ).astype(jnp.float32),
        lax.psum_scatter(
            tp_sums[4].astype(jnp.bfloat16), "ep", scatter_dimension=0, tiled=True
        ).astype(jnp.float32),
        lax.psum_scatter(
            tp_sums[5].astype(jnp.bfloat16), "ep", scatter_dimension=0, tiled=True
        ).astype(jnp.float32),
    )
    return (
        tp_sums[0],
        tp_sums[1],
        tp_sums[2],
        ep_sums[2],
        ep_sums[3],
        ep_sums[4],
        ep_sums[0],
        ep_sums[1],
    )


def on_device_general(
    tokens,
    gain_attn,
    w_query,
    w_key,
    w_value,
    w_output,
    gain_moe,
    w_router,
    w_gate,
    w_up,
    w_down,
    routes,
    piece_starts,
    cotangent,
):
    ep_count = lax.axis_size("ep")
    tp_count = lax.axis_size("tp")
    micro_count, slice_rows, width = tokens.shape
    span_rows = slice_rows * tp_count
    seq_len = span_rows * ep_count
    q_cols = w_query.shape[1]
    kv_cols = w_key.shape[1]
    kv_here = kv_cols // HEAD_DIM
    group_size = q_cols // kv_cols
    query_rows = group_size * span_rows
    experts_here = w_gate.shape[0]
    experts_all = experts_here * ep_count
    top_count = routes.shape[2]
    capacity = max(2, slice_rows * top_count * 3 // (2 * experts_all))
    expert_rows = ep_count * capacity
    score_scale = HEAD_DIM ** (-0.5)
    key_block = math.gcd(seq_len, 512)
    block_count = seq_len // key_block
    local_pos = lax.axis_index("ep") * span_rows + jnp.arange(span_rows, dtype=jnp.int32)
    all_pos = jnp.arange(seq_len, dtype=jnp.int32)
    row_pos = jnp.tile(local_pos, group_size)
    cosine, sine = angle_tables(local_pos)
    slot_ids = jnp.arange(experts_all * capacity, dtype=jnp.int32)
    expert_ids = jnp.arange(experts_all, dtype=jnp.int32)
    gathered = (
        lax.all_gather(gain_attn, "ep", axis=0, tiled=True),
        lax.all_gather(w_query, "ep", axis=0, tiled=True),
        lax.all_gather(w_key, "ep", axis=0, tiled=True),
        lax.all_gather(w_value, "ep", axis=0, tiled=True),
        lax.all_gather(w_output, "ep", axis=1, tiled=True),
        lax.all_gather(gain_moe, "ep", axis=0, tiled=True),
        lax.all_gather(w_router, "ep", axis=0, tiled=True),
    )
    gain_one = gathered[0].astype(jnp.float32)
    w_proj = jnp.concatenate([gathered[1], gathered[2], gathered[3]], 1)
    w_out_full = gathered[4]
    gain_two = gathered[5].astype(jnp.float32)
    w_route_full = gathered[6]
    totals = None
    mixed_rows = []
    grad_rows = []
    for micro_index in range(micro_count):
        starts = piece_starts[micro_index]
        key_pieces = piece_index(starts, all_pos)
        row_piece = jnp.tile(piece_index(starts, local_pos), group_size)
        x_rows = tokens[micro_index].astype(jnp.float32)
        scale_one = rms_scale(x_rows)
        normed = (x_rows * scale_one * gain_one).astype(jnp.bfloat16)
        normed_all = lax.all_gather(normed, "tp", axis=0, tiled=True)
        projected = jnp.dot(normed_all, w_proj, preferred_element_type=jnp.float32)
        queries = rotate(
            projected[:, :q_cols].reshape(span_rows, -1, HEAD_DIM), cosine, sine
        ).astype(jnp.bfloat16)
        q_grouped = to_groups(queries.reshape(span_rows, q_cols), kv_here, group_size)
        keys_own = (
            rotate(
                projected[:, q_cols : q_cols + kv_cols].reshape(span_rows, kv_here, HEAD_DIM),
                cosine,
                sine,
            )
            .astype(jnp.bfloat16)
            .reshape(span_rows, kv_cols)
        )
        values_own = projected[:, q_cols + kv_cols :].astype(jnp.bfloat16)
        keys_all, values_all = (
            lax.all_gather(keys_own, "ep", axis=0, tiled=True),
            lax.all_gather(values_own, "ep", axis=0, tiled=True),
        )

        def block_scores(first_row, block_size):
            key_blk = lax.dynamic_slice_in_dim(keys_all, first_row, block_size, 0).reshape(
                block_size, kv_here, HEAD_DIM
            )
            value_blk = lax.dynamic_slice_in_dim(values_all, first_row, block_size, 0).reshape(
                block_size, kv_here, HEAD_DIM
            )
            key_pos = first_row + jnp.arange(block_size, dtype=jnp.int32)
            piece_blk = lax.dynamic_slice_in_dim(key_pieces, first_row, block_size, 0)
            allowed = allowed_mask(row_pos, row_piece, key_pos, piece_blk)[None]
            scores = (
                jnp.einsum("hrd,khd->hrk", q_grouped, key_blk, preferred_element_type=jnp.float32)
                * score_scale
            )
            return (scores, allowed, key_blk, value_blk)

        def forward_step(block_index, running):
            run_max, run_sum, run_acc = running
            scores, allowed, key_blk, value_blk = block_scores(block_index * key_block, key_block)
            scores = jnp.where(allowed, scores, NEG)
            new_max = jnp.maximum(run_max, jnp.max(scores, -1))
            weights = jnp.where(allowed, jnp.exp(scores - new_max[..., None]), 0.0)
            factor = jnp.exp(run_max - new_max)
            run_sum = run_sum * factor + jnp.sum(weights, -1)
            run_acc = run_acc * factor[..., None] + jnp.einsum(
                "hrk,khd->hrd",
                weights.astype(jnp.bfloat16),
                value_blk,
                preferred_element_type=jnp.float32,
            )
            return (new_max, run_sum, run_acc)

        start_state = (
            jnp.full((kv_here, query_rows), NEG, jnp.float32),
            jnp.zeros((kv_here, query_rows), jnp.float32),
            jnp.zeros((kv_here, query_rows, HEAD_DIM), jnp.float32),
        )
        run_max, run_sum, run_acc = lax.fori_loop(0, block_count, forward_step, start_state)
        log_total = run_max + jnp.log(run_sum)
        attended_f = run_acc / run_sum[..., None]
        attended = from_groups(attended_f.astype(jnp.bfloat16), span_rows)
        partial_attn = jnp.dot(attended, w_out_full, preferred_element_type=jnp.float32)
        attn_rows = lax.psum_scatter(
            partial_attn.astype(jnp.bfloat16), "tp", scatter_dimension=0, tiled=True
        ).astype(jnp.float32)
        resid = x_rows + attn_rows
        scale_two = rms_scale(resid)
        normed_two = (resid * scale_two * gain_two).astype(jnp.bfloat16)
        logits = jnp.dot(normed_two, w_route_full, preferred_element_type=jnp.float32)
        route_rows = routes[micro_index]
        route_hot = (route_rows[:, :, None] == expert_ids[None, None, :]).astype(jnp.float32)
        picked = jnp.sum(route_hot * logits[:, None, :], -1)
        highest = jnp.max(picked, -1, keepdims=True)
        raised = jnp.exp(picked - highest)
        gates = raised / jnp.sum(raised, -1, keepdims=True)
        flat_hot = route_hot.reshape(-1, experts_all)
        earlier = jnp.cumsum(flat_hot, 0) - flat_hot
        slot_of = jnp.sum(earlier * flat_hot, -1).astype(jnp.int32)
        target = route_rows.reshape(-1) * capacity + slot_of
        place_pairs = slot_ids[:, None] == target[None, :]
        place_pairs_b = place_pairs.astype(jnp.bfloat16)
        place_tokens = jnp.any(place_pairs.reshape(-1, slice_rows, top_count), -1).astype(
            jnp.bfloat16
        )
        send_rows = (
            jnp.dot(place_tokens, normed_two, preferred_element_type=jnp.float32)
            .astype(jnp.bfloat16)
            .reshape(ep_count, experts_here, capacity, width)
        )
        received = lax.all_to_all(send_rows, "ep", split_axis=0, concat_axis=0, tiled=True)
        expert_in = jnp.swapaxes(received, 0, 1).reshape(experts_here, expert_rows, width)
        gate_pre = jnp.einsum("erd,edf->erf", expert_in, w_gate, preferred_element_type=jnp.float32)
        up_pre = jnp.einsum("erd,edf->erf", expert_in, w_up, preferred_element_type=jnp.float32)
        sigmoid_val = jax.nn.sigmoid(gate_pre)
        silu_val = gate_pre * sigmoid_val
        hidden = (silu_val * up_pre).astype(jnp.bfloat16)
        expert_out = jnp.einsum(
            "erf,efd->erd", hidden, w_down, preferred_element_type=jnp.float32
        ).astype(jnp.bfloat16)
        returned = lax.all_to_all(
            jnp.swapaxes(expert_out.reshape(experts_here, ep_count, capacity, width), 0, 1),
            "ep",
            split_axis=0,
            concat_axis=0,
            tiled=True,
        )
        slot_rows = returned.reshape(-1, width)
        picked_rows = jnp.einsum(
            "sn,sd->nd", place_pairs_b, slot_rows, preferred_element_type=jnp.float32
        ).reshape(slice_rows, top_count, width)
        mixture = jnp.einsum("tk,tkd->td", gates, picked_rows)
        mixed_rows.append((resid + mixture).astype(jnp.bfloat16))
        grad_out = cotangent[micro_index].astype(jnp.float32)
        grad_gates = jnp.einsum("tkd,td->tk", picked_rows, grad_out)
        weighted = (
            (gates[:, :, None] * grad_out[:, None, :]).astype(jnp.bfloat16).reshape(-1, width)
        )
        grad_slots = (
            jnp.dot(place_pairs_b, weighted, preferred_element_type=jnp.float32)
            .astype(jnp.bfloat16)
            .reshape(ep_count, experts_here, capacity, width)
        )
        grad_recv = lax.all_to_all(grad_slots, "ep", split_axis=0, concat_axis=0, tiled=True)
        grad_expert = jnp.swapaxes(grad_recv, 0, 1).reshape(experts_here, expert_rows, width)
        grad_hidden = jnp.einsum(
            "erd,efd->erf", grad_expert, w_down, preferred_element_type=jnp.float32
        )
        grad_down_w = jnp.einsum(
            "erf,erd->efd", hidden, grad_expert, preferred_element_type=jnp.float32
        )
        silu_slope = sigmoid_val * (1.0 + gate_pre * (1.0 - sigmoid_val))
        grad_gate_pre = (grad_hidden * up_pre * silu_slope).astype(jnp.bfloat16)
        grad_up_pre = (grad_hidden * silu_val).astype(jnp.bfloat16)
        grad_gate_w = jnp.einsum(
            "erd,erf->edf", expert_in, grad_gate_pre, preferred_element_type=jnp.float32
        )
        grad_up_w = jnp.einsum(
            "erd,erf->edf", expert_in, grad_up_pre, preferred_element_type=jnp.float32
        )
        grad_copy = (
            jnp.einsum("erf,edf->erd", grad_gate_pre, w_gate, preferred_element_type=jnp.float32)
            + jnp.einsum("erf,edf->erd", grad_up_pre, w_up, preferred_element_type=jnp.float32)
        ).astype(jnp.bfloat16)
        grad_back = lax.all_to_all(
            jnp.swapaxes(grad_copy.reshape(experts_here, ep_count, capacity, width), 0, 1),
            "ep",
            split_axis=0,
            concat_axis=0,
            tiled=True,
        ).reshape(-1, width)
        grad_spread = gates * (grad_gates - jnp.sum(gates * grad_gates, -1, keepdims=True))
        grad_logits = jnp.einsum("tk,tke->te", grad_spread, route_hot).astype(jnp.bfloat16)
        grad_normed_two = jnp.einsum(
            "st,sd->td", place_tokens, grad_back, preferred_element_type=jnp.float32
        ) + jnp.einsum("te,de->td", grad_logits, w_route_full, preferred_element_type=jnp.float32)
        grad_route = jnp.einsum(
            "td,te->de", normed_two, grad_logits, preferred_element_type=jnp.float32
        )
        gained_two = grad_normed_two * gain_two
        grad_gain_two = jnp.sum(grad_normed_two * resid * scale_two, 0)
        grad_resid = (
            grad_out
            + scale_two * gained_two
            - resid * scale_two**3 * jnp.mean(resid * gained_two, -1, keepdims=True)
        )
        grad_attn = lax.all_gather(grad_resid.astype(jnp.bfloat16), "tp", axis=0, tiled=True)
        grad_outw = jnp.einsum("cq,cd->qd", attended, grad_attn, preferred_element_type=jnp.float32)
        grad_att_rows = jnp.einsum(
            "cd,qd->cq", grad_attn, w_out_full, preferred_element_type=jnp.float32
        ).astype(jnp.bfloat16)
        grad_grouped = to_groups(grad_att_rows, kv_here, group_size)
        delta = jnp.sum(grad_grouped.astype(jnp.float32) * attended_f, -1)

        def block_grads(first_row, block_size):
            scores, allowed, key_blk, value_blk = block_scores(first_row, block_size)
            probs = jnp.where(allowed, jnp.exp(scores - log_total[..., None]), 0.0)
            grad_probs = jnp.einsum(
                "hrd,khd->hrk", grad_grouped, value_blk, preferred_element_type=jnp.float32
            )
            grad_scores = (probs * (grad_probs - delta[..., None])).astype(jnp.bfloat16)
            return (probs, grad_scores, key_blk)

        def key_side(first_row, block_size):
            probs, grad_scores, key_blk = block_grads(first_row, block_size)
            grad_keys = (
                jnp.einsum(
                    "hrk,hrd->khd", grad_scores, q_grouped, preferred_element_type=jnp.float32
                ).reshape(block_size, kv_cols)
                * score_scale
            )
            grad_values = jnp.einsum(
                "hrk,hrd->khd",
                probs.astype(jnp.bfloat16),
                grad_grouped,
                preferred_element_type=jnp.float32,
            ).reshape(block_size, kv_cols)
            return (jnp.concatenate([grad_keys, grad_values], 1), grad_scores, key_blk)

        query_zero = jnp.zeros((kv_here, query_rows, HEAD_DIM), jnp.float32)

        def backward_step(block_index, running):
            grad_query, grad_kv = running
            first_row = block_index * key_block
            kv_terms, grad_scores, key_blk = key_side(first_row, key_block)
            grad_query = grad_query + jnp.einsum(
                "hrk,khd->hrd", grad_scores, key_blk, preferred_element_type=jnp.float32
            )
            grad_kv = lax.dynamic_update_slice_in_dim(grad_kv, kv_terms, first_row, 0)
            return (grad_query, grad_kv)

        grad_query, grad_kv = lax.fori_loop(
            0,
            block_count,
            backward_step,
            (query_zero, jnp.zeros((seq_len, 2 * kv_cols), jnp.float32)),
        )
        grad_kv_own = lax.psum_scatter(
            grad_kv.astype(jnp.bfloat16), "ep", scatter_dimension=0, tiled=True
        ).astype(jnp.float32)
        grad_query_rows = from_groups(grad_query * score_scale, span_rows).reshape(
            span_rows, -1, HEAD_DIM
        )
        grad_query_raw = (
            rotate(grad_query_rows, cosine, -sine).astype(jnp.bfloat16).reshape(span_rows, q_cols)
        )
        grad_key_raw = (
            rotate(grad_kv_own[:, :kv_cols].reshape(span_rows, kv_here, HEAD_DIM), cosine, -sine)
            .astype(jnp.bfloat16)
            .reshape(span_rows, kv_cols)
        )
        grad_value_raw = grad_kv_own[:, kv_cols:].astype(jnp.bfloat16)
        grad_proj_rows = jnp.concatenate([grad_query_raw, grad_key_raw, grad_value_raw], 1)
        grad_proj = jnp.einsum(
            "cd,cp->dp", normed_all, grad_proj_rows, preferred_element_type=jnp.float32
        )
        grad_normed_part = jnp.einsum(
            "cp,dp->cd", grad_proj_rows, w_proj, preferred_element_type=jnp.float32
        )
        grad_normed = lax.psum_scatter(
            grad_normed_part.astype(jnp.bfloat16), "tp", scatter_dimension=0, tiled=True
        ).astype(jnp.float32)
        gained_one = grad_normed * gain_one
        grad_gain_one = jnp.sum(grad_normed * x_rows * scale_one, 0)
        grad_rows.append(
            grad_resid
            + scale_one * gained_one
            - x_rows * scale_one**3 * jnp.mean(x_rows * gained_one, -1, keepdims=True)
        )
        parts = (
            grad_gate_w,
            grad_up_w,
            grad_down_w,
            grad_gain_one,
            grad_gain_two,
            grad_route,
            grad_proj,
            grad_outw,
        )
        reduced = reduce_grads(parts, ep_count, tp_count)
        totals = reduced if totals is None else add_all(totals, reduced)
    grad_qkv = totals[6]
    return (
        jnp.stack(mixed_rows),
        jnp.stack(grad_rows),
        totals[3],
        grad_qkv[:, :q_cols],
        grad_qkv[:, q_cols : q_cols + kv_cols],
        grad_qkv[:, q_cols + kv_cols :],
        totals[7],
        totals[4],
        totals[5],
        totals[0],
        totals[1],
        totals[2],
    )


RAISE_AT = 40.0


def dot_f32(left, right, left_dim, right_dim):
    return lax.dot_general(
        left, right, (((left_dim,), (right_dim,)), ((), ())), preferred_element_type=jnp.float32
    )


def at_rows(first_row, count):
    return pl.ds(pl.multiple_of(first_row, count), count)


def whole_vmem():
    return pl.BlockSpec(memory_space=pltpu.VMEM)


def attend_kernel(
    tp_ref, own_ref, other_ref, limit_ref, out_ref, out_f_ref, log_ref,
    keys, queries, values, highest, total,
    *, query_block, key_block, chain
):
    core = tp_ref[0]
    blocks, _, rows = own_ref.shape
    seq_len = blocks * rows
    chains = query_block // chain

    def fill(block, _):
        cols = at_rows(block * rows, rows)
        first, second = own_ref[block, HEAD_DIM:, :], other_ref[block]
        key_rows = jnp.where(core == 0, first, second).astype(jnp.float32)
        queries[:, cols] = own_ref[block, :HEAD_DIM, :]
        values[:HEAD_DIM, cols] = jnp.where(core == 0, second, first)
        values[HEAD_DIM:, cols] = jnp.ones((16, rows), jnp.bfloat16)
        keys[cols, :] = (key_rows * HEAD_DIM ** (-0.5)).T.astype(jnp.bfloat16)
        return 0

    lax.fori_loop(0, blocks, fill, 0)
    keys[seq_len:, :] = jnp.zeros((rows, HEAD_DIM), jnp.bfloat16)
    values[:, seq_len:] = jnp.zeros((HEAD_DIM + 16, rows), jnp.bfloat16)

    def diagonal_step(index, _):
        firsts = [pl.multiple_of((index * chains + part) * chain, chain) for part in range(chains)]
        spans = [pl.ds(first, chain + rows) for first in firsts]
        scores = [
            dot_f32(keys[span, :], queries[:, pl.ds(first, chain)], 1, 0)
            for first, span in zip(firsts, spans)
        ]
        for first, span, score in zip(firsts, spans, scores):
            here = pl.ds(first, chain)
            key_pos = first + lax.broadcasted_iota(jnp.int32, score.shape, 0)
            score = jnp.where(key_pos <= limit_ref[:, here], score, NEG)
            most = jnp.max(score, 0, keepdims=True)
            highest[:, here] = most
            total[:, here] = dot_f32(
                values[:, span], jnp.exp(score - most).astype(jnp.bfloat16), 1, 0
            )
        return 0

    lax.fori_loop(0, seq_len // query_block, diagonal_step, 0)

    def earlier_keys(span, firsts):
        terms, over = [], []
        for first in firsts:
            here = pl.ds(first, chain)
            score = dot_f32(keys[span, :], queries[:, here], 1, 0)
            most = highest[:, here]
            over.append(jnp.max(score, 0, keepdims=True) - most)
            weights = jnp.exp(score - most).astype(jnp.bfloat16)
            terms.append(dot_f32(values[:, span], weights, 1, 0))
        most_over = jnp.max(functools.reduce(jnp.maximum, over))

        @pl.when(most_over <= RAISE_AT)
        def _():
            for first, term in zip(firsts, terms):
                total[:, pl.ds(first, chain)] += term

        @pl.when(most_over > RAISE_AT)
        def _():
            for first in firsts:
                here = pl.ds(first, chain)
                score = dot_f32(keys[span, :], queries[:, here], 1, 0)
                before = highest[:, here]
                after_all = jnp.maximum(before, jnp.max(score, 0, keepdims=True))
                weights = jnp.exp(score - after_all).astype(jnp.bfloat16)
                highest[:, here] = after_all
                total[:, here] = total[:, here] * jnp.exp(before - after_all) + dot_f32(
                    values[:, span], weights, 1, 0
                )

    def query_step(index, _):
        first = index * query_block
        firsts = [pl.multiple_of(first + part * chain, chain) for part in range(chains)]

        def full_step(step, _):
            earlier_keys(at_rows(step * key_block, key_block), firsts)
            return 0

        lax.fori_loop(0, first // key_block, full_step, 0)
        for part in range(1, chains):
            earlier_keys(pl.ds(firsts[part - 1], chain), firsts[part:])
        for piece in range(query_block // rows):
            here = at_rows(first + piece * rows, rows)
            row_sum = total[HEAD_DIM : HEAD_DIM + 1, here]
            result = total[:HEAD_DIM, here] / row_sum
            block = index * (query_block // rows) + piece
            out_ref[block] = result.astype(jnp.bfloat16)
            out_f_ref[block] = result
            log_ref[:, here] = highest[:, here] + jnp.log(row_sum)
        return 0

    lax.fori_loop(0, seq_len // query_block, query_step, 0)


def attend(core, own, other, limit):
    blocks, _, rows = own.shape
    seq_len = blocks * rows
    query_block = math.gcd(seq_len, 2048)
    key_block = math.gcd(query_block, 2048)
    block_shape = (blocks, HEAD_DIM, rows)
    return pl.pallas_call(
        functools.partial(
            attend_kernel,
            query_block=query_block,
            key_block=key_block,
            chain=math.gcd(query_block, 512),
        ),
        out_shape=(
            jax.ShapeDtypeStruct(block_shape, jnp.bfloat16),
            jax.ShapeDtypeStruct(block_shape, jnp.float32),
            jax.ShapeDtypeStruct((1, seq_len), jnp.float32),
        ),
        in_specs=[pl.BlockSpec(memory_space=pltpu.SMEM)] + [whole_vmem()] * 3,
        out_specs=(whole_vmem(),) * 3,
        scratch_shapes=[
            pltpu.VMEM((seq_len + rows, HEAD_DIM), jnp.bfloat16),
            pltpu.VMEM((HEAD_DIM, seq_len), jnp.bfloat16),
            pltpu.VMEM((HEAD_DIM + 16, seq_len + rows), jnp.bfloat16),
            pltpu.VMEM((1, seq_len), jnp.float32),
            pltpu.VMEM((HEAD_DIM + 16, seq_len), jnp.float32),
        ],
        cost_estimate=pl.CostEstimate(
            flops=seq_len * seq_len * 512, bytes_accessed=8 * MIB, transcendentals=0
        ),
        compiler_params=pltpu.CompilerParams(vmem_limit_bytes=56 * MIB),
        name="attend",
    )(core, own, other, limit)


def split_three(values):
    high = values.astype(jnp.bfloat16).astype(jnp.float32)
    middle = (values - high).astype(jnp.bfloat16).astype(jnp.float32)
    return high, middle, values - high - middle


def three_parts(values):
    high, middle, low = split_three(values)
    row = lax.broadcasted_iota(jnp.int32, (16, values.shape[1]), 0)
    return jnp.where(
        row == 0, high, jnp.where(row == 1, middle, jnp.where(row == 2, low, 0.0))
    )


def attend_back_kernel(
    tp_ref, own_ref, other_ref, limit_ref, out_f_ref, log_ref, grad_ref,
    grad_q_ref, keep_ref, send_ref,
    queries, queries_t, keys_t, values_t, grads, grads_t, grad_k, grad_v, grad_q,
    *, query_block, key_block, chain
):
    core = tp_ref[0]
    blocks, _, rows = own_ref.shape
    seq_len = blocks * rows
    chains = query_block // chain

    def fill(block, _):
        cols = at_rows(block * rows, rows)
        first, second = own_ref[block, HEAD_DIM:, :], other_ref[block]
        key_rows = jnp.where(core == 0, first, second).astype(jnp.float32)
        key_rows = key_rows * HEAD_DIM ** (-0.5)
        query, grad = own_ref[block, :HEAD_DIM, :], grad_ref[block]
        grad_f = grad.astype(jnp.float32)
        delta = jnp.sum(grad_f * out_f_ref[block], 0, keepdims=True)
        ones = jnp.ones((16, rows), jnp.bfloat16)
        query_parts = [query.astype(jnp.float32), three_parts(-log_ref[:, cols])]
        queries[cols, :] = jnp.concatenate(query_parts, 0).T.astype(jnp.bfloat16)
        queries_t[:, cols] = query
        keys_t[:HEAD_DIM, cols] = key_rows.astype(jnp.bfloat16)
        keys_t[HEAD_DIM:, cols] = ones
        values_t[:HEAD_DIM, cols] = jnp.where(core == 0, second, first)
        values_t[HEAD_DIM:, cols] = ones
        grads[cols, :] = jnp.concatenate([grad_f, three_parts(-delta)], 0).T.astype(jnp.bfloat16)
        grads_t[:, cols] = grad
        grad_k[:, cols] = jnp.zeros((HEAD_DIM, rows), jnp.float32)
        grad_v[:, cols] = jnp.zeros((HEAD_DIM, rows), jnp.float32)
        return 0

    lax.fori_loop(0, blocks, fill, 0)

    def tile(query_rows, here, key_cols, key_first):
        probs = jnp.exp(dot_f32(queries[query_rows, :], keys_t[:, key_cols], 1, 0))
        if key_first is not None:
            limit = limit_ref[:, query_rows].astype(jnp.float32)
            limit = jnp.broadcast_to(limit, (8, limit.shape[1])).T[:, :1]
            key_pos = key_first + lax.broadcasted_iota(jnp.int32, probs.shape, 1)
            probs = jnp.where(key_pos.astype(jnp.float32) <= limit, probs, 0.0)
        grad_probs = dot_f32(grads[query_rows, :], values_t[:, key_cols], 1, 0)
        grad_scores = (probs * grad_probs).astype(jnp.bfloat16)
        grad_v[:, key_cols] += dot_f32(grads_t[:, query_rows], probs.astype(jnp.bfloat16), 1, 0)
        grad_k[:, key_cols] += dot_f32(queries_t[:, query_rows], grad_scores, 1, 0)
        grad_q[:, here] += dot_f32(keys_t[:HEAD_DIM, key_cols], grad_scores, 1, 1)

    def query_step(index, _):
        first = index * query_block
        grad_q[...] = jnp.zeros_like(grad_q)

        def full_step(step, _):
            tile(
                at_rows(first, query_block),
                slice(0, query_block),
                at_rows(step * key_block, key_block),
                None,
            )
            return 0

        lax.fori_loop(0, first // key_block, full_step, 0)
        for low in range(0, query_block, chain):
            here = pl.multiple_of(first + low, chain)
            if low:
                tile(
                    pl.ds(here, query_block - low),
                    slice(low, query_block),
                    pl.ds(pl.multiple_of(here - chain, chain), chain),
                    None,
                )
            tile(pl.ds(here, chain), slice(low, low + chain), pl.ds(here, chain), here)
            tile(
                at_rows(here + chain - rows, rows),
                slice(low + chain - rows, low + chain),
                at_rows(jnp.minimum(here + chain, seq_len - rows), rows),
                here + chain,
            )
        for piece in range(query_block // rows):
            here = grad_q[:, piece * rows : (piece + 1) * rows]
            grad_q_ref[index * (query_block // rows) + piece] = here.astype(jnp.bfloat16)
        return 0

    lax.fori_loop(0, seq_len // query_block, query_step, 0)

    def finish(block, _):
        cols = at_rows(block * rows, rows)
        key_part = grad_k[:, cols] * HEAD_DIM ** (-0.5)
        value_part = grad_v[:, cols]
        keep_ref[block] = jnp.where(core == 0, key_part, value_part)
        send_ref[block] = jnp.where(core == 0, value_part, key_part).astype(jnp.bfloat16)
        return 0

    lax.fori_loop(0, blocks, finish, 0)


def attend_back(core, own, other, limit, out_f, log_total, grad):
    blocks, _, rows = own.shape
    seq_len = blocks * rows
    query_block = math.gcd(seq_len, 2048)
    key_block = math.gcd(query_block, 1024)
    block_shape = (blocks, HEAD_DIM, rows)
    wide = HEAD_DIM + 16
    return pl.pallas_call(
        functools.partial(
            attend_back_kernel,
            query_block=query_block,
            key_block=key_block,
            chain=math.gcd(query_block, 512),
        ),
        out_shape=(
            jax.ShapeDtypeStruct(block_shape, jnp.bfloat16),
            jax.ShapeDtypeStruct(block_shape, jnp.float32),
            jax.ShapeDtypeStruct(block_shape, jnp.bfloat16),
        ),
        in_specs=[pl.BlockSpec(memory_space=pltpu.SMEM)] + [whole_vmem()] * 6,
        out_specs=(whole_vmem(),) * 3,
        scratch_shapes=[
            pltpu.VMEM((seq_len, wide), jnp.bfloat16),
            pltpu.VMEM((HEAD_DIM, seq_len), jnp.bfloat16),
            pltpu.VMEM((wide, seq_len), jnp.bfloat16),
            pltpu.VMEM((wide, seq_len), jnp.bfloat16),
            pltpu.VMEM((seq_len, wide), jnp.bfloat16),
            pltpu.VMEM((HEAD_DIM, seq_len), jnp.bfloat16),
            pltpu.VMEM((HEAD_DIM, seq_len), jnp.float32),
            pltpu.VMEM((HEAD_DIM, seq_len), jnp.float32),
            pltpu.VMEM((HEAD_DIM, query_block), jnp.float32),
        ],
        cost_estimate=pl.CostEstimate(
            flops=seq_len * seq_len * 1024, bytes_accessed=12 * MIB, transcendentals=0
        ),
        compiler_params=pltpu.CompilerParams(vmem_limit_bytes=60 * MIB),
        name="attend_back",
    )(core, own, other, limit, out_f, log_total, grad)


def project_kernel(*refs, count):
    place_ref, x_ref, cosine_ref, sine_ref = refs[:4]
    mine_refs, other_refs = refs[4 : 4 + count], refs[4 + count : 4 + 2 * count]
    normed_ref, sent_ref, heads_ref, small_ref = refs[4 + 2 * count :]
    core, level, spot = place_ref[0], place_ref[1], place_ref[2]
    micro_count, rows, width = x_ref.shape
    columns, shard, _ = mine_refs[0].shape
    half_cols = heads_ref.shape[2]
    half_dim = HEAD_DIM // 2
    units = half_cols // (2 * HEAD_DIM)
    kv_heads = units // 2
    for step in range(count):
        for up in range(columns):
            here = at_rows(((level ^ up) * count + (spot ^ step)) * shard, shard)
            heads_ref[core, here, :] = mine_refs[step][up, :, :half_cols]
            heads_ref[1 - core, here, :] = other_refs[step][up, :, :half_cols]
            small_ref[here, :] = mine_refs[step][up, :, half_cols:]
    cosine, sine = cosine_ref[...], sine_ref[...]
    gain_row = small_ref.shape[1] // 2
    gain = small_ref[...].astype(jnp.float32).T[gain_row : gain_row + 1]

    def rotated(heads):
        first, second = heads[:half_dim], heads[half_dim:]
        return jnp.concatenate(
            [first * cosine - second * sine, second * cosine + first * sine], 0
        ).astype(jnp.bfloat16)

    for micro in range(micro_count):
        x = x_ref[micro].astype(jnp.float32)
        scale = lax.rsqrt(jnp.mean(x * x, -1, keepdims=True) + EPS)
        normed = (x * scale * gain).astype(jnp.bfloat16)
        normed_ref[micro * rows : (micro + 1) * rows, :] = normed
        for part in range(2):
            heads = dot_f32(normed, heads_ref[part], 1, 0).T
            for unit in range(units):
                first = unit * HEAD_DIM
                paired = (units + unit // 2 + unit % 2 * kv_heads) * HEAD_DIM
                block = (micro * 2 + part) * units + unit
                second = heads[paired : paired + HEAD_DIM]
                sent_ref[block, :HEAD_DIM, :] = rotated(heads[first : first + HEAD_DIM])
                sent_ref[block, HEAD_DIM:, :] = (
                    rotated(second) if unit % 2 == 0 else second.astype(jnp.bfloat16)
                )


def project(place, x, cosine, sine, mine, other, devices):
    micro_count, rows, width = x.shape
    half_cols = mine[0].shape[2] - LANES
    return pl.pallas_call(
        functools.partial(project_kernel, count=len(mine)),
        out_shape=(
            jax.ShapeDtypeStruct((micro_count * rows, width), jnp.bfloat16),
            jax.ShapeDtypeStruct((devices, 2 * HEAD_DIM, rows), jnp.bfloat16),
            jax.ShapeDtypeStruct((2, width, half_cols), jnp.bfloat16),
            jax.ShapeDtypeStruct((width, LANES), jnp.bfloat16),
        ),
        in_specs=[pl.BlockSpec(memory_space=pltpu.SMEM)]
        + [whole_vmem()] * (3 + len(mine) + len(other)),
        out_specs=(whole_vmem(),) * 4,
        compiler_params=pltpu.CompilerParams(vmem_limit_bytes=48 * MIB),
        name="project",
    )(place, x, cosine, sine, *mine, *other)


def project_back_kernel(
    tp_ref, grad_ref, heads_ref, normed_ref, x_ref, grad_resid_ref, gain_ref, cosine_ref,
    sine_ref, grad_x_ref, kept_ref, given_ref, grad_rows
):
    core = tp_ref[0]
    micro_count, rows, width = x_ref.shape
    half_cols = heads_ref.shape[2]
    half_dim = HEAD_DIM // 2
    units = half_cols // (2 * HEAD_DIM)
    cosine, sine = cosine_ref[...], sine_ref[...]

    def turned_back(heads):
        first, second = heads[:half_dim].astype(jnp.float32), heads[half_dim:].astype(jnp.float32)
        return [first * cosine + second * sine, second * cosine - first * sine]

    for micro in range(micro_count):
        for part in range(2):
            first_block = (micro * 2 + part) * units
            pieces = []
            for block in range(first_block, first_block + units):
                pieces += turned_back(grad_ref[block, :HEAD_DIM, :])
            for block in range(first_block, first_block + units, 2):
                pieces += turned_back(grad_ref[block, HEAD_DIM:, :])
            for block in range(first_block + 1, first_block + units, 2):
                pieces.append(grad_ref[block, HEAD_DIM:, :].astype(jnp.float32))
            grad_rows[part, micro * rows : (micro + 1) * rows, :] = (
                jnp.concatenate(pieces, 0).T.astype(jnp.bfloat16)
            )
    gain = gain_ref[...]
    grad_gain = jnp.zeros((1, width), jnp.float32)
    for micro in range(micro_count):
        here = slice(micro * rows, (micro + 1) * rows)
        grad_normed = dot_f32(grad_rows[0, here, :], heads_ref[0], 1, 1) + dot_f32(
            grad_rows[1, here, :], heads_ref[1], 1, 1
        )
        x = x_ref[micro].astype(jnp.float32)
        scale = lax.rsqrt(jnp.mean(x * x, -1, keepdims=True) + EPS)
        gained = grad_normed * gain
        grad_gain = grad_gain + jnp.sum(grad_normed * x * scale, 0, keepdims=True)
        grad_x_ref[micro] = (
            grad_resid_ref[here, :]
            + scale * gained
            - x * scale**3 * jnp.mean(x * gained, -1, keepdims=True)
        )
    normed_t = normed_ref[...].T
    gain_cols = jnp.broadcast_to(grad_gain, (LANES, width)).T.astype(jnp.bfloat16)
    for ref, part in ((kept_ref, core), (given_ref, 1 - core)):
        ref[:, :half_cols] = dot_f32(normed_t, grad_rows[part], 1, 0).astype(jnp.bfloat16)
        ref[:, half_cols:] = gain_cols


def project_back(core, grad_own, heads, normed, x, grad_resid, gain, cosine, sine):
    micro_count, rows, width = x.shape
    half_cols = heads.shape[2]
    share = jax.ShapeDtypeStruct((width, half_cols + LANES), jnp.bfloat16)
    return pl.pallas_call(
        project_back_kernel,
        out_shape=(jax.ShapeDtypeStruct(x.shape, jnp.float32), share, share),
        in_specs=[pl.BlockSpec(memory_space=pltpu.SMEM)] + [whole_vmem()] * 8,
        out_specs=(whole_vmem(),) * 3,
        scratch_shapes=[pltpu.VMEM((2, micro_count * rows, half_cols), jnp.bfloat16)],
        compiler_params=pltpu.CompilerParams(vmem_limit_bytes=56 * MIB),
        name="project_back",
    )(core, grad_own, heads, normed, x, grad_resid, gain, cosine, sine)


def experts_kernel(*refs, slots, first_call, pieces, piece_count, spread, spread_x):
    place_ref, refs = refs[0], refs[1:]
    x_refs, dy_refs = refs[:slots], refs[slots : 2 * slots]
    w_route_ref, weight_refs = refs[2 * slots], refs[2 * slots + 1 : 2 * slots + 1 + piece_count]
    refs = refs[2 * slots + 1 + piece_count :]
    if not first_call:
        before_refs, refs = refs[:3], refs[3:]
    x_outs = 1 if spread_x else slots
    mix_ref, grad_x_refs, refs = refs[0], refs[1 : 1 + x_outs], refs[1 + x_outs :]
    keep_ref, send_in_ref, send_out_ref = refs[:3]
    (
        x_all, x_t, dy_all, dy_t, gates, grad_gates, mix_sum, grad_x_sum, grad_w, weights, sems,
        hidden, grad_gate_pre, grad_up_pre,
    ) = refs[3:]
    expert, expert_count = pl.program_id(0), pl.num_programs(0)
    rows, width = x_refs[0].shape
    total = slots * rows
    half = width // 2
    core = place_ref[0]

    def moves(index):
        copies = []
        for number, (array, whose, first, last) in enumerate(pieces[index]):
            target = weights.at[index % 2, pl.ds(first, last - first)]
            if whose is not None:
                part = core if whose == 0 else 1 - core
                target = weights.at[
                    index % 2, pl.ds(first, last - first), pl.ds(pl.multiple_of(part * half, half), half)
                ]
            copies.append(
                pltpu.make_async_copy(weight_refs[array], target, sems.at[index, number])
            )
        return copies

    @pl.when(expert == 0)
    def _():
        for copy in moves(0) + moves(1):
            copy.start()
        for slot in range(slots):
            here = slice(slot * rows, (slot + 1) * rows)
            x, dy = x_refs[slot][...], dy_refs[slot][:, :width]
            x_all[here, :] = x
            x_t[:, here] = x.T
            dy_all[here, :] = dy
            dy_t[:, here] = dy.T
            chosen = dy_refs[slot][:, width:].astype(jnp.float32)
            gates[here, :] = chosen_gates(x, w_route_ref[...], chosen)
        grad_gates[...] = jnp.zeros_like(grad_gates)
        mix_sum[...] = jnp.zeros_like(mix_sum)
        grad_x_sum[...] = jnp.zeros_like(grad_x_sum)

    for index in range(len(pieces)):

        @pl.when(expert == index)
        def _():
            if 1 <= index < len(pieces) - 1:
                for copy in moves(index + 1):
                    copy.start()
            for copy in moves(index):
                copy.wait()

    if first_call:
        grad_w[...] = jnp.zeros_like(grad_w)
    else:
        keep_before, in_before, out_before = before_refs
        grad_w[core] = keep_before[0].astype(jnp.float32)
        grad_w[1 - core, :2] = in_before[0].astype(jnp.float32)
        grad_w[1 - core, 2:] = out_before[0].astype(jnp.float32)
    buffer = lax.rem(expert, 2)
    w_gate, w_up, w_down_t = weights[buffer, 0], weights[buffer, 1], weights[buffer, 2]
    lane = lax.broadcasted_iota(jnp.int32, (total, LANES), 1)
    gate = jnp.sum(jnp.where(lane == place_ref[1 + expert], gates[...], 0.0), 1, keepdims=True)
    gate_row = jnp.broadcast_to(gate, (total, LANES)).T[:1]
    x = x_all[...]
    dy = dy_all[...].astype(jnp.float32)
    gate_pre = dot_f32(x, w_gate, 1, 0)
    up_pre = dot_f32(x, w_up, 1, 0)
    sigmoid_val = 0.5 + 0.5 * jnp.tanh(0.5 * gate_pre)
    silu_val = gate_pre * sigmoid_val
    up_slope = up_pre * (sigmoid_val * (1.0 + gate_pre * (1.0 - sigmoid_val)))
    hidden[...] = (silu_val * up_pre).astype(jnp.bfloat16)
    grad_hidden = dot_f32((gate * dy).astype(jnp.bfloat16), w_down_t, 1, 0)
    grad_gate_pre[...] = (grad_hidden * up_slope).astype(jnp.bfloat16)
    grad_up_pre[...] = (grad_hidden * silu_val).astype(jnp.bfloat16)
    out = dot_f32(hidden[...], w_down_t, 1, 1).astype(jnp.bfloat16).astype(jnp.float32)
    grad_gate = jnp.sum(out * dy, 1, keepdims=True)
    grad_gates[pl.ds(expert, 1), :] = jnp.broadcast_to(grad_gate, (total, LANES)).T[:1]
    mix_sum[...] += gate * out
    grad_copy = dot_f32(grad_gate_pre[...], w_gate, 1, 1) + dot_f32(
        grad_up_pre[...], w_up, 1, 1
    )
    grad_x_sum[...] += grad_copy.astype(jnp.bfloat16).astype(jnp.float32)
    grad_out_t = (dy_t[...].astype(jnp.float32) * gate_row).astype(jnp.bfloat16)
    terms = (
        dot_f32(x_t[...], grad_gate_pre[...], 1, 0),
        dot_f32(x_t[...], grad_up_pre[...], 1, 0),
        dot_f32(grad_out_t, hidden[...], 1, 0),
    )
    for part in range(2):
        for matrix, term in enumerate(terms):
            grad_w[part, matrix] += term[part * half : (part + 1) * half]
    keep_ref[0] = grad_w[core].astype(jnp.bfloat16)
    send_in_ref[0] = grad_w[1 - core, :2].astype(jnp.bfloat16)
    send_out_ref[0] = grad_w[1 - core, 2:].astype(jnp.bfloat16)

    @pl.when(expert == expert_count - 1)
    def _():
        for slot in range(slots):
            here = slice(slot * rows, (slot + 1) * rows)
            block = (place_ref[place_ref.shape[0] - 1] ^ (slot + 1)) if spread else slot
            mix_ref[block] = mix_sum[here, :].astype(jnp.bfloat16)
            grad_x_ref = grad_x_refs[0].at[block] if spread_x else grad_x_refs[slot]
            grad_x_ref[:, :width] = grad_x_sum[here, :].astype(jnp.bfloat16)
            parts = split_three(grad_gates[:, here])
            rest = jnp.zeros((LANES - 3 * parts[0].shape[0], rows), jnp.float32)
            grad_x_ref[:, width:] = (
                jnp.concatenate([*parts, rest], 0).T.astype(jnp.bfloat16)
            )
        if spread:
            own_block = place_ref[place_ref.shape[0] - 1]
            mix_ref[own_block] = jnp.zeros((rows, width), jnp.bfloat16)
        if spread_x:
            grad_x_refs[0][own_block] = jnp.zeros((rows, width + LANES), jnp.bfloat16)


def experts(place, x_parts, dy_parts, w_route, weights, pieces, before, spread, spread_x):
    rows = dy_parts[0][0].shape[1]
    width, hidden_width = x_parts[0][0].shape[1], weights[0].shape[-1]
    count, slots = len(pieces), len(x_parts)
    total = slots * rows
    half = width // 2
    mix_slots = slots + 1 if spread else slots
    first_call = before is None
    before = () if first_call else tuple(before)

    def at_block(shape, index):
        return pl.BlockSpec(
            shape,
            lambda expert: (index,) + (0,) * (len(shape) - 1),
            pipeline_mode=pl.Buffered(1),
        )

    row_specs = (pl.BlockSpec((rows, width + LANES), lambda expert: (0, 0)),) * slots
    if spread_x:
        row_specs = (pl.BlockSpec((mix_slots, rows, width + LANES), lambda expert: (0, 0, 0)),)
    grad_specs = [
        pl.BlockSpec((1, size, half, hidden_width), lambda expert: (expert, 0, 0, 0))
        for size in (3, 2, 1)
    ]
    grad_shapes = tuple(
        jax.ShapeDtypeStruct((count, size, half, hidden_width), jnp.bfloat16) for size in (3, 2, 1)
    )
    row_shapes = (jax.ShapeDtypeStruct((rows, width + LANES), jnp.bfloat16),) * slots
    if spread_x:
        row_shapes = (jax.ShapeDtypeStruct((mix_slots, rows, width + LANES), jnp.bfloat16),)
    outs = pl.pallas_call(
        functools.partial(
            experts_kernel,
            slots=slots,
            first_call=first_call,
            pieces=pieces,
            piece_count=len(weights),
            spread=spread,
            spread_x=spread_x,
        ),
        grid=(count,),
        out_shape=(jax.ShapeDtypeStruct((mix_slots, rows, width), jnp.bfloat16),)
        + row_shapes
        + grad_shapes,
        in_specs=[pl.BlockSpec(memory_space=pltpu.SMEM)]
        + [at_block((rows, width), index) for _, index in x_parts]
        + [at_block((None, rows, width + LANES), index) for _, index in dy_parts]
        + [at_block((width, LANES), 0)]
        + [pl.BlockSpec(memory_space=pl.ANY)] * len(weights)
        + grad_specs[: len(before)],
        out_specs=(pl.BlockSpec((mix_slots, rows, width), lambda expert: (0, 0, 0)),)
        + row_specs
        + tuple(grad_specs),
        scratch_shapes=[
            pltpu.VMEM((total, width), jnp.bfloat16),
            pltpu.VMEM((width, total), jnp.bfloat16),
            pltpu.VMEM((total, width), jnp.bfloat16),
            pltpu.VMEM((width, total), jnp.bfloat16),
            pltpu.VMEM((total, LANES), jnp.float32),
            pltpu.VMEM((8, total), jnp.float32),
            pltpu.VMEM((total, width), jnp.float32),
            pltpu.VMEM((total, width), jnp.float32),
            pltpu.VMEM((2, 3, half, hidden_width), jnp.float32),
            pltpu.VMEM((2, 3, width, hidden_width), jnp.bfloat16),
            pltpu.SemaphoreType.DMA((count, max(len(group) for group in pieces))),
        ]
        + [pltpu.VMEM((total, hidden_width), jnp.bfloat16)] * 3,
        cost_estimate=pl.CostEstimate(
            flops=count * total * width * hidden_width * 18,
            bytes_accessed=count * width * hidden_width * 12,
            transcendentals=0,
        ),
        compiler_params=pltpu.CompilerParams(
            vmem_limit_bytes=62 * MIB, dimension_semantics=("arbitrary",)
        ),
        name="experts",
    )(
        place,
        *[array for array, _ in (*x_parts, *dy_parts)],
        w_route,
        *weights,
        *before,
    )
    return outs[0], outs[1 : 1 + len(row_shapes)], outs[1 + len(row_shapes) :]


def together(*values):
    return lax.optimization_barrier(values)


def chosen_gates(x, w_route, chosen):
    logits = jnp.where(chosen > 0.0, dot_f32(x, w_route, 1, 0), NEG)
    raised = jnp.exp(logits - jnp.max(logits, 1, keepdims=True)) * chosen
    return raised / jnp.sum(raised, 1, keepdims=True)


def resid_back_kernel(*refs, counts):
    ids_ref, resid_ref, normed_ref, dy_ref, gain_ref, w_route_ref, w_out_ref = refs[:7]
    part_refs, refs = refs[7 : 7 + sum(counts)], refs[7 + sum(counts) :]
    grad_resid_ref, grad_branch_ref, grad_att_ref, grad_logits_ref, grad_gain_ref = refs
    micro_count, rows, width = dy_ref.shape[0], dy_ref.shape[1], resid_ref.shape[1]
    columns = ids_ref.shape[0] // (2 * PLANE)
    heads = w_out_ref.shape[1] // HEAD_DIM
    lane = lax.broadcasted_iota(jnp.int32, (rows, LANES), 1)
    gain = gain_ref[...]
    grad_gain = jnp.zeros((1, width), jnp.float32)
    for micro in range(micro_count):
        here = slice(micro * rows, (micro + 1) * rows)
        grad_normed = jnp.zeros((rows, width), jnp.float32)
        grad_gates = jnp.zeros((rows, LANES), jnp.float32)
        group = part_refs[sum(counts[:micro]) : sum(counts[: micro + 1])]
        if counts[micro] == 2:
            sources = [(group[1].at[place], PLANE + place) for place in range(PLANE)]
            sources.append((group[0], 0))
        else:
            sources = [(part_ref, step) for step, part_ref in enumerate(group)]
        for part_ref, step in sources:
            grad_normed = grad_normed + part_ref[:, :width].astype(jnp.float32)
            three = part_ref[:, width:].astype(jnp.float32)
            for up in range(columns):
                column = three[:, up : up + 1] + three[:, 8 + up : 9 + up]
                column = column + three[:, 16 + up : 17 + up]
                grad_gates = jnp.where(lane == ids_ref[step * columns + up], column, grad_gates)
        chosen = dy_ref[micro, :, width:].astype(jnp.float32)
        gates = chosen_gates(normed_ref[here, :], w_route_ref[...], chosen)
        weighted = jnp.sum(gates * grad_gates, 1, keepdims=True)
        grad_logits = (gates * (grad_gates - weighted)).astype(jnp.bfloat16)
        grad_logits_ref[here, :] = grad_logits
        grad_normed = grad_normed + dot_f32(grad_logits, w_route_ref[...], 1, 1)
        resid = resid_ref[here, :]
        scale = lax.rsqrt(jnp.mean(resid * resid, -1, keepdims=True) + EPS)
        gained = grad_normed * gain
        grad_gain = grad_gain + jnp.sum(grad_normed * resid * scale, 0, keepdims=True)
        grad_resid = (
            dy_ref[micro, :, :width].astype(jnp.float32)
            + scale * gained
            - resid * scale**3 * jnp.mean(resid * gained, -1, keepdims=True)
        )
        grad_resid_ref[here, :] = grad_resid
        grad_branch = grad_resid.astype(jnp.bfloat16)
        grad_branch_ref[here, :] = grad_branch
        turned = dot_f32(grad_branch, w_out_ref[...], 1, 0).T
        for head in range(heads):
            grad_att_ref[micro * heads + head] = turned[
                head * HEAD_DIM : (head + 1) * HEAD_DIM
            ].astype(jnp.bfloat16)
    grad_gain_ref[...] = jnp.broadcast_to(grad_gain, grad_gain_ref.shape)


def resid_back(ids, resid, normed, dy, gain, w_route, w_out_t, parts):
    total, width = resid.shape
    rows = dy.shape[1]
    heads = dy.shape[0] * w_out_t.shape[1] // HEAD_DIM
    flat = [part for group in parts for part in group]
    return pl.pallas_call(
        functools.partial(resid_back_kernel, counts=tuple(len(group) for group in parts)),
        out_shape=(
            jax.ShapeDtypeStruct((total, width), jnp.float32),
            jax.ShapeDtypeStruct((total, width), jnp.bfloat16),
            jax.ShapeDtypeStruct((heads, HEAD_DIM, rows), jnp.bfloat16),
            jax.ShapeDtypeStruct((total, LANES), jnp.bfloat16),
            jax.ShapeDtypeStruct((8, width), jnp.float32),
        ),
        in_specs=[pl.BlockSpec(memory_space=pltpu.SMEM)] + [whole_vmem()] * (6 + len(flat)),
        out_specs=(whole_vmem(),) * 5,
        compiler_params=pltpu.CompilerParams(vmem_limit_bytes=48 * MIB),
        name="resid_back",
    )(ids, resid, normed, dy, gain, w_route, w_out_t, *flat)


def flip(values, bits):
    count = lax.axis_size("ep")
    return lax.ppermute(values, "ep", [(index, index ^ bits) for index in range(count)])


def swap_cores(values):
    return lax.ppermute(values, "tp", [(0, 1), (1, 0)])


def every_device(values):
    return lax.all_to_all(values, ("ep", "tp"), 0, 0, tiled=True)


def head_tables(first_pos, rows):
    positions = first_pos + jnp.arange(rows, dtype=jnp.int32)
    halves = jnp.arange(HEAD_DIM // 2, dtype=jnp.float32)
    freqs = THETA ** (-2.0 * halves / HEAD_DIM)
    angles = freqs[:, None] * positions.astype(jnp.float32)[None, :]
    return jnp.cos(angles), jnp.sin(angles)


def paired_layout(ep_count, tp_count, micro_count, slice_rows, width, q_cols, kv_cols, experts_here):
    group = q_cols // kv_cols
    kv_heads = kv_cols * tp_count // HEAD_DIM
    return (
        tp_count == 2
        and group == 2
        and ep_count == micro_count * kv_heads
        and ep_count == PLANE * PLANE
        and experts_here == 1
        and slice_rows >= PIECE
        and slice_rows % PIECE == 0
        and width % (2 * LANES) == 0
    )


def on_device_paired(
    tokens,
    gain_attn,
    w_query,
    w_key,
    w_value,
    w_output,
    gain_moe,
    w_router,
    w_gate,
    w_up,
    w_down,
    routes,
    piece_starts,
    cotangent,
):
    ep_count = lax.axis_size("ep")
    tp_count = lax.axis_size("tp")
    ep_index, tp_index = lax.axis_index("ep"), lax.axis_index("tp")
    micro_count, rows, width = tokens.shape
    devices = ep_count * tp_count
    seq_len = rows * devices
    all_rows = micro_count * rows
    shard = gain_attn.shape[0]
    q_cols, kv_cols = w_query.shape[1], w_key.shape[1]
    kv_here = kv_cols // HEAD_DIM
    half_cols = q_cols + 2 * kv_cols
    out_cols = w_output.shape[0]
    columns = ep_count // PLANE
    experts_all = ep_count
    core = tp_index.astype(jnp.int32).reshape(1)

    level, spot = ep_index // PLANE, ep_index % PLANE
    half = width // 2
    micros = range(micro_count)

    small = jnp.concatenate([w_router, jnp.zeros((shard, LANES - experts_all), w_router.dtype)], 1)
    lanes = jnp.arange(LANES, dtype=jnp.int32)
    small = jnp.where(lanes == LANES // 2, gain_attn[:, None], small)
    small = jnp.where(lanes == LANES // 2 + 1, gain_moe[:, None], small)
    packed = jnp.concatenate([w_query, w_key, w_value, small], 1)
    levels = [packed] + [flip(packed, PLANE * step) for step in range(1, columns)]
    mine = jnp.stack(levels)
    mine = [mine] + [flip(mine, step) for step in range(1, PLANE)]

    w_down_t = w_down[0].T
    first_half = tp_index * half
    expert_half = jnp.stack(
        [
            lax.dynamic_slice_in_dim(whole, first_half, half, 0)
            for whole in (w_gate[0], w_up[0], w_down_t)
        ]
    )
    expert_half, levels = together(expert_half, levels)
    far_out = flip(expert_half[2:], 2 * PLANE)
    near_out = flip(expert_half[2:], PLANE)
    mine, far_out, near_out = together(mine, far_out, near_out)
    other = [swap_cores(part) for part in mine]

    x_rows = tokens.reshape(all_rows, width).astype(jnp.float32)
    device_index = ep_index * tp_count + tp_index
    cosine, sine = head_tables(device_index * rows, rows)
    spot_here = jnp.stack([tp_index, level, spot]).astype(jnp.int32)
    normed, sent, w_heads, small_all = project(
        spot_here, tokens, cosine, sine, mine, other, devices
    )
    w_route_full = small_all[:, :experts_all]
    gain_one = small_all[:, LANES // 2].astype(jnp.float32)
    gain_two = small_all[:, LANES // 2 + 1].astype(jnp.float32)
    nearfar_out = flip(far_out, PLANE)
    sent, nearfar_out = together(sent, nearfar_out)
    own = every_device(sent)
    other = swap_cores(own[:, HEAD_DIM:, :])

    chosen = jnp.any(routes[:, :, :, None] == lanes, 2).astype(jnp.bfloat16)
    own_dy = jnp.concatenate([cotangent, chosen], 2)
    w_output_t, expert_late, far_out, dy_late, other = together(
        w_output.T, expert_half, far_out, own_dy, other
    )
    far_in = flip(expert_late[:2], 2 * PLANE)
    near_in = flip(expert_late[:2], PLANE)
    plane_dy = [flip(dy_late, step) for step in range(1, PLANE)]
    gathered_out = lax.all_gather(w_output_t, ("ep", "tp"), axis=0, tiled=False)

    micro_here = ep_index // (ep_count // micro_count)
    starts = lax.dynamic_index_in_dim(piece_starts, micro_here, 0, keepdims=False)
    all_pos = jnp.arange(seq_len, dtype=jnp.int32)[None, :]
    inside = (all_pos >= starts[:, None]) & (all_pos < starts[:, None] + PIECE)
    piece_last = jnp.max(jnp.where(inside, starts[:, None] + (PIECE - 1), -1), 0, keepdims=True)
    limit = jnp.maximum(all_pos, piece_last).astype(jnp.int32)
    out_b, out_f, log_total = attend(core, own, other, limit)
    out_b, near_in, far_in, plane_dy = together(out_b, near_in, far_in, plane_dy)
    nearfar_in = flip(far_in, PLANE)
    attended_t = every_device(out_b).reshape(micro_count, out_cols * tp_count, rows)
    gathered_out = gathered_out.reshape(ep_count, tp_count, shard, out_cols)
    w_out_t = jnp.concatenate(
        [gathered_out[:, part].reshape(width, out_cols) for part in range(2)], 1
    )

    attn_rows = jnp.concatenate(
        [dot_f32(attended_t[micro], w_out_t, 0, 1) for micro in micros], 0
    )
    resid = x_rows + attn_rows
    scale_two = rms_scale(resid)
    normed_two = (resid * scale_two * gain_two).astype(jnp.bfloat16)
    normed_parts = [normed_two[micro * rows : (micro + 1) * rows] for micro in micros]
    plane_x = [[flip(normed_parts[0], step) for step in range(1, PLANE)]]

    weights = [w_gate, w_up, w_down_t[None]]
    nearfar_in, normed_late = together(nearfar_in, normed_two)
    for piece in (near_in, near_out, far_in, far_out, nearfar_in, nearfar_out):
        weights += [piece, swap_cores(piece)]
    pieces = [[(0, None, 0, 1), (1, None, 1, 2), (2, None, 2, 3)]]
    for first in (3, 7, 11):
        pieces.append(
            [(first, 0, 0, 2), (first + 1, 1, 0, 2), (first + 2, 0, 2, 3), (first + 3, 1, 2, 3)]
        )

    spot_here = spot.astype(jnp.int32).reshape(1)
    column_ids = jnp.stack([(level ^ up) * PLANE + spot for up in range(columns)])
    place = jnp.concatenate([core, column_ids.astype(jnp.int32), spot_here])
    own_mix, own_grad_x, before = experts(
        place,
        [(normed_two, micro) for micro in micros],
        [(own_dy, micro) for micro in micros],
        small_all,
        weights,
        pieces,
        None,
        False,
        False,
    )
    leaving = normed_parts[1:]
    leaving, own_mix = together(leaving, own_mix)
    plane_x += [[flip(part, step) for step in range(1, PLANE)] for part in leaving]
    plane_groups = [[up * PLANE + step for step in range(PLANE)] for up in range(columns)]
    column_groups = [[up * PLANE + step for up in range(columns)] for step in range(PLANE)]

    def within_plane(parts):
        return lax.all_to_all(parts, "ep", 0, 0, tiled=True, axis_index_groups=plane_groups)

    far_mix, far_grad_x = [], []
    for micro in micros:
        mix, grad_x, before = experts(
            place,
            [(part, 0) for part in plane_x[micro]],
            [(part, micro) for part in plane_dy],
            small_all,
            weights,
            pieces,
            before,
            True,
            micro == micro_count - 1,
        )
        if micro:
            grad_x, before, far_grad_x = together(grad_x, before, far_grad_x)
        if micro < micro_count - 1:
            far_grad_x.append([flip(grad_x[step - 1], step) for step in range(1, PLANE)])
        else:
            far_grad_x.append([within_plane(grad_x[0])])
        far_mix.append(mix)
    keep_w, send_in_w, send_out_w = before
    given_out = swap_cores(send_out_w)

    def out_sum_of(slot):
        return keep_w[slot, 2].astype(jnp.float32) + given_out[slot, 0].astype(jnp.float32)

    near_out_w = jnp.stack([out_sum_of(slot).astype(jnp.bfloat16) for slot in (1, 3)])
    near_out_w = flip(near_out_w, PLANE)
    far_grad_x[-1], near_out_w, given_out = together(far_grad_x[-1], near_out_w, given_out)
    near_out_w = near_out_w.astype(jnp.float32)

    plane_ids = jnp.stack(
        [
            (level ^ up) * PLANE + (spot ^ step)
            for step in range(PLANE)
            for up in range(columns)
        ]
        + [(level ^ up) * PLANE + place for place in range(PLANE) for up in range(columns)]
    )
    grad_resid, grad_branch, grad_att, grad_logits, grad_gain_two = resid_back(
        plane_ids.astype(jnp.int32),
        resid,
        normed_two,
        own_dy,
        gain_two[None, :],
        small_all,
        w_out_t,
        [[own_grad_x[micro], *far_grad_x[micro]] for micro in micros],
    )
    grad_route = dot_f32(normed_late, grad_logits, 0, 0)[:, :experts_all]
    grad_gain_two = grad_gain_two[0]
    grad_outw = sum(
        dot_f32(grad_branch[micro * rows : (micro + 1) * rows], attended_t[micro], 0, 1)
        for micro in micros
    ).astype(jnp.bfloat16)
    grad_heads = every_device(grad_att)
    far_out_w = (out_sum_of(2) + near_out_w[1]).astype(jnp.bfloat16)
    own_out_w = out_sum_of(0)
    given_in = swap_cores(send_in_w)

    def column_sum(slot):
        kept = keep_w[slot, :2].astype(jnp.float32)
        return (kept + given_in[slot].astype(jnp.float32)).astype(jnp.bfloat16)

    own_w = keep_w[0, :2].astype(jnp.float32) + given_in[0].astype(jnp.float32)
    near_in_w, far_in_w, last_in_w = column_sum(1), column_sum(2), column_sum(3)
    all_mix = jnp.concatenate(far_mix, 1)
    grad_heads, near_in_w, last_in_w, far_in_w, far_out_w, own_w, all_mix = together(
        grad_heads, near_in_w, last_in_w, far_in_w, far_out_w, own_w, all_mix
    )
    all_mix = within_plane(all_mix)
    near_in_w = flip(near_in_w, PLANE)
    last_in_w = flip(last_in_w, 3 * PLANE)
    far_in_w = flip(far_in_w, 2 * PLANE)
    far_out_w = flip(far_out_w, 2 * PLANE)

    def to_shards(kept, given):
        core_sum = kept.astype(jnp.float32) + swap_cores(given).astype(jnp.float32)
        shares = lax.all_to_all(
            core_sum.astype(jnp.bfloat16).reshape(ep_count, shard, -1), "ep", 0, 0, tiled=True
        )
        return jnp.sum(shares.astype(jnp.float32), 0)

    def in_lanes(columns_f):
        small = jnp.concatenate(columns_f, 1)
        return jnp.pad(small, ((0, 0), (0, LANES - small.shape[1]))).astype(jnp.bfloat16)

    def own_rows(values):
        return lax.dynamic_slice_in_dim(values, tp_index * (shard // 2), shard // 2, 0)

    late_small = in_lanes([grad_route, grad_gain_two[:, None]])
    out_parts = [
        jnp.concatenate([grad_outw[:, part * out_cols : (part + 1) * out_cols], late_small], 1)
        for part in range(2)
    ]
    out_kept = jnp.where(tp_index == 0, out_parts[0], out_parts[1])
    out_given = jnp.where(tp_index == 0, out_parts[1], out_parts[0])
    grad_q, keep_kv, send_kv = attend_back(
        core, own, other, limit, out_f, log_total, grad_heads
    )
    grad_q, keep_kv, send_kv, near_in_w, last_in_w, far_in_w, far_out_w, all_mix = together(
        grad_q, keep_kv, send_kv, near_in_w, last_in_w, far_in_w, far_out_w, all_mix
    )
    grad_kv = (keep_kv + swap_cores(send_kv).astype(jnp.float32)).astype(jnp.bfloat16)
    sent_back = jnp.concatenate([grad_q, grad_kv], 1)
    grad_own = every_device(sent_back)
    out_sum = out_kept.astype(jnp.float32) + swap_cores(out_given).astype(jnp.float32)
    out_sum = out_sum.astype(jnp.bfloat16).reshape(columns, PLANE, shard, -1)

    def summed(values, axis, place_here, stride):
        own_part = lax.dynamic_index_in_dim(values, place_here, axis, False).astype(jnp.float32)
        return own_part, [
            flip(lax.dynamic_index_in_dim(values, place_here ^ step, axis, False), stride * step)
            for step in range(1, values.shape[axis])
        ]

    out_own, out_far = summed(out_sum, 1, spot, 1)
    out_levels = out_own + sum(part.astype(jnp.float32) for part in out_far)
    out_own, out_far = summed(out_levels.astype(jnp.bfloat16), 0, level, PLANE)
    grad_own, out_far = together(grad_own, out_far)
    out_share = out_own + sum(part.astype(jnp.float32) for part in out_far)
    out_small = own_rows(out_share[:, out_cols:])
    grad_tokens, kept, given = project_back(
        core, grad_own, w_heads, normed, tokens, grad_resid, gain_one[None, :], cosine, sine
    )
    kept, given, near_in_w, last_in_w, far_in_w, far_out_w = together(
        kept, given, near_in_w, last_in_w, far_in_w, far_out_w
    )
    grad_w = [
        own_w[matrix]
        + sum(part[matrix].astype(jnp.float32) for part in (near_in_w, last_in_w, far_in_w))
        for matrix in range(2)
    ]
    grad_w.append(own_out_w + near_out_w[0] + far_out_w.astype(jnp.float32))
    mixed = resid + own_mix.reshape(all_rows, width).astype(jnp.float32)
    mixed = (mixed + jnp.sum(all_mix.astype(jnp.float32), 0)).astype(jnp.bfloat16)

    own_share = to_shards(kept, given)
    return (
        mixed.reshape(micro_count, rows, width),
        grad_tokens,
        own_rows(own_share[:, half_cols:])[:, 0],
        own_share[:, :q_cols],
        own_share[:, q_cols : q_cols + kv_cols],
        own_share[:, q_cols + kv_cols : half_cols],
        out_share[:, :out_cols].T,
        out_small[:, experts_all],
        out_small[:, :experts_all],
        grad_w[0][None],
        grad_w[1][None],
        grad_w[2].T[None],
    )


def on_device(*args):
    tokens, w_query, w_key, w_gate = args[0], args[2], args[3], args[8]
    paired = paired_layout(
        lax.axis_size("ep"),
        lax.axis_size("tp"),
        *tokens.shape,
        w_query.shape[1],
        w_key.shape[1],
        w_gate.shape[0],
    )
    return (on_device_paired if paired else on_device_general)(*args)


def solution(mesh):
    in_specs = (
        P(None, ("ep", "tp"), None),
        P("ep"),
        P("ep", "tp"),
        P("ep", "tp"),
        P("ep", "tp"),
        P("tp", "ep"),
        P("ep"),
        P("ep", None),
        P("ep", None, None),
        P("ep", None, None),
        P("ep", None, None),
        P(None, ("ep", "tp"), None),
        P(),
        P(None, ("ep", "tp"), None),
    )
    out_specs = (
        P(None, ("ep", "tp"), None),
        P(None, ("ep", "tp"), None),
        P(("ep", "tp")),
        P("ep", "tp"),
        P("ep", "tp"),
        P("ep", "tp"),
        P("tp", "ep"),
        P(("ep", "tp")),
        P(("ep", "tp"), None),
        P("ep", "tp", None),
        P("ep", "tp", None),
        P("ep", None, "tp"),
    )
    return jax.shard_map(
        on_device, mesh=mesh, in_specs=in_specs, out_specs=out_specs, check_vma=False
    )
```

```python
import functools
import math

import jax
import jax.numpy as jnp
from jax import lax
from jax.experimental import pallas as pl
from jax.experimental.pallas import tpu as pltpu
from jax.sharding import PartitionSpec as P

HEAD_DIM = 64
PIECE = 256
PLANE = 4
LANES = 128
MIB = 1 << 20


EPS = 1e-06
THETA = 10000.0
NEG = -1e30


def rms_scale(values):
    return lax.rsqrt(jnp.mean(values * values, -1, keepdims=True) + EPS)


def angle_tables(positions):
    halves = jnp.arange(HEAD_DIM // 2, dtype=jnp.float32)
    freqs = THETA ** (-2.0 * halves / HEAD_DIM)
    angles = positions.astype(jnp.float32)[:, None] * freqs[None, :]
    return (jnp.cos(angles)[:, None, :], jnp.sin(angles)[:, None, :])


def rotate(values, cosine, sine):
    half_dim = values.shape[-1] // 2
    first_half = values[..., :half_dim]
    second_half = values[..., half_dim:]
    return jnp.concatenate(
        [first_half * cosine - second_half * sine, second_half * cosine + first_half * sine], -1
    )


def piece_index(starts, positions):
    inside = (positions[:, None] >= starts[None, :]) & (
        positions[:, None] < starts[None, :] + PIECE
    )
    numbers = jnp.arange(1, starts.shape[0] + 1, dtype=jnp.int32)
    return jnp.sum(jnp.where(inside, numbers[None, :], 0), -1) - 1


def allowed_mask(query_pos, query_piece, key_pos, key_piece):
    return (key_pos[None, :] <= query_pos[:, None]) | (
        key_piece[None, :] == query_piece[:, None]
    ) & (query_piece[:, None] >= 0)


def to_groups(rows, kv_here, group_size):
    row_total = rows.shape[0]
    return (
        rows.reshape(row_total, kv_here, group_size, HEAD_DIM)
        .transpose(1, 2, 0, 3)
        .reshape(kv_here, group_size * row_total, HEAD_DIM)
    )


def from_groups(grouped, row_total):
    kv_here = grouped.shape[0]
    return (
        grouped.reshape(kv_here, -1, row_total, HEAD_DIM)
        .transpose(2, 0, 1, 3)
        .reshape(row_total, -1)
    )


def tp_major(values, ep_count, tp_count):
    leading = values.shape[0]
    shaped = values.reshape(
        (ep_count, tp_count, leading // (ep_count * tp_count)) + values.shape[1:]
    )
    return jnp.swapaxes(shaped, 0, 1).reshape(values.shape)


def add_all(left_parts, right_parts):
    return tuple((left_part + right_part for left_part, right_part in zip(left_parts, right_parts)))


def reduce_grads(parts, ep_count, tp_count):
    (
        grad_gate_w,
        grad_up_w,
        grad_down_w,
        grad_gain_one,
        grad_gain_two,
        grad_route,
        grad_proj,
        grad_outw,
    ) = parts
    tp_sums = (
        lax.psum_scatter(
            grad_gate_w.astype(jnp.bfloat16), "tp", scatter_dimension=1, tiled=True
        ).astype(jnp.float32),
        lax.psum_scatter(
            grad_up_w.astype(jnp.bfloat16), "tp", scatter_dimension=1, tiled=True
        ).astype(jnp.float32),
        lax.psum_scatter(
            grad_down_w.astype(jnp.bfloat16), "tp", scatter_dimension=2, tiled=True
        ).astype(jnp.float32),
        lax.psum_scatter(
            tp_major(grad_gain_one, ep_count, tp_count).astype(jnp.bfloat16),
            "tp",
            scatter_dimension=0,
            tiled=True,
        ).astype(jnp.float32),
        lax.psum_scatter(
            tp_major(grad_gain_two, ep_count, tp_count).astype(jnp.bfloat16),
            "tp",
            scatter_dimension=0,
            tiled=True,
        ).astype(jnp.float32),
        lax.psum_scatter(
            tp_major(grad_route, ep_count, tp_count).astype(jnp.bfloat16),
            "tp",
            scatter_dimension=0,
            tiled=True,
        ).astype(jnp.float32),
    )
    ep_sums = (
        lax.psum_scatter(
            grad_proj.astype(jnp.bfloat16), "ep", scatter_dimension=0, tiled=True
        ).astype(jnp.float32),
        lax.psum_scatter(
            grad_outw.astype(jnp.bfloat16), "ep", scatter_dimension=1, tiled=True
        ).astype(jnp.float32),
        lax.psum_scatter(
            tp_sums[3].astype(jnp.bfloat16), "ep", scatter_dimension=0, tiled=True
        ).astype(jnp.float32),
        lax.psum_scatter(
            tp_sums[4].astype(jnp.bfloat16), "ep", scatter_dimension=0, tiled=True
        ).astype(jnp.float32),
        lax.psum_scatter(
            tp_sums[5].astype(jnp.bfloat16), "ep", scatter_dimension=0, tiled=True
        ).astype(jnp.float32),
    )
    return (
        tp_sums[0],
        tp_sums[1],
        tp_sums[2],
        ep_sums[2],
        ep_sums[3],
        ep_sums[4],
        ep_sums[0],
        ep_sums[1],
    )


def on_device_general(
    tokens,
    gain_attn,
    w_query,
    w_key,
    w_value,
    w_output,
    gain_moe,
    w_router,
    w_gate,
    w_up,
    w_down,
    routes,
    piece_starts,
    cotangent,
):
    ep_count = lax.axis_size("ep")
    tp_count = lax.axis_size("tp")
    micro_count, slice_rows, width = tokens.shape
    span_rows = slice_rows * tp_count
    seq_len = span_rows * ep_count
    q_cols = w_query.shape[1]
    kv_cols = w_key.shape[1]
    kv_here = kv_cols // HEAD_DIM
    group_size = q_cols // kv_cols
    query_rows = group_size * span_rows
    experts_here = w_gate.shape[0]
    experts_all = experts_here * ep_count
    top_count = routes.shape[2]
    capacity = max(2, slice_rows * top_count * 3 // (2 * experts_all))
    expert_rows = ep_count * capacity
    score_scale = HEAD_DIM ** (-0.5)
    key_block = math.gcd(seq_len, 512)
    block_count = seq_len // key_block
    local_pos = lax.axis_index("ep") * span_rows + jnp.arange(span_rows, dtype=jnp.int32)
    all_pos = jnp.arange(seq_len, dtype=jnp.int32)
    row_pos = jnp.tile(local_pos, group_size)
    cosine, sine = angle_tables(local_pos)
    slot_ids = jnp.arange(experts_all * capacity, dtype=jnp.int32)
    expert_ids = jnp.arange(experts_all, dtype=jnp.int32)
    gathered = (
        lax.all_gather(gain_attn, "ep", axis=0, tiled=True),
        lax.all_gather(w_query, "ep", axis=0, tiled=True),
        lax.all_gather(w_key, "ep", axis=0, tiled=True),
        lax.all_gather(w_value, "ep", axis=0, tiled=True),
        lax.all_gather(w_output, "ep", axis=1, tiled=True),
        lax.all_gather(gain_moe, "ep", axis=0, tiled=True),
        lax.all_gather(w_router, "ep", axis=0, tiled=True),
    )
    gain_one = gathered[0].astype(jnp.float32)
    w_proj = jnp.concatenate([gathered[1], gathered[2], gathered[3]], 1)
    w_out_full = gathered[4]
    gain_two = gathered[5].astype(jnp.float32)
    w_route_full = gathered[6]
    totals = None
    mixed_rows = []
    grad_rows = []
    for micro_index in range(micro_count):
        starts = piece_starts[micro_index]
        key_pieces = piece_index(starts, all_pos)
        row_piece = jnp.tile(piece_index(starts, local_pos), group_size)
        x_rows = tokens[micro_index].astype(jnp.float32)
        scale_one = rms_scale(x_rows)
        normed = (x_rows * scale_one * gain_one).astype(jnp.bfloat16)
        normed_all = lax.all_gather(normed, "tp", axis=0, tiled=True)
        projected = jnp.dot(normed_all, w_proj, preferred_element_type=jnp.float32)
        queries = rotate(
            projected[:, :q_cols].reshape(span_rows, -1, HEAD_DIM), cosine, sine
        ).astype(jnp.bfloat16)
        q_grouped = to_groups(queries.reshape(span_rows, q_cols), kv_here, group_size)
        keys_own = (
            rotate(
                projected[:, q_cols : q_cols + kv_cols].reshape(span_rows, kv_here, HEAD_DIM),
                cosine,
                sine,
            )
            .astype(jnp.bfloat16)
            .reshape(span_rows, kv_cols)
        )
        values_own = projected[:, q_cols + kv_cols :].astype(jnp.bfloat16)
        keys_all, values_all = (
            lax.all_gather(keys_own, "ep", axis=0, tiled=True),
            lax.all_gather(values_own, "ep", axis=0, tiled=True),
        )

        def block_scores(first_row, block_size):
            key_blk = lax.dynamic_slice_in_dim(keys_all, first_row, block_size, 0).reshape(
                block_size, kv_here, HEAD_DIM
            )
            value_blk = lax.dynamic_slice_in_dim(values_all, first_row, block_size, 0).reshape(
                block_size, kv_here, HEAD_DIM
            )
            key_pos = first_row + jnp.arange(block_size, dtype=jnp.int32)
            piece_blk = lax.dynamic_slice_in_dim(key_pieces, first_row, block_size, 0)
            allowed = allowed_mask(row_pos, row_piece, key_pos, piece_blk)[None]
            scores = (
                jnp.einsum("hrd,khd->hrk", q_grouped, key_blk, preferred_element_type=jnp.float32)
                * score_scale
            )
            return (scores, allowed, key_blk, value_blk)

        def forward_step(block_index, running):
            run_max, run_sum, run_acc = running
            scores, allowed, key_blk, value_blk = block_scores(block_index * key_block, key_block)
            scores = jnp.where(allowed, scores, NEG)
            new_max = jnp.maximum(run_max, jnp.max(scores, -1))
            weights = jnp.where(allowed, jnp.exp(scores - new_max[..., None]), 0.0)
            factor = jnp.exp(run_max - new_max)
            run_sum = run_sum * factor + jnp.sum(weights, -1)
            run_acc = run_acc * factor[..., None] + jnp.einsum(
                "hrk,khd->hrd",
                weights.astype(jnp.bfloat16),
                value_blk,
                preferred_element_type=jnp.float32,
            )
            return (new_max, run_sum, run_acc)

        start_state = (
            jnp.full((kv_here, query_rows), NEG, jnp.float32),
            jnp.zeros((kv_here, query_rows), jnp.float32),
            jnp.zeros((kv_here, query_rows, HEAD_DIM), jnp.float32),
        )
        run_max, run_sum, run_acc = lax.fori_loop(0, block_count, forward_step, start_state)
        log_total = run_max + jnp.log(run_sum)
        attended_f = run_acc / run_sum[..., None]
        attended = from_groups(attended_f.astype(jnp.bfloat16), span_rows)
        partial_attn = jnp.dot(attended, w_out_full, preferred_element_type=jnp.float32)
        attn_rows = lax.psum_scatter(
            partial_attn.astype(jnp.bfloat16), "tp", scatter_dimension=0, tiled=True
        ).astype(jnp.float32)
        resid = x_rows + attn_rows
        scale_two = rms_scale(resid)
        normed_two = (resid * scale_two * gain_two).astype(jnp.bfloat16)
        logits = jnp.dot(normed_two, w_route_full, preferred_element_type=jnp.float32)
        route_rows = routes[micro_index]
        route_hot = (route_rows[:, :, None] == expert_ids[None, None, :]).astype(jnp.float32)
        picked = jnp.sum(route_hot * logits[:, None, :], -1)
        highest = jnp.max(picked, -1, keepdims=True)
        raised = jnp.exp(picked - highest)
        gates = raised / jnp.sum(raised, -1, keepdims=True)
        flat_hot = route_hot.reshape(-1, experts_all)
        earlier = jnp.cumsum(flat_hot, 0) - flat_hot
        slot_of = jnp.sum(earlier * flat_hot, -1).astype(jnp.int32)
        target = route_rows.reshape(-1) * capacity + slot_of
        place_pairs = slot_ids[:, None] == target[None, :]
        place_pairs_b = place_pairs.astype(jnp.bfloat16)
        place_tokens = jnp.any(place_pairs.reshape(-1, slice_rows, top_count), -1).astype(
            jnp.bfloat16
        )
        send_rows = (
            jnp.dot(place_tokens, normed_two, preferred_element_type=jnp.float32)
            .astype(jnp.bfloat16)
            .reshape(ep_count, experts_here, capacity, width)
        )
        received = lax.all_to_all(send_rows, "ep", split_axis=0, concat_axis=0, tiled=True)
        expert_in = jnp.swapaxes(received, 0, 1).reshape(experts_here, expert_rows, width)
        gate_pre = jnp.einsum("erd,edf->erf", expert_in, w_gate, preferred_element_type=jnp.float32)
        up_pre = jnp.einsum("erd,edf->erf", expert_in, w_up, preferred_element_type=jnp.float32)
        sigmoid_val = jax.nn.sigmoid(gate_pre)
        silu_val = gate_pre * sigmoid_val
        hidden = (silu_val * up_pre).astype(jnp.bfloat16)
        expert_out = jnp.einsum(
            "erf,efd->erd", hidden, w_down, preferred_element_type=jnp.float32
        ).astype(jnp.bfloat16)
        returned = lax.all_to_all(
            jnp.swapaxes(expert_out.reshape(experts_here, ep_count, capacity, width), 0, 1),
            "ep",
            split_axis=0,
            concat_axis=0,
            tiled=True,
        )
        slot_rows = returned.reshape(-1, width)
        picked_rows = jnp.einsum(
            "sn,sd->nd", place_pairs_b, slot_rows, preferred_element_type=jnp.float32
        ).reshape(slice_rows, top_count, width)
        mixture = jnp.einsum("tk,tkd->td", gates, picked_rows)
        mixed_rows.append((resid + mixture).astype(jnp.bfloat16))
        grad_out = cotangent[micro_index].astype(jnp.float32)
        grad_gates = jnp.einsum("tkd,td->tk", picked_rows, grad_out)
        weighted = (
            (gates[:, :, None] * grad_out[:, None, :]).astype(jnp.bfloat16).reshape(-1, width)
        )
        grad_slots = (
            jnp.dot(place_pairs_b, weighted, preferred_element_type=jnp.float32)
            .astype(jnp.bfloat16)
            .reshape(ep_count, experts_here, capacity, width)
        )
        grad_recv = lax.all_to_all(grad_slots, "ep", split_axis=0, concat_axis=0, tiled=True)
        grad_expert = jnp.swapaxes(grad_recv, 0, 1).reshape(experts_here, expert_rows, width)
        grad_hidden = jnp.einsum(
            "erd,efd->erf", grad_expert, w_down, preferred_element_type=jnp.float32
        )
        grad_down_w = jnp.einsum(
            "erf,erd->efd", hidden, grad_expert, preferred_element_type=jnp.float32
        )
        silu_slope = sigmoid_val * (1.0 + gate_pre * (1.0 - sigmoid_val))
        grad_gate_pre = (grad_hidden * up_pre * silu_slope).astype(jnp.bfloat16)
        grad_up_pre = (grad_hidden * silu_val).astype(jnp.bfloat16)
        grad_gate_w = jnp.einsum(
            "erd,erf->edf", expert_in, grad_gate_pre, preferred_element_type=jnp.float32
        )
        grad_up_w = jnp.einsum(
            "erd,erf->edf", expert_in, grad_up_pre, preferred_element_type=jnp.float32
        )
        grad_copy = (
            jnp.einsum("erf,edf->erd", grad_gate_pre, w_gate, preferred_element_type=jnp.float32)
            + jnp.einsum("erf,edf->erd", grad_up_pre, w_up, preferred_element_type=jnp.float32)
        ).astype(jnp.bfloat16)
        grad_back = lax.all_to_all(
            jnp.swapaxes(grad_copy.reshape(experts_here, ep_count, capacity, width), 0, 1),
            "ep",
            split_axis=0,
            concat_axis=0,
            tiled=True,
        ).reshape(-1, width)
        grad_spread = gates * (grad_gates - jnp.sum(gates * grad_gates, -1, keepdims=True))
        grad_logits = jnp.einsum("tk,tke->te", grad_spread, route_hot).astype(jnp.bfloat16)
        grad_normed_two = jnp.einsum(
            "st,sd->td", place_tokens, grad_back, preferred_element_type=jnp.float32
        ) + jnp.einsum("te,de->td", grad_logits, w_route_full, preferred_element_type=jnp.float32)
        grad_route = jnp.einsum(
            "td,te->de", normed_two, grad_logits, preferred_element_type=jnp.float32
        )
        gained_two = grad_normed_two * gain_two
        grad_gain_two = jnp.sum(grad_normed_two * resid * scale_two, 0)
        grad_resid = (
            grad_out
            + scale_two * gained_two
            - resid * scale_two**3 * jnp.mean(resid * gained_two, -1, keepdims=True)
        )
        grad_attn = lax.all_gather(grad_resid.astype(jnp.bfloat16), "tp", axis=0, tiled=True)
        grad_outw = jnp.einsum("cq,cd->qd", attended, grad_attn, preferred_element_type=jnp.float32)
        grad_att_rows = jnp.einsum(
            "cd,qd->cq", grad_attn, w_out_full, preferred_element_type=jnp.float32
        ).astype(jnp.bfloat16)
        grad_grouped = to_groups(grad_att_rows, kv_here, group_size)
        delta = jnp.sum(grad_grouped.astype(jnp.float32) * attended_f, -1)

        def block_grads(first_row, block_size):
            scores, allowed, key_blk, value_blk = block_scores(first_row, block_size)
            probs = jnp.where(allowed, jnp.exp(scores - log_total[..., None]), 0.0)
            grad_probs = jnp.einsum(
                "hrd,khd->hrk", grad_grouped, value_blk, preferred_element_type=jnp.float32
            )
            grad_scores = (probs * (grad_probs - delta[..., None])).astype(jnp.bfloat16)
            return (probs, grad_scores, key_blk)

        def key_side(first_row, block_size):
            probs, grad_scores, key_blk = block_grads(first_row, block_size)
            grad_keys = (
                jnp.einsum(
                    "hrk,hrd->khd", grad_scores, q_grouped, preferred_element_type=jnp.float32
                ).reshape(block_size, kv_cols)
                * score_scale
            )
            grad_values = jnp.einsum(
                "hrk,hrd->khd",
                probs.astype(jnp.bfloat16),
                grad_grouped,
                preferred_element_type=jnp.float32,
            ).reshape(block_size, kv_cols)
            return (jnp.concatenate([grad_keys, grad_values], 1), grad_scores, key_blk)

        query_zero = jnp.zeros((kv_here, query_rows, HEAD_DIM), jnp.float32)

        def backward_step(block_index, running):
            grad_query, grad_kv = running
            first_row = block_index * key_block
            kv_terms, grad_scores, key_blk = key_side(first_row, key_block)
            grad_query = grad_query + jnp.einsum(
                "hrk,khd->hrd", grad_scores, key_blk, preferred_element_type=jnp.float32
            )
            grad_kv = lax.dynamic_update_slice_in_dim(grad_kv, kv_terms, first_row, 0)
            return (grad_query, grad_kv)

        grad_query, grad_kv = lax.fori_loop(
            0,
            block_count,
            backward_step,
            (query_zero, jnp.zeros((seq_len, 2 * kv_cols), jnp.float32)),
        )
        grad_kv_own = lax.psum_scatter(
            grad_kv.astype(jnp.bfloat16), "ep", scatter_dimension=0, tiled=True
        ).astype(jnp.float32)
        grad_query_rows = from_groups(grad_query * score_scale, span_rows).reshape(
            span_rows, -1, HEAD_DIM
        )
        grad_query_raw = (
            rotate(grad_query_rows, cosine, -sine).astype(jnp.bfloat16).reshape(span_rows, q_cols)
        )
        grad_key_raw = (
            rotate(grad_kv_own[:, :kv_cols].reshape(span_rows, kv_here, HEAD_DIM), cosine, -sine)
            .astype(jnp.bfloat16)
            .reshape(span_rows, kv_cols)
        )
        grad_value_raw = grad_kv_own[:, kv_cols:].astype(jnp.bfloat16)
        grad_proj_rows = jnp.concatenate([grad_query_raw, grad_key_raw, grad_value_raw], 1)
        grad_proj = jnp.einsum(
            "cd,cp->dp", normed_all, grad_proj_rows, preferred_element_type=jnp.float32
        )
        grad_normed_part = jnp.einsum(
            "cp,dp->cd", grad_proj_rows, w_proj, preferred_element_type=jnp.float32
        )
        grad_normed = lax.psum_scatter(
            grad_normed_part.astype(jnp.bfloat16), "tp", scatter_dimension=0, tiled=True
        ).astype(jnp.float32)
        gained_one = grad_normed * gain_one
        grad_gain_one = jnp.sum(grad_normed * x_rows * scale_one, 0)
        grad_rows.append(
            grad_resid
            + scale_one * gained_one
            - x_rows * scale_one**3 * jnp.mean(x_rows * gained_one, -1, keepdims=True)
        )
        parts = (
            grad_gate_w,
            grad_up_w,
            grad_down_w,
            grad_gain_one,
            grad_gain_two,
            grad_route,
            grad_proj,
            grad_outw,
        )
        reduced = reduce_grads(parts, ep_count, tp_count)
        totals = reduced if totals is None else add_all(totals, reduced)
    grad_qkv = totals[6]
    return (
        jnp.stack(mixed_rows),
        jnp.stack(grad_rows),
        totals[3],
        grad_qkv[:, :q_cols],
        grad_qkv[:, q_cols : q_cols + kv_cols],
        grad_qkv[:, q_cols + kv_cols :],
        totals[7],
        totals[4],
        totals[5],
        totals[0],
        totals[1],
        totals[2],
    )


RAISE_AT = 40.0


def dot_f32(left, right, left_dim, right_dim):
    return lax.dot_general(
        left, right, (((left_dim,), (right_dim,)), ((), ())), preferred_element_type=jnp.float32
    )


def at_rows(first_row, count):
    return pl.ds(pl.multiple_of(first_row, count), count)


def whole_vmem():
    return pl.BlockSpec(memory_space=pltpu.VMEM)


def attend_kernel(
    tp_ref, own_ref, other_ref, limit_ref, out_ref, out_f_ref, log_ref,
    keys, queries, values, highest, total,
    *, query_block, key_block, chain
):
    core = tp_ref[0]
    blocks, _, rows = own_ref.shape
    seq_len = blocks * rows
    chains = query_block // chain

    def fill(block, _):
        cols = at_rows(block * rows, rows)
        first, second = own_ref[block, HEAD_DIM:, :], other_ref[block]
        key_rows = jnp.where(core == 0, first, second).astype(jnp.float32)
        queries[:, cols] = own_ref[block, :HEAD_DIM, :]
        values[:HEAD_DIM, cols] = jnp.where(core == 0, second, first)
        values[HEAD_DIM:, cols] = jnp.ones((16, rows), jnp.bfloat16)
        keys[cols, :] = (key_rows * HEAD_DIM ** (-0.5)).T.astype(jnp.bfloat16)
        return 0

    lax.fori_loop(0, blocks, fill, 0)
    keys[seq_len:, :] = jnp.zeros((rows, HEAD_DIM), jnp.bfloat16)
    values[:, seq_len:] = jnp.zeros((HEAD_DIM + 16, rows), jnp.bfloat16)

    def diagonal_step(index, _):
        firsts = [pl.multiple_of((index * chains + part) * chain, chain) for part in range(chains)]
        spans = [pl.ds(first, chain + rows) for first in firsts]
        scores = [
            dot_f32(keys[span, :], queries[:, pl.ds(first, chain)], 1, 0)
            for first, span in zip(firsts, spans)
        ]
        for first, span, score in zip(firsts, spans, scores):
            here = pl.ds(first, chain)
            key_pos = first + lax.broadcasted_iota(jnp.int32, score.shape, 0)
            score = jnp.where(key_pos <= limit_ref[:, here], score, NEG)
            most = jnp.max(score, 0, keepdims=True)
            highest[:, here] = most
            total[:, here] = dot_f32(
                values[:, span], jnp.exp(score - most).astype(jnp.bfloat16), 1, 0
            )
        return 0

    lax.fori_loop(0, seq_len // query_block, diagonal_step, 0)

    def earlier_keys(span, firsts):
        terms, over = [], []
        for first in firsts:
            here = pl.ds(first, chain)
            score = dot_f32(keys[span, :], queries[:, here], 1, 0)
            most = highest[:, here]
            over.append(jnp.max(score, 0, keepdims=True) - most)
            weights = jnp.exp(score - most).astype(jnp.bfloat16)
            terms.append(dot_f32(values[:, span], weights, 1, 0))
        most_over = jnp.max(functools.reduce(jnp.maximum, over))

        @pl.when(most_over <= RAISE_AT)
        def _():
            for first, term in zip(firsts, terms):
                total[:, pl.ds(first, chain)] += term

        @pl.when(most_over > RAISE_AT)
        def _():
            for first in firsts:
                here = pl.ds(first, chain)
                score = dot_f32(keys[span, :], queries[:, here], 1, 0)
                before = highest[:, here]
                after_all = jnp.maximum(before, jnp.max(score, 0, keepdims=True))
                weights = jnp.exp(score - after_all).astype(jnp.bfloat16)
                highest[:, here] = after_all
                total[:, here] = total[:, here] * jnp.exp(before - after_all) + dot_f32(
                    values[:, span], weights, 1, 0
                )

    def query_step(index, _):
        first = index * query_block
        firsts = [pl.multiple_of(first + part * chain, chain) for part in range(chains)]

        def full_step(step, _):
            earlier_keys(at_rows(step * key_block, key_block), firsts)
            return 0

        lax.fori_loop(0, first // key_block, full_step, 0)
        for part in range(1, chains):
            earlier_keys(pl.ds(firsts[part - 1], chain), firsts[part:])
        for piece in range(query_block // rows):
            here = at_rows(first + piece * rows, rows)
            row_sum = total[HEAD_DIM : HEAD_DIM + 1, here]
            result = total[:HEAD_DIM, here] / row_sum
            block = index * (query_block // rows) + piece
            out_ref[block] = result.astype(jnp.bfloat16)
            out_f_ref[block] = result
            log_ref[:, here] = highest[:, here] + jnp.log(row_sum)
        return 0

    lax.fori_loop(0, seq_len // query_block, query_step, 0)


def attend(core, own, other, limit):
    blocks, _, rows = own.shape
    seq_len = blocks * rows
    query_block = math.gcd(seq_len, 2048)
    key_block = math.gcd(query_block, 2048)
    block_shape = (blocks, HEAD_DIM, rows)
    return pl.pallas_call(
        functools.partial(
            attend_kernel,
            query_block=query_block,
            key_block=key_block,
            chain=math.gcd(query_block, 512),
        ),
        out_shape=(
            jax.ShapeDtypeStruct(block_shape, jnp.bfloat16),
            jax.ShapeDtypeStruct(block_shape, jnp.float32),
            jax.ShapeDtypeStruct((1, seq_len), jnp.float32),
        ),
        in_specs=[pl.BlockSpec(memory_space=pltpu.SMEM)] + [whole_vmem()] * 3,
        out_specs=(whole_vmem(),) * 3,
        scratch_shapes=[
            pltpu.VMEM((seq_len + rows, HEAD_DIM), jnp.bfloat16),
            pltpu.VMEM((HEAD_DIM, seq_len), jnp.bfloat16),
            pltpu.VMEM((HEAD_DIM + 16, seq_len + rows), jnp.bfloat16),
            pltpu.VMEM((1, seq_len), jnp.float32),
            pltpu.VMEM((HEAD_DIM + 16, seq_len), jnp.float32),
        ],
        cost_estimate=pl.CostEstimate(
            flops=seq_len * seq_len * 512, bytes_accessed=8 * MIB, transcendentals=0
        ),
        compiler_params=pltpu.CompilerParams(vmem_limit_bytes=56 * MIB),
        name="attend",
    )(core, own, other, limit)


def split_three(values):
    high = values.astype(jnp.bfloat16).astype(jnp.float32)
    middle = (values - high).astype(jnp.bfloat16).astype(jnp.float32)
    return high, middle, values - high - middle


def three_parts(values):
    high, middle, low = split_three(values)
    row = lax.broadcasted_iota(jnp.int32, (16, values.shape[1]), 0)
    return jnp.where(
        row == 0, high, jnp.where(row == 1, middle, jnp.where(row == 2, low, 0.0))
    )


def attend_back_kernel(
    tp_ref, own_ref, other_ref, limit_ref, out_f_ref, log_ref, grad_ref,
    grad_q_ref, keep_ref, send_ref,
    queries, queries_t, keys_t, values_t, grads, grads_t, grad_k, grad_v, grad_q,
    *, query_block, key_block, chain
):
    core = tp_ref[0]
    blocks, _, rows = own_ref.shape
    seq_len = blocks * rows
    chains = query_block // chain

    def fill(block, _):
        cols = at_rows(block * rows, rows)
        first, second = own_ref[block, HEAD_DIM:, :], other_ref[block]
        key_rows = jnp.where(core == 0, first, second).astype(jnp.float32)
        key_rows = key_rows * HEAD_DIM ** (-0.5)
        query, grad = own_ref[block, :HEAD_DIM, :], grad_ref[block]
        grad_f = grad.astype(jnp.float32)
        delta = jnp.sum(grad_f * out_f_ref[block], 0, keepdims=True)
        ones = jnp.ones((16, rows), jnp.bfloat16)
        query_parts = [query.astype(jnp.float32), three_parts(-log_ref[:, cols])]
        queries[cols, :] = jnp.concatenate(query_parts, 0).T.astype(jnp.bfloat16)
        queries_t[:, cols] = query
        keys_t[:HEAD_DIM, cols] = key_rows.astype(jnp.bfloat16)
        keys_t[HEAD_DIM:, cols] = ones
        values_t[:HEAD_DIM, cols] = jnp.where(core == 0, second, first)
        values_t[HEAD_DIM:, cols] = ones
        grads[cols, :] = jnp.concatenate([grad_f, three_parts(-delta)], 0).T.astype(jnp.bfloat16)
        grads_t[:, cols] = grad
        grad_k[:, cols] = jnp.zeros((HEAD_DIM, rows), jnp.float32)
        grad_v[:, cols] = jnp.zeros((HEAD_DIM, rows), jnp.float32)
        return 0

    lax.fori_loop(0, blocks, fill, 0)

    def tile(query_rows, here, key_cols, key_first):
        probs = jnp.exp(dot_f32(queries[query_rows, :], keys_t[:, key_cols], 1, 0))
        if key_first is not None:
            limit = limit_ref[:, query_rows].astype(jnp.float32)
            limit = jnp.broadcast_to(limit, (8, limit.shape[1])).T[:, :1]
            key_pos = key_first + lax.broadcasted_iota(jnp.int32, probs.shape, 1)
            probs = jnp.where(key_pos.astype(jnp.float32) <= limit, probs, 0.0)
        grad_probs = dot_f32(grads[query_rows, :], values_t[:, key_cols], 1, 0)
        grad_scores = (probs * grad_probs).astype(jnp.bfloat16)
        grad_v[:, key_cols] += dot_f32(grads_t[:, query_rows], probs.astype(jnp.bfloat16), 1, 0)
        grad_k[:, key_cols] += dot_f32(queries_t[:, query_rows], grad_scores, 1, 0)
        grad_q[:, here] += dot_f32(keys_t[:HEAD_DIM, key_cols], grad_scores, 1, 1)

    def query_step(index, _):
        first = index * query_block
        grad_q[...] = jnp.zeros_like(grad_q)

        def full_step(step, _):
            tile(
                at_rows(first, query_block),
                slice(0, query_block),
                at_rows(step * key_block, key_block),
                None,
            )
            return 0

        lax.fori_loop(0, first // key_block, full_step, 0)
        for low in range(0, query_block, chain):
            here = pl.multiple_of(first + low, chain)
            if low:
                tile(
                    pl.ds(here, query_block - low),
                    slice(low, query_block),
                    pl.ds(pl.multiple_of(here - chain, chain), chain),
                    None,
                )
            tile(pl.ds(here, chain), slice(low, low + chain), pl.ds(here, chain), here)
            tile(
                at_rows(here + chain - rows, rows),
                slice(low + chain - rows, low + chain),
                at_rows(jnp.minimum(here + chain, seq_len - rows), rows),
                here + chain,
            )
        for piece in range(query_block // rows):
            here = grad_q[:, piece * rows : (piece + 1) * rows]
            grad_q_ref[index * (query_block // rows) + piece] = here.astype(jnp.bfloat16)
        return 0

    lax.fori_loop(0, seq_len // query_block, query_step, 0)

    def finish(block, _):
        cols = at_rows(block * rows, rows)
        key_part = grad_k[:, cols] * HEAD_DIM ** (-0.5)
        value_part = grad_v[:, cols]
        keep_ref[block] = jnp.where(core == 0, key_part, value_part)
        send_ref[block] = jnp.where(core == 0, value_part, key_part).astype(jnp.bfloat16)
        return 0

    lax.fori_loop(0, blocks, finish, 0)


def attend_back(core, own, other, limit, out_f, log_total, grad):
    blocks, _, rows = own.shape
    seq_len = blocks * rows
    query_block = math.gcd(seq_len, 2048)
    key_block = math.gcd(query_block, 1024)
    block_shape = (blocks, HEAD_DIM, rows)
    wide = HEAD_DIM + 16
    return pl.pallas_call(
        functools.partial(
            attend_back_kernel,
            query_block=query_block,
            key_block=key_block,
            chain=math.gcd(query_block, 512),
        ),
        out_shape=(
            jax.ShapeDtypeStruct(block_shape, jnp.bfloat16),
            jax.ShapeDtypeStruct(block_shape, jnp.float32),
            jax.ShapeDtypeStruct(block_shape, jnp.bfloat16),
        ),
        in_specs=[pl.BlockSpec(memory_space=pltpu.SMEM)] + [whole_vmem()] * 6,
        out_specs=(whole_vmem(),) * 3,
        scratch_shapes=[
            pltpu.VMEM((seq_len, wide), jnp.bfloat16),
            pltpu.VMEM((HEAD_DIM, seq_len), jnp.bfloat16),
            pltpu.VMEM((wide, seq_len), jnp.bfloat16),
            pltpu.VMEM((wide, seq_len), jnp.bfloat16),
            pltpu.VMEM((seq_len, wide), jnp.bfloat16),
            pltpu.VMEM((HEAD_DIM, seq_len), jnp.bfloat16),
            pltpu.VMEM((HEAD_DIM, seq_len), jnp.float32),
            pltpu.VMEM((HEAD_DIM, seq_len), jnp.float32),
            pltpu.VMEM((HEAD_DIM, query_block), jnp.float32),
        ],
        cost_estimate=pl.CostEstimate(
            flops=seq_len * seq_len * 1024, bytes_accessed=12 * MIB, transcendentals=0
        ),
        compiler_params=pltpu.CompilerParams(vmem_limit_bytes=60 * MIB),
        name="attend_back",
    )(core, own, other, limit, out_f, log_total, grad)


def project_kernel(*refs, count):
    place_ref, x_ref, cosine_ref, sine_ref = refs[:4]
    mine_refs, other_refs = refs[4 : 4 + count], refs[4 + count : 4 + 2 * count]
    normed_ref, sent_ref, heads_ref, small_ref = refs[4 + 2 * count :]
    core, level, spot = place_ref[0], place_ref[1], place_ref[2]
    micro_count, rows, width = x_ref.shape
    columns, shard, _ = mine_refs[0].shape
    half_cols = heads_ref.shape[2]
    half_dim = HEAD_DIM // 2
    units = half_cols // (2 * HEAD_DIM)
    kv_heads = units // 2
    for step in range(count):
        for up in range(columns):
            here = at_rows(((level ^ up) * count + (spot ^ step)) * shard, shard)
            heads_ref[core, here, :] = mine_refs[step][up, :, :half_cols]
            heads_ref[1 - core, here, :] = other_refs[step][up, :, :half_cols]
            small_ref[here, :] = mine_refs[step][up, :, half_cols:]
    cosine, sine = cosine_ref[...], sine_ref[...]
    gain_row = small_ref.shape[1] // 2
    gain = small_ref[...].astype(jnp.float32).T[gain_row : gain_row + 1]

    def rotated(heads):
        first, second = heads[:half_dim], heads[half_dim:]
        return jnp.concatenate(
            [first * cosine - second * sine, second * cosine + first * sine], 0
        ).astype(jnp.bfloat16)

    for micro in range(micro_count):
        x = x_ref[micro].astype(jnp.float32)
        scale = lax.rsqrt(jnp.mean(x * x, -1, keepdims=True) + EPS)
        normed = (x * scale * gain).astype(jnp.bfloat16)
        normed_ref[micro * rows : (micro + 1) * rows, :] = normed
        for part in range(2):
            heads = dot_f32(normed, heads_ref[part], 1, 0).T
            for unit in range(units):
                first = unit * HEAD_DIM
                paired = (units + unit // 2 + unit % 2 * kv_heads) * HEAD_DIM
                block = (micro * 2 + part) * units + unit
                second = heads[paired : paired + HEAD_DIM]
                sent_ref[block, :HEAD_DIM, :] = rotated(heads[first : first + HEAD_DIM])
                sent_ref[block, HEAD_DIM:, :] = (
                    rotated(second) if unit % 2 == 0 else second.astype(jnp.bfloat16)
                )


def project(place, x, cosine, sine, mine, other, devices):
    micro_count, rows, width = x.shape
    half_cols = mine[0].shape[2] - LANES
    return pl.pallas_call(
        functools.partial(project_kernel, count=len(mine)),
        out_shape=(
            jax.ShapeDtypeStruct((micro_count * rows, width), jnp.bfloat16),
            jax.ShapeDtypeStruct((devices, 2 * HEAD_DIM, rows), jnp.bfloat16),
            jax.ShapeDtypeStruct((2, width, half_cols), jnp.bfloat16),
            jax.ShapeDtypeStruct((width, LANES), jnp.bfloat16),
        ),
        in_specs=[pl.BlockSpec(memory_space=pltpu.SMEM)]
        + [whole_vmem()] * (3 + len(mine) + len(other)),
        out_specs=(whole_vmem(),) * 4,
        compiler_params=pltpu.CompilerParams(vmem_limit_bytes=48 * MIB),
        name="project",
    )(place, x, cosine, sine, *mine, *other)


def project_back_kernel(
    tp_ref, grad_ref, heads_ref, normed_ref, x_ref, grad_resid_ref, gain_ref, cosine_ref,
    sine_ref, grad_x_ref, kept_ref, given_ref, grad_rows
):
    core = tp_ref[0]
    micro_count, rows, width = x_ref.shape
    half_cols = heads_ref.shape[2]
    half_dim = HEAD_DIM // 2
    units = half_cols // (2 * HEAD_DIM)
    cosine, sine = cosine_ref[...], sine_ref[...]

    def turned_back(heads):
        first, second = heads[:half_dim].astype(jnp.float32), heads[half_dim:].astype(jnp.float32)
        return [first * cosine + second * sine, second * cosine - first * sine]

    for micro in range(micro_count):
        for part in range(2):
            first_block = (micro * 2 + part) * units
            pieces = []
            for block in range(first_block, first_block + units):
                pieces += turned_back(grad_ref[block, :HEAD_DIM, :])
            for block in range(first_block, first_block + units, 2):
                pieces += turned_back(grad_ref[block, HEAD_DIM:, :])
            for block in range(first_block + 1, first_block + units, 2):
                pieces.append(grad_ref[block, HEAD_DIM:, :].astype(jnp.float32))
            grad_rows[part, micro * rows : (micro + 1) * rows, :] = (
                jnp.concatenate(pieces, 0).T.astype(jnp.bfloat16)
            )
    gain = gain_ref[...]
    grad_gain = jnp.zeros((1, width), jnp.float32)
    for micro in range(micro_count):
        here = slice(micro * rows, (micro + 1) * rows)
        grad_normed = dot_f32(grad_rows[0, here, :], heads_ref[0], 1, 1) + dot_f32(
            grad_rows[1, here, :], heads_ref[1], 1, 1
        )
        x = x_ref[micro].astype(jnp.float32)
        scale = lax.rsqrt(jnp.mean(x * x, -1, keepdims=True) + EPS)
        gained = grad_normed * gain
        grad_gain = grad_gain + jnp.sum(grad_normed * x * scale, 0, keepdims=True)
        grad_x_ref[micro] = (
            grad_resid_ref[here, :]
            + scale * gained
            - x * scale**3 * jnp.mean(x * gained, -1, keepdims=True)
        )
    normed_t = normed_ref[...].T
    gain_cols = jnp.broadcast_to(grad_gain, (LANES, width)).T.astype(jnp.bfloat16)
    for ref, part in ((kept_ref, core), (given_ref, 1 - core)):
        ref[:, :half_cols] = dot_f32(normed_t, grad_rows[part], 1, 0).astype(jnp.bfloat16)
        ref[:, half_cols:] = gain_cols


def project_back(core, grad_own, heads, normed, x, grad_resid, gain, cosine, sine):
    micro_count, rows, width = x.shape
    half_cols = heads.shape[2]
    share = jax.ShapeDtypeStruct((width, half_cols + LANES), jnp.bfloat16)
    return pl.pallas_call(
        project_back_kernel,
        out_shape=(jax.ShapeDtypeStruct(x.shape, jnp.float32), share, share),
        in_specs=[pl.BlockSpec(memory_space=pltpu.SMEM)] + [whole_vmem()] * 8,
        out_specs=(whole_vmem(),) * 3,
        scratch_shapes=[pltpu.VMEM((2, micro_count * rows, half_cols), jnp.bfloat16)],
        compiler_params=pltpu.CompilerParams(vmem_limit_bytes=56 * MIB),
        name="project_back",
    )(core, grad_own, heads, normed, x, grad_resid, gain, cosine, sine)


def experts_kernel(*refs, slots, first_call, pieces, piece_count, spread, spread_x):
    place_ref, refs = refs[0], refs[1:]
    x_refs, dy_refs = refs[:slots], refs[slots : 2 * slots]
    w_route_ref, weight_refs = refs[2 * slots], refs[2 * slots + 1 : 2 * slots + 1 + piece_count]
    refs = refs[2 * slots + 1 + piece_count :]
    if not first_call:
        before_refs, refs = refs[:3], refs[3:]
    x_outs = 1 if spread_x else slots
    mix_ref, grad_x_refs, refs = refs[0], refs[1 : 1 + x_outs], refs[1 + x_outs :]
    keep_ref, send_in_ref, send_out_ref = refs[:3]
    (
        x_all, x_t, dy_all, dy_t, gates, grad_gates, mix_sum, grad_x_sum, grad_w, weights, sems,
        hidden, grad_gate_pre, grad_up_pre,
    ) = refs[3:]
    expert, expert_count = pl.program_id(0), pl.num_programs(0)
    rows, width = x_refs[0].shape
    total = slots * rows
    half = width // 2
    core = place_ref[0]

    def moves(index):
        copies = []
        for number, (array, whose, first, last) in enumerate(pieces[index]):
            target = weights.at[index % 2, pl.ds(first, last - first)]
            if whose is not None:
                part = core if whose == 0 else 1 - core
                target = weights.at[
                    index % 2, pl.ds(first, last - first), pl.ds(pl.multiple_of(part * half, half), half)
                ]
            copies.append(
                pltpu.make_async_copy(weight_refs[array], target, sems.at[index, number])
            )
        return copies

    @pl.when(expert == 0)
    def _():
        for copy in moves(0) + moves(1):
            copy.start()
        for slot in range(slots):
            here = slice(slot * rows, (slot + 1) * rows)
            x, dy = x_refs[slot][...], dy_refs[slot][:, :width]
            x_all[here, :] = x
            x_t[:, here] = x.T
            dy_all[here, :] = dy
            dy_t[:, here] = dy.T
            chosen = dy_refs[slot][:, width:].astype(jnp.float32)
            gates[here, :] = chosen_gates(x, w_route_ref[...], chosen)
        grad_gates[...] = jnp.zeros_like(grad_gates)
        mix_sum[...] = jnp.zeros_like(mix_sum)
        grad_x_sum[...] = jnp.zeros_like(grad_x_sum)

    for index in range(len(pieces)):

        @pl.when(expert == index)
        def _():
            if 1 <= index < len(pieces) - 1:
                for copy in moves(index + 1):
                    copy.start()
            for copy in moves(index):
                copy.wait()

    if first_call:
        grad_w[...] = jnp.zeros_like(grad_w)
    else:
        keep_before, in_before, out_before = before_refs
        grad_w[core] = keep_before[0].astype(jnp.float32)
        grad_w[1 - core, :2] = in_before[0].astype(jnp.float32)
        grad_w[1 - core, 2:] = out_before[0].astype(jnp.float32)
    buffer = lax.rem(expert, 2)
    w_gate, w_up, w_down_t = weights[buffer, 0], weights[buffer, 1], weights[buffer, 2]
    lane = lax.broadcasted_iota(jnp.int32, (total, LANES), 1)
    gate = jnp.sum(jnp.where(lane == place_ref[1 + expert], gates[...], 0.0), 1, keepdims=True)
    gate_row = jnp.broadcast_to(gate, (total, LANES)).T[:1]
    x = x_all[...]
    dy = dy_all[...].astype(jnp.float32)
    gate_pre = dot_f32(x, w_gate, 1, 0)
    up_pre = dot_f32(x, w_up, 1, 0)
    sigmoid_val = 0.5 + 0.5 * jnp.tanh(0.5 * gate_pre)
    silu_val = gate_pre * sigmoid_val
    up_slope = up_pre * (sigmoid_val * (1.0 + gate_pre * (1.0 - sigmoid_val)))
    hidden[...] = (silu_val * up_pre).astype(jnp.bfloat16)
    grad_hidden = dot_f32((gate * dy).astype(jnp.bfloat16), w_down_t, 1, 0)
    grad_gate_pre[...] = (grad_hidden * up_slope).astype(jnp.bfloat16)
    grad_up_pre[...] = (grad_hidden * silu_val).astype(jnp.bfloat16)
    out = dot_f32(hidden[...], w_down_t, 1, 1).astype(jnp.bfloat16).astype(jnp.float32)
    grad_gate = jnp.sum(out * dy, 1, keepdims=True)
    grad_gates[pl.ds(expert, 1), :] = jnp.broadcast_to(grad_gate, (total, LANES)).T[:1]
    mix_sum[...] += gate * out
    grad_copy = dot_f32(grad_gate_pre[...], w_gate, 1, 1) + dot_f32(
        grad_up_pre[...], w_up, 1, 1
    )
    grad_x_sum[...] += grad_copy.astype(jnp.bfloat16).astype(jnp.float32)
    grad_out_t = (dy_t[...].astype(jnp.float32) * gate_row).astype(jnp.bfloat16)
    terms = (
        dot_f32(x_t[...], grad_gate_pre[...], 1, 0),
        dot_f32(x_t[...], grad_up_pre[...], 1, 0),
        dot_f32(grad_out_t, hidden[...], 1, 0),
    )
    for part in range(2):
        for matrix, term in enumerate(terms):
            grad_w[part, matrix] += term[part * half : (part + 1) * half]
    keep_ref[0] = grad_w[core].astype(jnp.bfloat16)
    send_in_ref[0] = grad_w[1 - core, :2].astype(jnp.bfloat16)
    send_out_ref[0] = grad_w[1 - core, 2:].astype(jnp.bfloat16)

    @pl.when(expert == expert_count - 1)
    def _():
        for slot in range(slots):
            here = slice(slot * rows, (slot + 1) * rows)
            block = (place_ref[place_ref.shape[0] - 1] ^ (slot + 1)) if spread else slot
            mix_ref[block] = mix_sum[here, :].astype(jnp.bfloat16)
            grad_x_ref = grad_x_refs[0].at[block] if spread_x else grad_x_refs[slot]
            grad_x_ref[:, :width] = grad_x_sum[here, :].astype(jnp.bfloat16)
            parts = split_three(grad_gates[:, here])
            rest = jnp.zeros((LANES - 3 * parts[0].shape[0], rows), jnp.float32)
            grad_x_ref[:, width:] = (
                jnp.concatenate([*parts, rest], 0).T.astype(jnp.bfloat16)
            )
        if spread:
            own_block = place_ref[place_ref.shape[0] - 1]
            mix_ref[own_block] = jnp.zeros((rows, width), jnp.bfloat16)
        if spread_x:
            grad_x_refs[0][own_block] = jnp.zeros((rows, width + LANES), jnp.bfloat16)


def experts(place, x_parts, dy_parts, w_route, weights, pieces, before, spread, spread_x):
    rows = dy_parts[0][0].shape[1]
    width, hidden_width = x_parts[0][0].shape[1], weights[0].shape[-1]
    count, slots = len(pieces), len(x_parts)
    total = slots * rows
    half = width // 2
    mix_slots = slots + 1 if spread else slots
    first_call = before is None
    before = () if first_call else tuple(before)

    def at_block(shape, index):
        return pl.BlockSpec(
            shape,
            lambda expert: (index,) + (0,) * (len(shape) - 1),
            pipeline_mode=pl.Buffered(1),
        )

    row_specs = (pl.BlockSpec((rows, width + LANES), lambda expert: (0, 0)),) * slots
    if spread_x:
        row_specs = (pl.BlockSpec((mix_slots, rows, width + LANES), lambda expert: (0, 0, 0)),)
    grad_specs = [
        pl.BlockSpec((1, size, half, hidden_width), lambda expert: (expert, 0, 0, 0))
        for size in (3, 2, 1)
    ]
    grad_shapes = tuple(
        jax.ShapeDtypeStruct((count, size, half, hidden_width), jnp.bfloat16) for size in (3, 2, 1)
    )
    row_shapes = (jax.ShapeDtypeStruct((rows, width + LANES), jnp.bfloat16),) * slots
    if spread_x:
        row_shapes = (jax.ShapeDtypeStruct((mix_slots, rows, width + LANES), jnp.bfloat16),)
    outs = pl.pallas_call(
        functools.partial(
            experts_kernel,
            slots=slots,
            first_call=first_call,
            pieces=pieces,
            piece_count=len(weights),
            spread=spread,
            spread_x=spread_x,
        ),
        grid=(count,),
        out_shape=(jax.ShapeDtypeStruct((mix_slots, rows, width), jnp.bfloat16),)
        + row_shapes
        + grad_shapes,
        in_specs=[pl.BlockSpec(memory_space=pltpu.SMEM)]
        + [at_block((rows, width), index) for _, index in x_parts]
        + [at_block((None, rows, width + LANES), index) for _, index in dy_parts]
        + [at_block((width, LANES), 0)]
        + [pl.BlockSpec(memory_space=pl.ANY)] * len(weights)
        + grad_specs[: len(before)],
        out_specs=(pl.BlockSpec((mix_slots, rows, width), lambda expert: (0, 0, 0)),)
        + row_specs
        + tuple(grad_specs),
        scratch_shapes=[
            pltpu.VMEM((total, width), jnp.bfloat16),
            pltpu.VMEM((width, total), jnp.bfloat16),
            pltpu.VMEM((total, width), jnp.bfloat16),
            pltpu.VMEM((width, total), jnp.bfloat16),
            pltpu.VMEM((total, LANES), jnp.float32),
            pltpu.VMEM((8, total), jnp.float32),
            pltpu.VMEM((total, width), jnp.float32),
            pltpu.VMEM((total, width), jnp.float32),
            pltpu.VMEM((2, 3, half, hidden_width), jnp.float32),
            pltpu.VMEM((2, 3, width, hidden_width), jnp.bfloat16),
            pltpu.SemaphoreType.DMA((count, max(len(group) for group in pieces))),
        ]
        + [pltpu.VMEM((total, hidden_width), jnp.bfloat16)] * 3,
        cost_estimate=pl.CostEstimate(
            flops=count * total * width * hidden_width * 18,
            bytes_accessed=count * width * hidden_width * 12,
            transcendentals=0,
        ),
        compiler_params=pltpu.CompilerParams(
            vmem_limit_bytes=62 * MIB, dimension_semantics=("arbitrary",)
        ),
        name="experts",
    )(
        place,
        *[array for array, _ in (*x_parts, *dy_parts)],
        w_route,
        *weights,
        *before,
    )
    return outs[0], outs[1 : 1 + len(row_shapes)], outs[1 + len(row_shapes) :]


def together(*values):
    return lax.optimization_barrier(values)


def chosen_gates(x, w_route, chosen):
    logits = jnp.where(chosen > 0.0, dot_f32(x, w_route, 1, 0), NEG)
    raised = jnp.exp(logits - jnp.max(logits, 1, keepdims=True)) * chosen
    return raised / jnp.sum(raised, 1, keepdims=True)


def resid_back_kernel(*refs, counts):
    ids_ref, resid_ref, normed_ref, dy_ref, gain_ref, w_route_ref, w_out_ref = refs[:7]
    part_refs, refs = refs[7 : 7 + sum(counts)], refs[7 + sum(counts) :]
    grad_resid_ref, grad_branch_ref, grad_att_ref, grad_logits_ref, grad_gain_ref = refs
    micro_count, rows, width = dy_ref.shape[0], dy_ref.shape[1], resid_ref.shape[1]
    columns = ids_ref.shape[0] // (2 * PLANE)
    heads = w_out_ref.shape[1] // HEAD_DIM
    lane = lax.broadcasted_iota(jnp.int32, (rows, LANES), 1)
    gain = gain_ref[...]
    grad_gain = jnp.zeros((1, width), jnp.float32)
    for micro in range(micro_count):
        here = slice(micro * rows, (micro + 1) * rows)
        grad_normed = jnp.zeros((rows, width), jnp.float32)
        grad_gates = jnp.zeros((rows, LANES), jnp.float32)
        group = part_refs[sum(counts[:micro]) : sum(counts[: micro + 1])]
        if counts[micro] == 2:
            sources = [(group[1].at[place], PLANE + place) for place in range(PLANE)]
            sources.append((group[0], 0))
        else:
            sources = [(part_ref, step) for step, part_ref in enumerate(group)]
        for part_ref, step in sources:
            grad_normed = grad_normed + part_ref[:, :width].astype(jnp.float32)
            three = part_ref[:, width:].astype(jnp.float32)
            for up in range(columns):
                column = three[:, up : up + 1] + three[:, 8 + up : 9 + up]
                column = column + three[:, 16 + up : 17 + up]
                grad_gates = jnp.where(lane == ids_ref[step * columns + up], column, grad_gates)
        chosen = dy_ref[micro, :, width:].astype(jnp.float32)
        gates = chosen_gates(normed_ref[here, :], w_route_ref[...], chosen)
        weighted = jnp.sum(gates * grad_gates, 1, keepdims=True)
        grad_logits = (gates * (grad_gates - weighted)).astype(jnp.bfloat16)
        grad_logits_ref[here, :] = grad_logits
        grad_normed = grad_normed + dot_f32(grad_logits, w_route_ref[...], 1, 1)
        resid = resid_ref[here, :]
        scale = lax.rsqrt(jnp.mean(resid * resid, -1, keepdims=True) + EPS)
        gained = grad_normed * gain
        grad_gain = grad_gain + jnp.sum(grad_normed * resid * scale, 0, keepdims=True)
        grad_resid = (
            dy_ref[micro, :, :width].astype(jnp.float32)
            + scale * gained
            - resid * scale**3 * jnp.mean(resid * gained, -1, keepdims=True)
        )
        grad_resid_ref[here, :] = grad_resid
        grad_branch = grad_resid.astype(jnp.bfloat16)
        grad_branch_ref[here, :] = grad_branch
        turned = dot_f32(grad_branch, w_out_ref[...], 1, 0).T
        for head in range(heads):
            grad_att_ref[micro * heads + head] = turned[
                head * HEAD_DIM : (head + 1) * HEAD_DIM
            ].astype(jnp.bfloat16)
    grad_gain_ref[...] = jnp.broadcast_to(grad_gain, grad_gain_ref.shape)


def resid_back(ids, resid, normed, dy, gain, w_route, w_out_t, parts):
    total, width = resid.shape
    rows = dy.shape[1]
    heads = dy.shape[0] * w_out_t.shape[1] // HEAD_DIM
    flat = [part for group in parts for part in group]
    return pl.pallas_call(
        functools.partial(resid_back_kernel, counts=tuple(len(group) for group in parts)),
        out_shape=(
            jax.ShapeDtypeStruct((total, width), jnp.float32),
            jax.ShapeDtypeStruct((total, width), jnp.bfloat16),
            jax.ShapeDtypeStruct((heads, HEAD_DIM, rows), jnp.bfloat16),
            jax.ShapeDtypeStruct((total, LANES), jnp.bfloat16),
            jax.ShapeDtypeStruct((8, width), jnp.float32),
        ),
        in_specs=[pl.BlockSpec(memory_space=pltpu.SMEM)] + [whole_vmem()] * (6 + len(flat)),
        out_specs=(whole_vmem(),) * 5,
        compiler_params=pltpu.CompilerParams(vmem_limit_bytes=48 * MIB),
        name="resid_back",
    )(ids, resid, normed, dy, gain, w_route, w_out_t, *flat)


def flip(values, bits):
    count = lax.axis_size("ep")
    return lax.ppermute(values, "ep", [(index, index ^ bits) for index in range(count)])


def swap_cores(values):
    return lax.ppermute(values, "tp", [(0, 1), (1, 0)])


def every_device(values):
    return lax.all_to_all(values, ("ep", "tp"), 0, 0, tiled=True)


def head_tables(first_pos, rows):
    positions = first_pos + jnp.arange(rows, dtype=jnp.int32)
    halves = jnp.arange(HEAD_DIM // 2, dtype=jnp.float32)
    freqs = THETA ** (-2.0 * halves / HEAD_DIM)
    angles = freqs[:, None] * positions.astype(jnp.float32)[None, :]
    return jnp.cos(angles), jnp.sin(angles)


def paired_layout(ep_count, tp_count, micro_count, slice_rows, width, q_cols, kv_cols, experts_here):
    group = q_cols // kv_cols
    kv_heads = kv_cols * tp_count // HEAD_DIM
    return (
        tp_count == 2
        and group == 2
        and ep_count == micro_count * kv_heads
        and ep_count == PLANE * PLANE
        and experts_here == 1
        and slice_rows >= PIECE
        and slice_rows % PIECE == 0
        and width % (2 * LANES) == 0
    )


def on_device_paired(
    tokens,
    gain_attn,
    w_query,
    w_key,
    w_value,
    w_output,
    gain_moe,
    w_router,
    w_gate,
    w_up,
    w_down,
    routes,
    piece_starts,
    cotangent,
):
    ep_count = lax.axis_size("ep")
    tp_count = lax.axis_size("tp")
    ep_index, tp_index = lax.axis_index("ep"), lax.axis_index("tp")
    micro_count, rows, width = tokens.shape
    devices = ep_count * tp_count
    seq_len = rows * devices
    all_rows = micro_count * rows
    shard = gain_attn.shape[0]
    q_cols, kv_cols = w_query.shape[1], w_key.shape[1]
    kv_here = kv_cols // HEAD_DIM
    half_cols = q_cols + 2 * kv_cols
    out_cols = w_output.shape[0]
    columns = ep_count // PLANE
    experts_all = ep_count
    core = tp_index.astype(jnp.int32).reshape(1)

    level, spot = ep_index // PLANE, ep_index % PLANE
    half = width // 2
    micros = range(micro_count)

    small = jnp.concatenate([w_router, jnp.zeros((shard, LANES - experts_all), w_router.dtype)], 1)
    lanes = jnp.arange(LANES, dtype=jnp.int32)
    small = jnp.where(lanes == LANES // 2, gain_attn[:, None], small)
    small = jnp.where(lanes == LANES // 2 + 1, gain_moe[:, None], small)
    packed = jnp.concatenate([w_query, w_key, w_value, small], 1)
    levels = [packed] + [flip(packed, PLANE * step) for step in range(1, columns)]
    mine = jnp.stack(levels)
    mine = [mine] + [flip(mine, step) for step in range(1, PLANE)]

    w_down_t = w_down[0].T
    first_half = tp_index * half
    expert_half = jnp.stack(
        [
            lax.dynamic_slice_in_dim(whole, first_half, half, 0)
            for whole in (w_gate[0], w_up[0], w_down_t)
        ]
    )
    expert_half, levels = together(expert_half, levels)
    far_out = flip(expert_half[2:], 2 * PLANE)
    near_out = flip(expert_half[2:], PLANE)
    mine, far_out, near_out = together(mine, far_out, near_out)
    other = [swap_cores(part) for part in mine]

    x_rows = tokens.reshape(all_rows, width).astype(jnp.float32)
    device_index = ep_index * tp_count + tp_index
    cosine, sine = head_tables(device_index * rows, rows)
    spot_here = jnp.stack([tp_index, level, spot]).astype(jnp.int32)
    normed, sent, w_heads, small_all = project(
        spot_here, tokens, cosine, sine, mine, other, devices
    )
    gain_one = small_all[:, LANES // 2].astype(jnp.float32)
    gain_two = small_all[:, LANES // 2 + 1].astype(jnp.float32)
    nearfar_out = flip(far_out, PLANE)
    sent, nearfar_out = together(sent, nearfar_out)
    own = every_device(sent)
    other = swap_cores(own[:, HEAD_DIM:, :])

    chosen = jnp.any(routes[:, :, :, None] == lanes, 2).astype(jnp.bfloat16)
    own_dy = jnp.concatenate([cotangent, chosen], 2)
    early_dy, small_all = together(own_dy, small_all)
    plane_dy = [flip(early_dy, step) for step in range(1, PLANE - 1)]
    other, plane_dy = together(other, plane_dy)
    w_output_t, expert_late, dy_late, other = together(
        w_output.T, expert_half, own_dy, other
    )
    far_in = flip(expert_late[:2], 2 * PLANE)
    near_in = flip(expert_late[:2], PLANE)
    plane_dy = plane_dy + [flip(dy_late, PLANE - 1)]
    gathered_out = lax.all_gather(w_output_t, ("ep", "tp"), axis=0, tiled=False)

    micro_here = ep_index // (ep_count // micro_count)
    starts = lax.dynamic_index_in_dim(piece_starts, micro_here, 0, keepdims=False)
    all_pos = jnp.arange(seq_len, dtype=jnp.int32)[None, :]
    inside = (all_pos >= starts[:, None]) & (all_pos < starts[:, None] + PIECE)
    piece_last = jnp.max(jnp.where(inside, starts[:, None] + (PIECE - 1), -1), 0, keepdims=True)
    limit = jnp.maximum(all_pos, piece_last).astype(jnp.int32)
    out_b, out_f, log_total = attend(core, own, other, limit)
    out_b, near_in, far_in, plane_dy = together(out_b, near_in, far_in, plane_dy)
    nearfar_in = flip(far_in, PLANE)
    attended_t = every_device(out_b).reshape(micro_count, out_cols * tp_count, rows)
    gathered_out = gathered_out.reshape(ep_count, tp_count, shard, out_cols)
    w_out_t = jnp.concatenate(
        [gathered_out[:, part].reshape(width, out_cols) for part in range(2)], 1
    )

    attn_rows = jnp.concatenate(
        [dot_f32(attended_t[micro], w_out_t, 0, 1) for micro in micros], 0
    )
    resid = x_rows + attn_rows
    scale_two = rms_scale(resid)
    normed_two = (resid * scale_two * gain_two).astype(jnp.bfloat16)
    normed_parts = [normed_two[micro * rows : (micro + 1) * rows] for micro in micros]
    plane_x = [[flip(normed_parts[0], step) for step in range(1, PLANE)]]

    weights = [w_gate, w_up, w_down_t[None]]
    nearfar_in, normed_late = together(nearfar_in, normed_two)
    for piece in (near_in, near_out, far_in, far_out, nearfar_in, nearfar_out):
        weights += [piece, swap_cores(piece)]
    pieces = [[(0, None, 0, 1), (1, None, 1, 2), (2, None, 2, 3)]]
    for first in (3, 7, 11):
        pieces.append(
            [(first, 0, 0, 2), (first + 1, 1, 0, 2), (first + 2, 0, 2, 3), (first + 3, 1, 2, 3)]
        )

    spot_here = spot.astype(jnp.int32).reshape(1)
    column_ids = jnp.stack([(level ^ up) * PLANE + spot for up in range(columns)])
    place = jnp.concatenate([core, column_ids.astype(jnp.int32), spot_here])
    own_mix, own_grad_x, before = experts(
        place,
        [(normed_two, micro) for micro in micros],
        [(own_dy, micro) for micro in micros],
        small_all,
        weights,
        pieces,
        None,
        False,
        False,
    )
    leaving = normed_parts[1:]
    leaving, own_mix = together(leaving, own_mix)
    plane_x += [[flip(part, step) for step in range(1, PLANE)] for part in leaving]
    plane_groups = [[up * PLANE + step for step in range(PLANE)] for up in range(columns)]
    column_groups = [[up * PLANE + step for up in range(columns)] for step in range(PLANE)]

    def within_plane(parts):
        return lax.all_to_all(parts, "ep", 0, 0, tiled=True, axis_index_groups=plane_groups)

    far_mix, far_grad_x = [], []
    for micro in micros:
        mix, grad_x, before = experts(
            place,
            [(part, 0) for part in plane_x[micro]],
            [(part, micro) for part in plane_dy],
            small_all,
            weights,
            pieces,
            before,
            True,
            micro == micro_count - 1,
        )
        if micro:
            grad_x, before, far_grad_x = together(grad_x, before, far_grad_x)
        if micro < micro_count - 1:
            far_grad_x.append([flip(grad_x[step - 1], step) for step in range(1, PLANE)])
        else:
            far_grad_x.append([within_plane(grad_x[0])])
        far_mix.append(mix)
    keep_w, send_in_w, send_out_w = before
    given_out = swap_cores(send_out_w)

    def out_sum_of(slot):
        return keep_w[slot, 2].astype(jnp.float32) + given_out[slot, 0].astype(jnp.float32)

    near_out_w = jnp.stack([out_sum_of(slot).astype(jnp.bfloat16) for slot in (1, 3)])
    near_out_w = flip(near_out_w, PLANE)
    far_grad_x[-1], near_out_w, given_out = together(far_grad_x[-1], near_out_w, given_out)
    near_out_w = near_out_w.astype(jnp.float32)

    plane_ids = jnp.stack(
        [
            (level ^ up) * PLANE + (spot ^ step)
            for step in range(PLANE)
            for up in range(columns)
        ]
        + [(level ^ up) * PLANE + place for place in range(PLANE) for up in range(columns)]
    )
    grad_resid, grad_branch, grad_att, grad_logits, grad_gain_two = resid_back(
        plane_ids.astype(jnp.int32),
        resid,
        normed_two,
        own_dy,
        gain_two[None, :],
        small_all,
        w_out_t,
        [[own_grad_x[micro], *far_grad_x[micro]] for micro in micros],
    )
    grad_route = dot_f32(normed_late, grad_logits, 0, 0)[:, :experts_all]
    grad_gain_two = grad_gain_two[0]
    grad_outw = sum(
        dot_f32(grad_branch[micro * rows : (micro + 1) * rows], attended_t[micro], 0, 1)
        for micro in micros
    ).astype(jnp.bfloat16)
    grad_heads = every_device(grad_att)
    far_out_w = (out_sum_of(2) + near_out_w[1]).astype(jnp.bfloat16)
    own_out_w = out_sum_of(0)
    given_in = swap_cores(send_in_w)

    def column_sum(slot):
        kept = keep_w[slot, :2].astype(jnp.float32)
        return (kept + given_in[slot].astype(jnp.float32)).astype(jnp.bfloat16)

    own_w = keep_w[0, :2].astype(jnp.float32) + given_in[0].astype(jnp.float32)
    near_in_w, far_in_w, last_in_w = column_sum(1), column_sum(2), column_sum(3)
    all_mix = jnp.concatenate(far_mix, 1)
    grad_heads, near_in_w, last_in_w, far_in_w, far_out_w, own_w, all_mix = together(
        grad_heads, near_in_w, last_in_w, far_in_w, far_out_w, own_w, all_mix
    )
    all_mix = within_plane(all_mix)
    near_in_w = flip(near_in_w, PLANE)
    last_in_w = flip(last_in_w, 3 * PLANE)
    far_in_w = flip(far_in_w, 2 * PLANE)
    far_out_w = flip(far_out_w, 2 * PLANE)

    def to_shards(kept, given):
        core_sum = kept.astype(jnp.float32) + swap_cores(given).astype(jnp.float32)
        shares = lax.all_to_all(
            core_sum.astype(jnp.bfloat16).reshape(ep_count, shard, -1), "ep", 0, 0, tiled=True
        )
        return jnp.sum(shares.astype(jnp.float32), 0)

    def in_lanes(columns_f):
        small = jnp.concatenate(columns_f, 1)
        return jnp.pad(small, ((0, 0), (0, LANES - small.shape[1]))).astype(jnp.bfloat16)

    def own_rows(values):
        return lax.dynamic_slice_in_dim(values, tp_index * (shard // 2), shard // 2, 0)

    late_small = in_lanes([grad_route, grad_gain_two[:, None]])
    out_parts = [
        jnp.concatenate([grad_outw[:, part * out_cols : (part + 1) * out_cols], late_small], 1)
        for part in range(2)
    ]
    out_kept = jnp.where(tp_index == 0, out_parts[0], out_parts[1])
    out_given = jnp.where(tp_index == 0, out_parts[1], out_parts[0])
    grad_q, keep_kv, send_kv = attend_back(
        core, own, other, limit, out_f, log_total, grad_heads
    )
    grad_q, keep_kv, send_kv, near_in_w, last_in_w, far_in_w, far_out_w, all_mix = together(
        grad_q, keep_kv, send_kv, near_in_w, last_in_w, far_in_w, far_out_w, all_mix
    )
    grad_kv = (keep_kv + swap_cores(send_kv).astype(jnp.float32)).astype(jnp.bfloat16)
    sent_back = jnp.concatenate([grad_q, grad_kv], 1)
    grad_own = every_device(sent_back)
    out_sum = out_kept.astype(jnp.float32) + swap_cores(out_given).astype(jnp.float32)
    out_sum = out_sum.astype(jnp.bfloat16).reshape(columns, PLANE, shard, -1)

    def summed(values, axis, place_here, stride):
        own_part = lax.dynamic_index_in_dim(values, place_here, axis, False).astype(jnp.float32)
        return own_part, [
            flip(lax.dynamic_index_in_dim(values, place_here ^ step, axis, False), stride * step)
            for step in range(1, values.shape[axis])
        ]

    out_own, out_far = summed(out_sum, 1, spot, 1)
    out_levels = out_own + sum(part.astype(jnp.float32) for part in out_far)
    out_own, out_far = summed(out_levels.astype(jnp.bfloat16), 0, level, PLANE)
    grad_own, out_far = together(grad_own, out_far)
    out_share = out_own + sum(part.astype(jnp.float32) for part in out_far)
    out_small = own_rows(out_share[:, out_cols:])
    grad_tokens, kept, given = project_back(
        core, grad_own, w_heads, normed, tokens, grad_resid, gain_one[None, :], cosine, sine
    )
    kept, given, near_in_w, last_in_w, far_in_w, far_out_w = together(
        kept, given, near_in_w, last_in_w, far_in_w, far_out_w
    )
    grad_w = [
        own_w[matrix]
        + sum(part[matrix].astype(jnp.float32) for part in (near_in_w, last_in_w, far_in_w))
        for matrix in range(2)
    ]
    grad_w.append(own_out_w + near_out_w[0] + far_out_w.astype(jnp.float32))
    mixed = resid + own_mix.reshape(all_rows, width).astype(jnp.float32)
    mixed = (mixed + jnp.sum(all_mix.astype(jnp.float32), 0)).astype(jnp.bfloat16)

    own_share = to_shards(kept, given)
    return (
        mixed.reshape(micro_count, rows, width),
        grad_tokens,
        own_rows(own_share[:, half_cols:])[:, 0],
        own_share[:, :q_cols],
        own_share[:, q_cols : q_cols + kv_cols],
        own_share[:, q_cols + kv_cols : half_cols],
        out_share[:, :out_cols].T,
        out_small[:, experts_all],
        out_small[:, :experts_all],
        grad_w[0][None],
        grad_w[1][None],
        grad_w[2].T[None],
    )


def on_device(*args):
    tokens, w_query, w_key, w_gate = args[0], args[2], args[3], args[8]
    paired = paired_layout(
        lax.axis_size("ep"),
        lax.axis_size("tp"),
        *tokens.shape,
        w_query.shape[1],
        w_key.shape[1],
        w_gate.shape[0],
    )
    return (on_device_paired if paired else on_device_general)(*args)


def solution(mesh):
    in_specs = (
        P(None, ("ep", "tp"), None),
        P("ep"),
        P("ep", "tp"),
        P("ep", "tp"),
        P("ep", "tp"),
        P("tp", "ep"),
        P("ep"),
        P("ep", None),
        P("ep", None, None),
        P("ep", None, None),
        P("ep", None, None),
        P(None, ("ep", "tp"), None),
        P(),
        P(None, ("ep", "tp"), None),
    )
    out_specs = (
        P(None, ("ep", "tp"), None),
        P(None, ("ep", "tp"), None),
        P(("ep", "tp")),
        P("ep", "tp"),
        P("ep", "tp"),
        P("ep", "tp"),
        P("tp", "ep"),
        P(("ep", "tp")),
        P(("ep", "tp"), None),
        P("ep", "tp", None),
        P("ep", "tp", None),
        P("ep", None, "tp"),
    )
    return jax.shard_map(
        on_device, mesh=mesh, in_specs=in_specs, out_specs=out_specs, check_vma=False
    )
```
